32 devices in a mesh: grp: 2 (over y), gy: 4 (over z), gx: 2 (over x), ch: 2 (over core).
Axes of the slice: x: 2, y: 2, z: 4, core: 2. Of those that a mesh axis runs over, the one named last changes fastest.
Arguments:
- cells: bfloat16 [128, 128, 512], P(('grp', 'gy'), 'gx'), parts along dimension 0, may hold values from -6 to 6
- w_expand: bfloat16 [512, 2048], P(None, 'ch'), may hold values from -0.25 to 0.25
- b_expand: float32 [2048], P('ch'), may hold values from -3 to 3
- w_depth: bfloat16 [3, 3, 2048], P(None, None, 'ch'), may hold values from -2 to 2
- b_depth: float32 [2048], P('ch'), may hold values from -3 to 3
- w_project: bfloat16 [2048, 512], P('ch'), may hold values from -0.125 to 0.125
- b_project: float32 [512], replicated, may hold values from -3 to 3
- ln_gain: float32 [512], replicated, may hold values from 0.5 to 1.5
- w_qkv: bfloat16 [512, 3, 512], P(None, None, 'ch'), as said below
- w_out: bfloat16 [512, 512], P('ch'), may hold values from -0.25 to 0.25
- b_out: float32 [512], P('ch'), may hold values from -3 to 3
Outputs:
- result: bfloat16 [128, 128, 512], P(('grp', 'gy'), 'gx', 'ch'), parts along dimension 0
The draws below stay inside these ranges and needn't reach their ends.
There are 2 independent parts, one for each index of `grp`. The reference program is written for one: setup_inputs(seed, part) draws one part's arguments, and reference() takes and returns one part's arrays. A program takes and returns all parts, laid end to end along the dimension named above; an argument that names none is the same for every part. Nothing has to cross between parts.
Inputs may be any that keep to these rules, and one draw needn't show every extreme that they name: `w_qkv`: dense projection weights of every head.
All inputs are finite; a program needn't handle non-finite values.
Results may differ from the reference program's by a relative error of at most 0.01.
Values may be sent and summed in bfloat16 or wider, within the bound.
No kernel may reach another device: no remote copies, remote signals or barrier semaphores. Data moves between devices by JAX's collectives and lax.ppermute only.
A program may use at most 64 MiB of HBM per device.

```python
import jax
import jax.numpy as jnp
from jax import lax

C = 512
EXP = 2048
HEADS = 16
HEAD_DIM = 32
GRID = 8
ROWS = 64
COLS = 128


def draw_w_qkv(key, part):
    key_base = jax.random.fold_in(key, 11)
    weight_scale = C ** (-0.5)
    return (jax.random.normal(key_base, (C, 3, C), jnp.float32) * weight_scale).astype(jnp.bfloat16)


def levels(own_key, dims, pieces, least, high):
    gain = 1.0
    for position, blocks in pieces:
        draws = jax.random.uniform(jax.random.fold_in(jax.random.fold_in(own_key, 6), position), (blocks,), jnp.float32, least / len(pieces), high / len(pieces))
        gain = gain * jnp.repeat(jnp.exp(draws), dims[position] // blocks).reshape((-1,) + (1,) * (len(dims) - 1 - position))
    return gain


def normal_values(stream_key, extent, scale, bound, split=(), kind=jnp.bfloat16):
    gain = levels(stream_key, extent, split, -0.22, 0.18) if split else 1.0
    values = jax.random.normal(stream_key, extent, jnp.float32) * scale * gain
    return jnp.minimum(jnp.maximum(values, -bound), bound).astype(kind)


def setup_inputs(seed: int = 0, part: int = 0) -> dict:
    splits = jax.random.split(jax.random.key(seed), 12)
    part_splits = jax.random.split(jax.random.fold_in(splits[11], part), 12)
    return {
        "cells": normal_values(part_splits[0], (ROWS, COLS, C), 1.0, 6.0, ((0, 4), (1, 2))),
        "w_expand": normal_values(splits[1], (C, EXP), C ** -0.5, 0.25, ((1, 2),)),
        "b_expand": normal_values(splits[2], (EXP,), 0.5, 3.0, ((0, 2),), jnp.float32),
        "w_depth": normal_values(splits[3], (3, 3, EXP), 9 ** -0.5, 2.0, ((2, 2),)),
        "b_depth": normal_values(splits[4], (EXP,), 0.5, 3.0, ((0, 2),), jnp.float32),
        "w_project": normal_values(splits[5], (EXP, C), EXP ** -0.5, 0.125, ((0, 2),)),
        "b_project": normal_values(splits[6], (C,), 0.5, 3.0, (), jnp.float32),
        "ln_gain": jnp.clip(jax.random.uniform(splits[7], (C,), jnp.float32, 0.5, 1.5), 0.5, 1.5),
        "w_qkv": draw_w_qkv(jax.random.fold_in(splits[11], 71), part),
        "w_out": normal_values(splits[9], (C, C), C ** -0.5, 0.25, ((0, 2),)),
        "b_out": normal_values(splits[10], (C,), 0.5, 3.0, ((0, 2),), jnp.float32),
    }


def gelu_exact(values):
    return jax.nn.gelu(values, approximate=False)

def normalize(source, ln_gain):
    values = source.astype(jnp.float32)
    centre = lax.optimization_barrier(jnp.mean(values, axis=-1, keepdims=True))
    centered = values - centre
    spread = lax.optimization_barrier(jnp.mean(centered * centered, axis=-1, keepdims=True))
    return (centered * lax.rsqrt(spread + 1e-05) * ln_gain).astype(jnp.bfloat16)

def reference(cells, w_expand, b_expand, w_depth, b_depth, w_project, b_project, ln_gain, w_qkv, w_out, b_out):
    rows, cols, width = cells.shape
    blocks = 8
    piece = EXP // blocks
    expand_blocks = w_expand.reshape(width, blocks, piece).transpose(1, 0, 2)
    bias_blocks = b_expand.reshape(blocks, piece)
    depth_blocks = w_depth.reshape(3, 3, blocks, piece).transpose(2, 0, 1, 3)
    depth_bias = b_depth.reshape(blocks, piece)
    project_blocks = w_project.reshape(blocks, piece, width)
    flat_cells = cells.reshape(rows * cols, width)

    def add_block(total, parts):
        w_e, b_e, w_d, b_d, w_p = parts
        pre = jnp.dot(flat_cells, w_e, preferred_element_type=jnp.float32).reshape(rows, cols, piece)
        expanded = gelu_exact(pre + b_e).astype(jnp.bfloat16)
        padded = jnp.pad(expanded, ((1, 1), (1, 1), (0, 0)))
        summed = jnp.zeros((rows, cols, piece), jnp.float32)
        for row_off in range(3):
            for col_off in range(3):
                summed = summed + padded[row_off:row_off + rows, col_off:col_off + cols].astype(jnp.float32) * w_d[row_off, col_off].astype(jnp.float32)
        depth = gelu_exact(summed + b_d).astype(jnp.bfloat16)
        term = jnp.dot(depth.reshape(rows * cols, piece), w_p, preferred_element_type=jnp.float32)
        return (total + term.reshape(rows, cols, width), None)
    total, _ = lax.scan(add_block, jnp.zeros((rows, cols, width), jnp.float32), (expand_blocks, bias_blocks, depth_blocks, depth_bias, project_blocks))
    mixed = (cells.astype(jnp.float32) + total + b_project).astype(jnp.bfloat16)
    stride_h = rows // GRID
    stride_w = cols // GRID
    windows = mixed.reshape(GRID, stride_h, GRID, stride_w, width).transpose(1, 3, 0, 2, 4)
    windows = windows.reshape(stride_h * stride_w, GRID * GRID, width)
    count = stride_h * stride_w
    tokens = GRID * GRID
    normed = normalize(windows, ln_gain).reshape(count * tokens, width)

    def project_heads(index):
        projected = jnp.dot(normed, w_qkv[:, index, :], preferred_element_type=jnp.float32).astype(jnp.bfloat16)
        return projected.reshape(count, tokens, HEADS, HEAD_DIM).transpose(2, 0, 1, 3)
    query = project_heads(0)
    keyset = project_heads(1)
    valueset = project_heads(2)

    def one_head(parts):
        head_q, head_k, head_v = parts
        scores = jnp.einsum('wqd,wkd->wqk', head_q.astype(jnp.float32), head_k.astype(jnp.float32)) * HEAD_DIM ** (-0.5)
        weights = jax.nn.softmax(scores, axis=-1).astype(jnp.bfloat16)
        return jnp.einsum('wqk,wkd->wqd', weights.astype(jnp.float32), head_v.astype(jnp.float32)).astype(jnp.bfloat16)
    heads_out = lax.map(one_head, (query, keyset, valueset))
    attended = heads_out.transpose(1, 2, 0, 3).reshape(count * tokens, width)
    projected_out = jnp.dot(attended, w_out, preferred_element_type=jnp.float32).reshape(count, tokens, width)
    outcome = (windows.astype(jnp.float32) + projected_out + b_out).astype(jnp.bfloat16)
    outcome = outcome.reshape(stride_h, stride_w, GRID, GRID, width).transpose(2, 0, 3, 1, 4)
    return outcome.reshape(rows, cols, width)
```

```python
import functools

import jax
import jax.numpy as jnp
import numpy as np
from jax import lax
from jax.experimental import pallas as pl
from jax.experimental.pallas import tpu as pltpu
from jax.sharding import PartitionSpec as P

SUBLANES = 8
CHUNK = 256
VMEM_BYTES = 48 * 2**20

HEAD_DIM = 32
GRID = 8


def extended(block, sides, width):
    for axis, dim in sides:
        count = lax.axis_size(axis)
        forward = [(i, i + 1) for i in range(count - 1)]
        backward = [(target, source) for source, target in forward]
        low = lax.ppermute(
            lax.slice_in_dim(block, block.shape[dim] - width, None, axis=dim), axis, forward
        )
        high = lax.ppermute(lax.slice_in_dim(block, 0, width, axis=dim), axis, backward)
        block = jnp.concatenate([low, block, high], axis=dim)
    return block


def gelu_exact(values):
    return jax.nn.gelu(values, approximate=False)


def expand_cells(source, w_expand, b_expand):
    pre = jnp.einsum("hwc,ce->hwe", source, w_expand, preferred_element_type=jnp.float32)
    return gelu_exact(pre + b_expand).astype(jnp.bfloat16)


def depthwise(padded, w_depth, b_depth, tile_h, tile_w):
    summed = jnp.zeros((tile_h, tile_w, padded.shape[2]), jnp.float32)
    for row_off in range(3):
        for col_off in range(3):
            summed = summed + padded[row_off : row_off + tile_h, col_off : col_off + tile_w].astype(
                jnp.float32
            ) * w_depth[row_off, col_off].astype(jnp.float32)
    return gelu_exact(summed + b_depth).astype(jnp.bfloat16)


def split_order(tile, depth_h, depth_w):
    tile_h, tile_w, width = tile.shape
    shaped = tile.reshape(tile_h // depth_h, depth_h, tile_w // depth_w, depth_w, width)
    return shaped.transpose(1, 0, 3, 2, 4)


def join_order(arranged):
    depth_h, outer_h, depth_w, outer_w, width = arranged.shape
    return arranged.transpose(1, 0, 3, 2, 4).reshape(outer_h * depth_h, outer_w * depth_w, width)


def into_windows(arrived, steps_h, steps_w):
    local_h, span_h, local_w, span_w, width = arrived.shape
    grouped = arrived.reshape(local_h, GRID, steps_h, local_w, GRID, steps_w, width)
    grouped = grouped.transpose(2, 0, 5, 3, 1, 4, 6)
    return grouped.reshape(steps_h * local_h * steps_w * local_w, GRID * GRID, width)


def out_of_windows(windows, local_h, steps_h, local_w, steps_w):
    width = windows.shape[2]
    grouped = windows.reshape(steps_h, local_h, steps_w, local_w, GRID, GRID, width)
    grouped = grouped.transpose(1, 4, 0, 3, 5, 2, 6)
    return grouped.reshape(local_h, GRID * steps_h, local_w, GRID * steps_w, width)


def attend(window_full, ln_gain, w_qkv):
    values = window_full.astype(jnp.float32)
    centre = jnp.mean(values, axis=-1, keepdims=True)
    centered = values - centre
    spread = jnp.mean(centered * centered, axis=-1, keepdims=True)
    normed = (centered * lax.rsqrt(spread + 1e-05) * ln_gain).astype(jnp.bfloat16)
    projected = jnp.einsum(
        "wtc,cke->kwte", normed, w_qkv, preferred_element_type=jnp.float32
    ).astype(jnp.bfloat16)
    window_count = projected.shape[1]
    tokens = projected.shape[2]
    own_width = projected.shape[3]
    heads_own = own_width // HEAD_DIM
    shaped = projected.reshape(3, window_count, tokens, heads_own, HEAD_DIM)
    scores = jnp.einsum(
        "wqhd,wkhd->whqk", shaped[0], shaped[1], preferred_element_type=jnp.float32
    ) * HEAD_DIM ** (-0.5)
    weights = jax.nn.softmax(scores, axis=-1).astype(jnp.bfloat16)
    heads_out = jnp.einsum(
        "whqk,wkhd->wqhd", weights, shaped[2], preferred_element_type=jnp.float32
    ).astype(jnp.bfloat16)
    return heads_out.reshape(window_count, tokens, own_width)


def general_device(
    cells, w_expand, b_expand, w_depth, b_depth, w_project, b_project, ln_gain, w_qkv, w_out, b_out
):
    tile_h, tile_w, width = cells.shape
    n_rows = lax.axis_size("gy")
    n_cols = lax.axis_size("gx")
    half = width // lax.axis_size("ch")
    own = lax.axis_index("ch")
    stride_h = tile_h * n_rows // GRID
    stride_w = tile_w * n_cols // GRID
    depth_h = min(tile_h, stride_h)
    depth_w = min(tile_w, stride_w)
    steps_h = stride_h // depth_h
    steps_w = stride_w // depth_w
    local_h = depth_h // n_rows
    local_w = depth_w // n_cols
    expanded = expand_cells(cells, w_expand, b_expand)
    padded = extended(expanded, (("gy", 0), ("gx", 1)), 1)
    depth = depthwise(padded, w_depth, b_depth, tile_h, tile_w)
    partial_value = jnp.einsum("hwe,ec->hwc", depth, w_project, preferred_element_type=jnp.float32)
    share = lax.psum_scatter(
        partial_value.astype(jnp.bfloat16), "ch", scatter_dimension=2, tiled=True
    ).astype(jnp.float32)
    cells_own = lax.dynamic_slice_in_dim(cells, own * half, half, 2)
    bias_own = lax.dynamic_slice_in_dim(b_project, own * half, half, 0)
    mixed_own = (cells_own.astype(jnp.float32) + share + bias_own).astype(jnp.bfloat16)
    arranged = split_order(mixed_own, depth_h, depth_w)
    arrived = lax.all_to_all(
        lax.all_to_all(arranged, "gy", split_axis=0, concat_axis=1, tiled=True),
        "gx",
        split_axis=2,
        concat_axis=3,
        tiled=True,
    )
    window_own = into_windows(arrived, steps_h, steps_w)
    window_full = lax.all_gather(window_own, "ch", axis=2, tiled=True)
    heads_out = attend(window_full, ln_gain, w_qkv)
    attention_terms = jnp.einsum(
        "wte,ec->wtc", heads_out, w_out, preferred_element_type=jnp.float32
    )
    attention_own = lax.psum_scatter(
        attention_terms.astype(jnp.bfloat16), "ch", scatter_dimension=2, tiled=True
    ).astype(jnp.float32)
    outcome = (window_own.astype(jnp.float32) + attention_own + b_out).astype(jnp.bfloat16)
    leaving = out_of_windows(outcome, local_h, steps_h, local_w, steps_w)
    returned = lax.all_to_all(
        lax.all_to_all(leaving, "gy", split_axis=1, concat_axis=0, tiled=True),
        "gx",
        split_axis=3,
        concat_axis=2,
        tiled=True,
    )
    return join_order(returned)


class Plan:
    def __init__(self, cells, n_rows, n_cols, n_ch):
        tile_h, tile_w, self.width = cells.shape
        stride_h, stride_w = tile_h * n_rows // GRID, tile_w * n_cols // GRID
        self.depth_h, self.depth_w = min(tile_h, stride_h), min(tile_w, stride_w)
        self.outer_h, self.outer_w = tile_h // self.depth_h, tile_w // self.depth_w
        self.n_rows, self.n_cols, self.n_ch = n_rows, n_cols, n_ch
        self.fits = (
            self.depth_h == stride_h
            and self.depth_w == stride_w
            and self.outer_h * self.outer_w == SUBLANES
            and min(self.outer_h, self.outer_w) >= 2
            and self.depth_h == n_rows * n_ch
            and self.depth_w == n_cols * SUBLANES
            and n_ch == 2
            and n_rows * n_cols * SUBLANES == GRID * GRID
            and self.width % CHUNK == 0
        )

    def order(self):
        count = self.depth_w * SUBLANES
        source = np.arange(count).reshape(self.outer_h, self.outer_w, self.depth_w)
        source = source.transpose(2, 0, 1).reshape(count)
        return np.eye(count, dtype=np.float32)[source]

    def sides(self):
        planes, rows = self.depth_h + 2, self.outer_h * self.depth_h + 2
        left = np.zeros((planes, self.outer_h, self.outer_w, rows), np.float32)
        right = np.zeros_like(left)
        for plane in range(planes):
            for i in range(self.outer_h):
                left[plane, i, 0, i * self.depth_h + plane] = 1
                right[plane, i, -1, i * self.depth_h + plane] = 1
        return left.reshape(-1, rows), right.reshape(-1, rows)


def gelu_erf(values):
    return (0.5 * values) * (1.0 + lax.erf(values * 0.5**0.5))


def expand_kernel(cells_ref, w_ref, b_ref, order_ref, out_ref, arranged_ref):
    planes = cells_ref.shape[1]
    count, width = arranged_ref.shape[1:]
    for plane in range(planes):
        block = cells_ref[:, plane].reshape(count, width)
        arranged_ref[plane] = jnp.dot(
            order_ref[...], block, preferred_element_type=jnp.float32
        ).astype(jnp.bfloat16)
    source = arranged_ref[...].reshape(planes * count, width)
    for low in range(0, out_ref.shape[2], CHUNK):
        part = slice(low, low + CHUNK)
        pre = jnp.dot(source, w_ref[:, part], preferred_element_type=jnp.float32)
        out_ref[:, :, part] = (
            gelu_erf(pre + b_ref[:, part]).astype(jnp.bfloat16).reshape(planes, count, CHUNK)
        )


def expand(plan, cells, w_expand, b_expand, order):
    planes = 2
    count = plan.depth_w * SUBLANES
    own = w_expand.shape[1]
    shaped = cells.reshape(plan.outer_h, plan.depth_h, count // plan.outer_h, plan.width)
    return pl.pallas_call(
        expand_kernel,
        grid=(plan.depth_h // planes,),
        in_specs=[
            pl.BlockSpec((plan.outer_h, planes) + shaped.shape[2:], lambda i: (0, i, 0, 0)),
            pl.BlockSpec(w_expand.shape, lambda i: (0, 0)),
            pl.BlockSpec(b_expand.shape, lambda i: (0, 0)),
            pl.BlockSpec(order.shape, lambda i: (0, 0)),
        ],
        out_specs=[
            pl.BlockSpec((planes, count, own), lambda i: (i, 0, 0)),
            pl.BlockSpec((planes, count, plan.width), lambda i: (i, 0, 0)),
        ],
        out_shape=[
            jax.ShapeDtypeStruct((plan.depth_h, count, own), jnp.bfloat16),
            jax.ShapeDtypeStruct((plan.depth_h, count, plan.width), jnp.bfloat16),
        ],
        compiler_params=pltpu.CompilerParams(vmem_limit_bytes=VMEM_BYTES),
        cost_estimate=pl.CostEstimate(
            flops=2 * cells.size * own, bytes_accessed=8 * cells.size, transcendentals=0
        ),
        name="expand",
    )(shaped, w_expand, b_expand, order)


def depth_kernel(
    plan, flag_ref, e_ref, x_ref, up_ref, down_ref, left_ref, right_ref, order_ref, left_at_ref,
    right_at_ref, we_ref, be_ref, wd_ref, bd_ref, wp_ref, bp_ref, sib_ref, own_ref, held, deep,
):
    step = pl.program_id(0)
    deep_h, deep_w, outer_w = plan.depth_h, plan.depth_w, plan.outer_w
    count = deep_w * SUBLANES
    chunk = e_ref.shape[2]
    flags = [flag_ref[i].astype(jnp.float32) for i in range(1, 5)]
    up, down, left, right = flags

    def expanded(cells):
        pre = jnp.dot(cells, we_ref[...], preferred_element_type=jnp.float32)
        return gelu_erf(pre + be_ref[...])

    row = lax.broadcasted_iota(jnp.int32, (1, SUBLANES, chunk), 1)
    halo = jnp.concatenate([up_ref[...], down_ref[...]], axis=0)
    spare = count - halo.shape[0]
    if spare:
        middle = jnp.zeros((spare, plan.width), halo.dtype)
        halo = jnp.concatenate([up_ref[...], middle, down_ref[...]], axis=0)
    halo = jnp.dot(order_ref[...], halo, preferred_element_type=jnp.float32).astype(jnp.bfloat16)
    halo = expanded(halo).reshape(deep_w, SUBLANES, chunk)
    halo = halo * jnp.where(row < outer_w, up, down)
    side = jnp.dot(left_at_ref[...], left_ref[...], preferred_element_type=jnp.float32)
    side = side + jnp.dot(right_at_ref[...], right_ref[...], preferred_element_type=jnp.float32)
    side = expanded(side.astype(jnp.bfloat16)).reshape(deep_h + 2, SUBLANES, chunk)
    side = side * jnp.where(row % outer_w == 0, left, right)
    plane = lax.broadcasted_iota(jnp.int32, (deep_h + 2, SUBLANES, 1), 0)
    at = lax.broadcasted_iota(jnp.int32, (deep_h + 2, SUBLANES, 1), 1)
    side = side * jnp.where((plane == 0) & (at < outer_w), up, 1.0)
    side = side * jnp.where((plane == deep_h + 1) & (at >= SUBLANES - outer_w), down, 1.0)

    for a in range(deep_h):
        values = e_ref[a].astype(jnp.float32).reshape(deep_w, SUBLANES, chunk)
        held[a + 1, 1 : deep_w + 1] = values
        if a == deep_h - 1:
            held[0, 1 : deep_w + 1] = jnp.where(
                row < outer_w, halo, pltpu.roll(values, outer_w, 1)
            )
        if a == 0:
            held[deep_h + 1, 1 : deep_w + 1] = jnp.where(
                row >= SUBLANES - outer_w, halo, pltpu.roll(values, SUBLANES - outer_w, 1)
            )
    held[:, 0] = jnp.where(row % outer_w == 0, side, pltpu.roll(held[:, deep_w], 1, 1))
    held[:, deep_w + 1] = jnp.where(
        row % outer_w == outer_w - 1, side, pltpu.roll(held[:, 1], SUBLANES - 1, 1)
    )
    for low in range(0, chunk, 128):
        lanes = slice(low, low + 128)
        for a in range(deep_h):
            total = jnp.broadcast_to(bd_ref[:, lanes], (deep_w, SUBLANES, 128))
            for di in range(3):
                for dj in range(3):
                    total = total + held[a + di, dj : dj + deep_w, :, lanes] * wd_ref[
                        3 * di + dj : 3 * di + dj + 1, lanes
                    ].astype(jnp.float32)
            deep[step, a, :, lanes] = (
                gelu_erf(total).astype(jnp.bfloat16).reshape(count, 128)
            )

    @pl.when(step == pl.num_programs(0) - 1)
    def _():
        core = flag_ref[0]

        def projected(a):
            total = jnp.zeros((count, plan.width), jnp.float32)
            for piece in range(deep.shape[0]):
                total = total + jnp.dot(
                    deep[piece, a],
                    wp_ref[piece * chunk : (piece + 1) * chunk],
                    preferred_element_type=jnp.float32,
                )
            return total

        for block in range(plan.n_rows):
            sib_ref[block] = projected(2 * block + 1 - core).astype(jnp.bfloat16)
        for block in range(plan.n_rows):
            a = 2 * block + core
            own_ref[block] = projected(a) + (x_ref[a].astype(jnp.float32) + bp_ref[...])


def deepen(plan, flags, e, x, rows, cols, w_expand, b_expand, w_depth, b_depth, w_project, b_project, order):
    own = w_expand.shape[1]
    count = plan.depth_w * SUBLANES
    steps = own // CHUNK
    left_at, right_at = (jnp.asarray(m, jnp.bfloat16) for m in plan.sides())
    whole = lambda v: pl.BlockSpec(v.shape, lambda i: (0,) * v.ndim)
    columns = lambda v: pl.BlockSpec((v.shape[0], CHUNK), lambda i: (0, i))
    up, down = rows
    left, right = cols
    operands = (
        (flags, pl.BlockSpec(memory_space=pltpu.SMEM)),
        (e, pl.BlockSpec(e.shape[:2] + (CHUNK,), lambda i: (0, 0, i))),
        (x, whole(x)),
        (up, whole(up)),
        (down, whole(down)),
        (left, whole(left)),
        (right, whole(right)),
        (order, whole(order)),
        (left_at, whole(left_at)),
        (right_at, whole(right_at)),
        (w_expand, columns(w_expand)),
        (b_expand, columns(b_expand)),
        (w_depth, columns(w_depth)),
        (b_depth, columns(b_depth)),
        (w_project, whole(w_project)),
        (b_project, whole(b_project)),
    )
    half = (plan.n_rows, count, plan.width)
    return pl.pallas_call(
        functools.partial(depth_kernel, plan),
        grid=(steps,),
        in_specs=[spec for _, spec in operands],
        out_specs=[pl.BlockSpec(half, lambda i: (0, 0, 0))] * 2,
        out_shape=[
            jax.ShapeDtypeStruct(half, jnp.bfloat16),
            jax.ShapeDtypeStruct(half, jnp.float32),
        ],
        scratch_shapes=[
            pltpu.VMEM((plan.depth_h + 2, plan.depth_w + 2, SUBLANES, CHUNK), jnp.float32),
            pltpu.VMEM((steps, plan.depth_h, count, CHUNK), jnp.bfloat16),
        ],
        compiler_params=pltpu.CompilerParams(vmem_limit_bytes=VMEM_BYTES),
        cost_estimate=pl.CostEstimate(
            flops=2 * x.size * own, bytes_accessed=2 * e.size, transcendentals=0
        ),
        name="deepen",
    )(*[value for value, _ in operands])


def attend_kernel(
    plan, flag_ref, x_ref, gain_ref, wqkv_ref, wqkv_sib_ref, wo_ref, wo_sib_ref, bo_ref, bo_sib_ref,
    out_ref, values, qkv, attended,
):
    sources, tokens, width = x_ref.shape
    windows = tokens // SUBLANES
    span = sources * SUBLANES
    half = wo_ref.shape[0]
    for source in range(sources):
        values[:, source] = x_ref[source].astype(jnp.float32).reshape(windows, SUBLANES, width)
    full = values[...].reshape(windows * span, width)
    centred = full - jnp.mean(full, axis=-1, keepdims=True)
    spread = jnp.mean(centred * centred, axis=-1, keepdims=True)
    normed = (centred * lax.rsqrt(spread + 1e-05) * gain_ref[...]).astype(jnp.bfloat16)
    for side, weight in enumerate((wqkv_ref, wqkv_sib_ref)):
        for kind in range(3):
            qkv[kind, :, side * half : (side + 1) * half] = jnp.dot(
                normed, weight[:, kind * half : (kind + 1) * half], preferred_element_type=jnp.float32
            ).astype(jnp.bfloat16)
    heads = 128 // HEAD_DIM
    lane = lax.broadcasted_iota(jnp.int32, (1, 128), 1) // HEAD_DIM
    scale = HEAD_DIM ** (-0.5) * np.log2(np.e)
    for window in range(windows):
        rows = slice(window * span, (window + 1) * span)
        for low in range(0, width, 128):
            lanes = slice(low, low + 128)
            query, keys, value = (qkv[kind, rows, lanes] for kind in range(3))
            spread_query = jnp.concatenate(
                [jnp.where(lane == h, query, jnp.zeros_like(query)) for h in range(heads)], axis=0
            )
            scores = lax.dot_general(
                keys, spread_query, (((1,), (1,)), ((), ())), preferred_element_type=jnp.float32
            )
            top = jnp.max(scores, axis=0, keepdims=True)
            powers = jnp.exp2((scores - top) * scale)
            weights = powers * (1.0 / jnp.sum(powers, axis=0, keepdims=True))
            mixed = lax.dot_general(
                weights.astype(jnp.bfloat16), value, (((0,), (0,)), ((), ())),
                preferred_element_type=jnp.float32,
            )
            chosen = mixed[:span]
            for h in range(1, heads):
                chosen = jnp.where(lane == h, mixed[h * span : (h + 1) * span], chosen)
            attended[rows, lanes] = chosen.astype(jnp.bfloat16)
    first = flag_ref[0] == 0
    bias = jnp.concatenate(
        [
            jnp.where(first, bo_ref[...], bo_sib_ref[...]),
            jnp.where(first, bo_sib_ref[...], bo_ref[...]),
        ],
        axis=1,
    )
    summed = jnp.dot(attended[:, :half], wo_ref[...], preferred_element_type=jnp.float32)
    summed = summed + jnp.dot(attended[:, half:], wo_sib_ref[...], preferred_element_type=jnp.float32)
    result = values[...] + (summed + bias).reshape(values.shape)
    for target in range(sources):
        part = result[:, target].reshape(tokens, width).astype(jnp.bfloat16)
        for core in range(plan.n_ch):
            out_ref[target, core] = part[:, core * half : (core + 1) * half]


def attend_windows(plan, flags, arrived, ln_gain, w_qkv, w_qkv_sib, w_out, w_out_sib, b_out, b_out_sib):
    sources, tokens, width = arrived.shape
    windows = tokens // SUBLANES
    half = w_out.shape[0]
    operands = (arrived, ln_gain, w_qkv, w_qkv_sib, w_out, w_out_sib, b_out, b_out_sib)
    return pl.pallas_call(
        functools.partial(attend_kernel, plan),
        in_specs=[pl.BlockSpec(memory_space=pltpu.SMEM)]
        + [pl.BlockSpec(memory_space=pltpu.VMEM)] * len(operands),
        out_specs=pl.BlockSpec(memory_space=pltpu.VMEM),
        out_shape=jax.ShapeDtypeStruct((sources, plan.n_ch, tokens, half), jnp.bfloat16),
        scratch_shapes=[
            pltpu.VMEM((windows, sources, SUBLANES, width), jnp.float32),
            pltpu.VMEM((3, sources * tokens, width), jnp.bfloat16),
            pltpu.VMEM((sources * tokens, width), jnp.bfloat16),
        ],
        compiler_params=pltpu.CompilerParams(vmem_limit_bytes=VMEM_BYTES),
        cost_estimate=pl.CostEstimate(
            flops=8 * arrived.size * width, bytes_accessed=4 * arrived.size, transcendentals=0
        ),
        name="attend",
    )(flags, *operands)


def halo_rows(cells):
    count = lax.axis_size("gy")
    forward = [(i, i + 1) for i in range(count - 1)]
    backward = [(target, source) for source, target in forward]
    return lax.ppermute(cells[-1], "gy", forward), lax.ppermute(cells[0], "gy", backward)


def halo_cols(cells, rows):
    count = lax.axis_size("gx")
    up, down = rows

    def column(index):
        parts = [up[None], cells, down[None]]
        return jnp.concatenate(
            [lax.dynamic_slice_in_dim(part, index, 1, axis=1)[:, 0] for part in parts], axis=0
        )

    last = cells.shape[1] - 1
    if count == 2:
        met = lax.ppermute(
            column(jnp.where(lax.axis_index("gx") == 0, last, 0)), "gx", [(0, 1), (1, 0)]
        )
        return met, met
    forward = [(i, i + 1) for i in range(count - 1)]
    backward = [(target, source) for source, target in forward]
    return lax.ppermute(column(last), "gx", forward), lax.ppermute(column(0), "gx", backward)


def fast_device(
    plan, cells, w_expand, b_expand, w_depth, b_depth, w_project, b_project, ln_gain, w_qkv, w_out, b_out
):
    n_rows, n_cols, n_ch = plan.n_rows, plan.n_cols, plan.n_ch
    width = plan.width
    own_y, own_x, own_c = (lax.axis_index(axis) for axis in ("gy", "gx", "ch"))
    flags = jnp.stack(
        [own_c, own_y > 0, own_y < n_rows - 1, own_x > 0, own_x < n_cols - 1]
    ).astype(jnp.int32)
    order = jnp.asarray(plan.order(), jnp.bfloat16)
    swap = [(0, 1), (1, 0)]
    rows = halo_rows(cells)
    e, x = expand(plan, cells, w_expand, b_expand[None], order)
    cols = halo_cols(cells, rows)
    w_qkv = w_qkv.reshape(width, -1)
    w_qkv_sib, w_out_sib, b_out_sib = (
        lax.ppermute(value, "ch", swap) for value in (w_qkv, w_out, b_out[None])
    )
    sib, own = deepen(
        plan, flags, e, x, rows, cols, w_expand, b_expand[None], w_depth.reshape(9, -1), b_depth[None],
        w_project, b_project[None], order,
    )
    mixed = (own + lax.ppermute(sib, "ch", swap).astype(jnp.float32)).astype(jnp.bfloat16)
    mixed = mixed.reshape(n_rows * n_cols, -1, width)
    arrived = lax.all_to_all(mixed, ("gy", "gx"), 0, 0, tiled=True)
    leaving = attend_windows(
        plan, flags, arrived, ln_gain[None], w_qkv, w_qkv_sib, w_out, w_out_sib, b_out[None], b_out_sib
    )
    leaving = leaving.reshape((n_rows * n_cols * n_ch,) + leaving.shape[2:])
    returned = lax.all_to_all(leaving, ("gy", "gx", "ch"), 0, 0, tiled=True)
    returned = returned.reshape(
        n_rows, n_cols, n_ch, SUBLANES, plan.outer_h, plan.outer_w, width // n_ch
    )
    return returned.transpose(4, 0, 2, 5, 1, 3, 6).reshape(cells.shape[0], cells.shape[1], -1)


def per_device(cells, *rest):
    plan = Plan(cells, *(lax.axis_size(axis) for axis in ("gy", "gx", "ch")))
    if plan.fits:
        return fast_device(plan, cells, *rest)
    return general_device(cells, *rest)


def solution(mesh):
    placed = (
        P(("grp", "gy"), "gx", None),
        P(None, "ch"),
        P("ch"),
        P(None, None, "ch"),
        P("ch"),
        P("ch", None),
        P(),
        P(),
        P(None, None, "ch"),
        P("ch", None),
        P("ch"),
    )
    return jax.shard_map(
        per_device,
        mesh=mesh,
        in_specs=placed,
        out_specs=P(("grp", "gy"), "gx", "ch"),
        check_vma=False,
    )
```

```python
import functools

import jax
import jax.numpy as jnp
import numpy as np
from jax import lax
from jax.experimental import pallas as pl
from jax.experimental.pallas import tpu as pltpu
from jax.sharding import PartitionSpec as P

SUBLANES = 8
CHUNK = 512
VMEM_BYTES = 24 * 2**20
EDGES_VMEM_BYTES = 61 * 2**20
B_EXPAND, B_DEPTH, B_OUT, B_PROJECT, GAIN = (slice(row, row + 1) for row in range(9, 14))

HEAD_DIM = 32
GRID = 8


def extended(block, sides, width):
    for axis, dim in sides:
        count = lax.axis_size(axis)
        forward = [(i, i + 1) for i in range(count - 1)]
        backward = [(target, source) for source, target in forward]
        low = lax.ppermute(
            lax.slice_in_dim(block, block.shape[dim] - width, None, axis=dim), axis, forward
        )
        high = lax.ppermute(lax.slice_in_dim(block, 0, width, axis=dim), axis, backward)
        block = jnp.concatenate([low, block, high], axis=dim)
    return block


def gelu_exact(values):
    return jax.nn.gelu(values, approximate=False)


def expand_cells(source, w_expand, b_expand):
    pre = jnp.einsum("hwc,ce->hwe", source, w_expand, preferred_element_type=jnp.float32)
    return gelu_exact(pre + b_expand).astype(jnp.bfloat16)


def depthwise(padded, w_depth, b_depth, tile_h, tile_w):
    summed = jnp.zeros((tile_h, tile_w, padded.shape[2]), jnp.float32)
    for row_off in range(3):
        for col_off in range(3):
            summed = summed + padded[row_off : row_off + tile_h, col_off : col_off + tile_w].astype(
                jnp.float32
            ) * w_depth[row_off, col_off].astype(jnp.float32)
    return gelu_exact(summed + b_depth).astype(jnp.bfloat16)


def split_order(tile, depth_h, depth_w):
    tile_h, tile_w, width = tile.shape
    shaped = tile.reshape(tile_h // depth_h, depth_h, tile_w // depth_w, depth_w, width)
    return shaped.transpose(1, 0, 3, 2, 4)


def join_order(arranged):
    depth_h, outer_h, depth_w, outer_w, width = arranged.shape
    return arranged.transpose(1, 0, 3, 2, 4).reshape(outer_h * depth_h, outer_w * depth_w, width)


def into_windows(arrived, steps_h, steps_w):
    local_h, span_h, local_w, span_w, width = arrived.shape
    grouped = arrived.reshape(local_h, GRID, steps_h, local_w, GRID, steps_w, width)
    grouped = grouped.transpose(2, 0, 5, 3, 1, 4, 6)
    return grouped.reshape(steps_h * local_h * steps_w * local_w, GRID * GRID, width)


def out_of_windows(windows, local_h, steps_h, local_w, steps_w):
    width = windows.shape[2]
    grouped = windows.reshape(steps_h, local_h, steps_w, local_w, GRID, GRID, width)
    grouped = grouped.transpose(1, 4, 0, 3, 5, 2, 6)
    return grouped.reshape(local_h, GRID * steps_h, local_w, GRID * steps_w, width)


def attend(window_full, ln_gain, w_qkv):
    values = window_full.astype(jnp.float32)
    centre = jnp.mean(values, axis=-1, keepdims=True)
    centered = values - centre
    spread = jnp.mean(centered * centered, axis=-1, keepdims=True)
    normed = (centered * lax.rsqrt(spread + 1e-05) * ln_gain).astype(jnp.bfloat16)
    projected = jnp.einsum(
        "wtc,cke->kwte", normed, w_qkv, preferred_element_type=jnp.float32
    ).astype(jnp.bfloat16)
    window_count = projected.shape[1]
    tokens = projected.shape[2]
    own_width = projected.shape[3]
    heads_own = own_width // HEAD_DIM
    shaped = projected.reshape(3, window_count, tokens, heads_own, HEAD_DIM)
    scores = jnp.einsum(
        "wqhd,wkhd->whqk", shaped[0], shaped[1], preferred_element_type=jnp.float32
    ) * HEAD_DIM ** (-0.5)
    weights = jax.nn.softmax(scores, axis=-1).astype(jnp.bfloat16)
    heads_out = jnp.einsum(
        "whqk,wkhd->wqhd", weights, shaped[2], preferred_element_type=jnp.float32
    ).astype(jnp.bfloat16)
    return heads_out.reshape(window_count, tokens, own_width)


def general_device(
    cells, w_expand, b_expand, w_depth, b_depth, w_project, b_project, ln_gain, w_qkv, w_out, b_out
):
    tile_h, tile_w, width = cells.shape
    n_rows = lax.axis_size("gy")
    n_cols = lax.axis_size("gx")
    half = width // lax.axis_size("ch")
    own = lax.axis_index("ch")
    stride_h = tile_h * n_rows // GRID
    stride_w = tile_w * n_cols // GRID
    depth_h = min(tile_h, stride_h)
    depth_w = min(tile_w, stride_w)
    steps_h = stride_h // depth_h
    steps_w = stride_w // depth_w
    local_h = depth_h // n_rows
    local_w = depth_w // n_cols
    expanded = expand_cells(cells, w_expand, b_expand)
    padded = extended(expanded, (("gy", 0), ("gx", 1)), 1)
    depth = depthwise(padded, w_depth, b_depth, tile_h, tile_w)
    partial_value = jnp.einsum("hwe,ec->hwc", depth, w_project, preferred_element_type=jnp.float32)
    share = lax.psum_scatter(
        partial_value.astype(jnp.bfloat16), "ch", scatter_dimension=2, tiled=True
    ).astype(jnp.float32)
    cells_own = lax.dynamic_slice_in_dim(cells, own * half, half, 2)
    bias_own = lax.dynamic_slice_in_dim(b_project, own * half, half, 0)
    mixed_own = (cells_own.astype(jnp.float32) + share + bias_own).astype(jnp.bfloat16)
    arranged = split_order(mixed_own, depth_h, depth_w)
    arrived = lax.all_to_all(
        lax.all_to_all(arranged, "gy", split_axis=0, concat_axis=1, tiled=True),
        "gx",
        split_axis=2,
        concat_axis=3,
        tiled=True,
    )
    window_own = into_windows(arrived, steps_h, steps_w)
    window_full = lax.all_gather(window_own, "ch", axis=2, tiled=True)
    heads_out = attend(window_full, ln_gain, w_qkv)
    attention_terms = jnp.einsum(
        "wte,ec->wtc", heads_out, w_out, preferred_element_type=jnp.float32
    )
    attention_own = lax.psum_scatter(
        attention_terms.astype(jnp.bfloat16), "ch", scatter_dimension=2, tiled=True
    ).astype(jnp.float32)
    outcome = (window_own.astype(jnp.float32) + attention_own + b_out).astype(jnp.bfloat16)
    leaving = out_of_windows(outcome, local_h, steps_h, local_w, steps_w)
    returned = lax.all_to_all(
        lax.all_to_all(leaving, "gy", split_axis=1, concat_axis=0, tiled=True),
        "gx",
        split_axis=3,
        concat_axis=2,
        tiled=True,
    )
    return join_order(returned)


class Plan:
    def __init__(self, cells, n_rows, n_cols, n_ch):
        tile_h, tile_w, self.width = cells.shape
        stride_h, stride_w = tile_h * n_rows // GRID, tile_w * n_cols // GRID
        self.depth_h, self.depth_w = min(tile_h, stride_h), min(tile_w, stride_w)
        self.outer_h, self.outer_w = tile_h // self.depth_h, tile_w // self.depth_w
        self.n_rows, self.n_cols, self.n_ch = n_rows, n_cols, n_ch
        self.span_w = self.depth_w // n_ch
        self.half_h = self.depth_h // 2
        self.fits = (
            (n_rows, n_cols, n_ch) == (4, 2, 2)
            and self.depth_h == stride_h
            and self.depth_w == stride_w
            and self.outer_h * self.outer_w == SUBLANES
            and min(self.outer_h, self.outer_w) >= 2
            and self.depth_h % n_rows == 0
            and self.span_w % (2 * n_cols) == 0
            and self.width % CHUNK == 0
        )

    def columns(self, shape, core):
        token = lax.broadcasted_iota(jnp.int32, shape, 0)
        slot, j = token // SUBLANES, token % self.outer_w
        return token, j * self.depth_w + core * self.span_w + slot - 1

    def order(self, core):
        wide = self.outer_w * self.depth_w
        shape = ((self.span_w + 2) * SUBLANES, self.outer_h * wide)
        token, column = self.columns(shape, core)
        place = token // self.outer_w % self.outer_h * wide + column
        inside = (column >= 0) & (column < wide)
        return one_hot(jnp.where(inside, place, -1))

    def row_order(self, core):
        shape = ((self.span_w + 2) * SUBLANES, self.outer_w * self.depth_w)
        return one_hot(self.columns(shape, core)[1])

    def column_order(self, part):
        shape = ((self.half_h + 2) * SUBLANES, self.outer_h * self.depth_h + 2)
        token = lax.broadcasted_iota(jnp.int32, shape, 0)
        i, plane = token // self.outer_w % self.outer_h, token // SUBLANES
        return one_hot(i * self.depth_h + part * self.half_h + plane)


def one_hot(place):
    return (lax.broadcasted_iota(jnp.int32, place.shape, 1) == place).astype(jnp.bfloat16)


def gelu_erf(values):
    return (0.5 * values) * (1.0 + lax.erf(values * 0.5**0.5))


def in_vmem(count):
    return [pl.BlockSpec(memory_space=pltpu.VMEM)] * count


def grow(plan, source_ref, weight, small, e_ref):
    slots = plan.span_w + 2
    for low_a in range(0, plan.depth_h, plan.half_h):
        planes = slice(low_a, low_a + plan.half_h)
        source = source_ref[planes].reshape(-1, plan.width)
        for low in range(0, weight.shape[1], CHUNK):
            part = slice(low, low + CHUNK)
            pre = jnp.dot(source, weight[:, part], preferred_element_type=jnp.float32)
            e_ref[planes, :, part] = (
                gelu_erf(pre + small[B_EXPAND, part])
                .astype(jnp.bfloat16)
                .reshape(plan.half_h, slots * SUBLANES, CHUNK)
            )


def expand_first_kernel(plan, flag_ref, cells_ref, w_ref, small_ref, e_ref, x_ref, ordered_ref):
    order = plan.order(flag_ref[0])
    for a in range(plan.depth_h):
        block = cells_ref[:, a].reshape(-1, plan.width)
        picked = jnp.dot(order, block, preferred_element_type=jnp.float32)
        ordered_ref[a] = picked.astype(jnp.bfloat16)
        x_ref[a] = picked[SUBLANES:-SUBLANES].astype(jnp.bfloat16)
    grow(plan, ordered_ref, w_ref, small_ref, e_ref)


def expand_first(plan, flags, cells, weight, small):
    shaped = cells.reshape(plan.outer_h, plan.depth_h, -1, plan.width)
    rows = (plan.span_w + 2) * SUBLANES
    return pl.pallas_call(
        functools.partial(expand_first_kernel, plan),
        in_specs=[pl.BlockSpec(memory_space=pltpu.SMEM)] + in_vmem(3),
        out_specs=in_vmem(3),
        out_shape=[
            jax.ShapeDtypeStruct((plan.depth_h, rows, weight.shape[1]), jnp.bfloat16),
            jax.ShapeDtypeStruct((plan.depth_h, plan.span_w * SUBLANES, plan.width), jnp.bfloat16),
            jax.ShapeDtypeStruct((plan.depth_h, rows, plan.width), jnp.bfloat16),
        ],
        compiler_params=pltpu.CompilerParams(vmem_limit_bytes=VMEM_BYTES),
        cost_estimate=pl.CostEstimate(
            flops=8 * cells.size * weight.shape[1], bytes_accessed=8 * cells.size, transcendentals=0
        ),
        name="expand_first",
    )(flags, shaped, weight, small)


def expand_second_kernel(plan, ordered_ref, w_ref, small_ref, *refs):
    count = (len(refs) - 2) // 2
    others, (e_ref, *kept), sems = refs[:count], refs[count:-1], refs[-1]
    copies = [
        pltpu.make_async_copy(*pair, sems.at[i]) for i, pair in enumerate(zip((w_ref, *others), kept))
    ]
    for copy in copies:
        copy.start()
    grow(plan, ordered_ref, w_ref, small_ref, e_ref)
    for copy in copies:
        copy.wait()


def expand_second(plan, ordered, weight, small, others):
    kept = weight, *others
    return pl.pallas_call(
        functools.partial(expand_second_kernel, plan),
        in_specs=in_vmem(3) + [pl.BlockSpec(memory_space=pl.ANY)] * len(others),
        out_specs=in_vmem(1 + len(kept)),
        out_shape=[
            jax.ShapeDtypeStruct((*ordered.shape[:2], weight.shape[1]), jnp.bfloat16),
            *(jax.ShapeDtypeStruct(v.shape, v.dtype) for v in kept),
        ],
        scratch_shapes=[pltpu.SemaphoreType.DMA((len(kept),))],
        compiler_params=pltpu.CompilerParams(vmem_limit_bytes=VMEM_BYTES),
        cost_estimate=pl.CostEstimate(
            flops=2 * ordered.size * weight.shape[1], bytes_accessed=4 * ordered.size, transcendentals=0
        ),
        name="expand_second",
    )(ordered, weight, small, *others)


def deepen_kernel(
    plan, targets, flag_ref, e_own_ref, e_sib_ref, x_ref, up_ref, down_ref, beside_ref, we_ref, we_sib_ref,
    small_ref, small_sib_ref, wp_ref, wp_sib_ref, *rest,
):
    *outs, held, deep, mixed = rest[-len(targets) - 3 :]
    core, up, down, left, right, own_y, own_x = (flag_ref[i] for i in range(7))
    far = targets[0][0] // 2
    part = (own_y // 2) ^ far
    base = part * plan.half_h
    planes, slots, outer_w = plan.half_h + 2, plan.span_w + 2, plan.outer_w
    own = we_ref.shape[1]
    row = lax.broadcasted_iota(jnp.int32, (1, SUBLANES, CHUNK), 1)
    plane = lax.broadcasted_iota(jnp.int32, (planes, SUBLANES, CHUNK), 0)
    at = lax.broadcasted_iota(jnp.int32, (planes, SUBLANES, CHUNK), 1)
    first = part == 0

    edge = jnp.where(first, up, down).astype(jnp.float32)
    beside = jnp.where(core == 0, left, right).astype(jnp.float32)
    side_mask = beside * jnp.where(
        (plane == part * (planes - 1)) & (at // outer_w == part * (plan.outer_h - 1)), edge, 1.0
    )
    low_rows = jnp.where(first, outer_w, 0)
    high_rows = outer_w - low_rows
    at_side = row % outer_w == core * (outer_w - 1)
    halo_cells = jnp.where(first, up_ref[...], down_ref[...])
    halo_cells = jnp.dot(
        plan.row_order(core), halo_cells, preferred_element_type=jnp.float32
    ).astype(jnp.bfloat16)
    side_cells = jnp.dot(
        plan.column_order(part), beside_ref[...], preferred_element_type=jnp.float32
    ).astype(jnp.bfloat16)
    outside = jnp.concatenate([halo_cells, side_cells], axis=0)
    before = lax.rem(base + plan.depth_h - 1, plan.depth_h)
    after = lax.rem(base + plan.half_h, plan.depth_h)

    sides = (e_own_ref, we_ref, small_ref), (e_sib_ref, we_sib_ref, small_sib_ref)
    for side, (e_ref, we, small) in enumerate(sides):
        for low in range(0, own, CHUNK):
            lanes = slice(low, low + CHUNK)
            pre = jnp.dot(outside, we[:, lanes], preferred_element_type=jnp.float32)
            grown = gelu_erf(pre + small[B_EXPAND, lanes])
            halo = grown[: slots * SUBLANES].reshape(slots, SUBLANES, CHUNK) * edge
            beside_cells = grown[slots * SUBLANES :].reshape(planes, SUBLANES, CHUNK) * side_mask

            def plane_of(index):
                return e_ref[index, :, lanes].astype(jnp.float32).reshape(slots, SUBLANES, CHUNK)

            for p in range(1, planes - 1):
                held[p] = plane_of(base + p - 1)
            values = plane_of(before)
            held[0] = jnp.where(row < low_rows, halo, pltpu.roll(values, low_rows, 1))
            values = plane_of(after)
            held[planes - 1] = jnp.where(
                row >= SUBLANES - high_rows,
                halo,
                pltpu.roll(values, lax.rem(SUBLANES - high_rows, SUBLANES), 1),
            )
            slot = core * (slots - 1)
            held[:, slot] = jnp.where(at_side, beside_cells, held[:, slot])
            for lane in range(0, CHUNK, 128):
                here = slice(lane, lane + 128)
                now = slice(low + lane, low + lane + 128)
                for a in range(plan.half_h):
                    total = jnp.broadcast_to(
                        small[B_DEPTH, now], (plan.span_w, SUBLANES, 128)
                    )
                    for di in range(3):
                        for dj in range(3):
                            tap = small[3 * di + dj : 3 * di + dj + 1, now]
                            total = total + held[a + di, dj : dj + plan.span_w, :, here] * tap
                    deep[a, :, side * own + low + lane : side * own + low + lane + 128] = (
                        gelu_erf(total).astype(jnp.bfloat16).reshape(-1, 128)
                    )
    source = deep[...].reshape(-1, 2 * own)
    total = jnp.dot(source[:, :own], wp_ref[...], preferred_element_type=jnp.float32)
    total = total + jnp.dot(source[:, own:], wp_sib_ref[...], preferred_element_type=jnp.float32)
    residual = x_ref[pl.ds(base, plan.half_h)].astype(jnp.float32) + small_ref[B_PROJECT, : plan.width]
    mixed[...] = (total.reshape(residual.shape) + residual).reshape(mixed.shape)
    planes_each = plan.depth_h // plan.n_rows
    rows = plan.span_w // plan.n_cols * SUBLANES
    for out, (dy, dx) in zip(outs, targets):
        block = (own_y ^ dy) & 1
        column = own_x ^ dx
        for k in range(planes_each):
            out[k * rows : (k + 1) * rows] = mixed[block * planes_each + k, column].astype(jnp.bfloat16)


def deepen(plan, targets, flags, e, x, rows, cols, weights, after):
    own = weights[0].shape[1]
    planes, slots = plan.half_h + 2, plan.span_w + 2
    tokens = plan.span_w * SUBLANES
    message = (plan.depth_h // plan.n_rows * (tokens // plan.n_cols), plan.width)
    operands = (*e, x, *rows, cols, *weights)
    return pl.pallas_call(
        functools.partial(deepen_kernel, plan, targets),
        in_specs=[pl.BlockSpec(memory_space=pltpu.SMEM)]
        + in_vmem(len(operands))
        + [pl.BlockSpec(memory_space=pl.ANY)] * len(after),
        out_specs=in_vmem(len(targets)),
        out_shape=[jax.ShapeDtypeStruct(message, jnp.bfloat16)] * len(targets),
        scratch_shapes=[
            pltpu.VMEM((planes, slots, SUBLANES, CHUNK), jnp.float32),
            pltpu.VMEM((plan.half_h, tokens, 2 * own), jnp.bfloat16),
            pltpu.VMEM((plan.half_h, plan.n_cols, tokens // plan.n_cols, plan.width), jnp.float32),
        ],
        compiler_params=pltpu.CompilerParams(vmem_limit_bytes=VMEM_BYTES),
        cost_estimate=pl.CostEstimate(
            flops=2 * x.size * own, bytes_accessed=4 * e[0].size, transcendentals=0
        ),
        name="deepen",
    )(flags, *operands, *after)


def attend_kernel(
    plan, targets, flag_ref, wqkv_ref, wqkv_sib_ref, wo_ref, wo_sib_ref, small_ref, small_sib_ref, *rest
):
    sources = len(targets)
    xs, (out_ref, values, qkv, attended) = rest[:sources], rest[sources:]
    tokens, width = xs[0].shape
    windows = tokens // SUBLANES
    span = sources * SUBLANES
    half = wo_ref.shape[0]
    for source in range(sources):
        values[:, source] = xs[source][...].astype(jnp.float32).reshape(windows, SUBLANES, width)
    full = values[...].reshape(windows * span, width)
    centred = full - jnp.mean(full, axis=-1, keepdims=True)
    spread = jnp.mean(centred * centred, axis=-1, keepdims=True)
    normed = (centred * lax.rsqrt(spread + 1e-05) * small_ref[GAIN, :width]).astype(jnp.bfloat16)
    for side, weight in enumerate((wqkv_ref, wqkv_sib_ref)):
        for kind in range(3):
            qkv[kind, :, side * half : (side + 1) * half] = jnp.dot(
                normed, weight[kind], preferred_element_type=jnp.float32
            ).astype(jnp.bfloat16)
    heads = 128 // HEAD_DIM
    lane = lax.broadcasted_iota(jnp.int32, (1, 128), 1) // HEAD_DIM
    scale = HEAD_DIM ** (-0.5) * np.log2(np.e)
    for window in range(windows):
        rows = slice(window * span, (window + 1) * span)
        for low in range(0, width, 128):
            lanes = slice(low, low + 128)
            query, keys, value = (qkv[kind, rows, lanes] for kind in range(3))
            spread_query = jnp.concatenate(
                [jnp.where(lane == h, query, jnp.zeros_like(query)) for h in range(heads)], axis=0
            )
            scores = lax.dot_general(
                keys, spread_query, (((1,), (1,)), ((), ())), preferred_element_type=jnp.float32
            )
            top = jnp.max(scores, axis=0, keepdims=True)
            powers = jnp.exp2((scores - top) * scale)
            weights = powers * (1.0 / jnp.sum(powers, axis=0, keepdims=True))
            mixed = lax.dot_general(
                weights.astype(jnp.bfloat16), value, (((0,), (0,)), ((), ())),
                preferred_element_type=jnp.float32,
            )
            chosen = mixed[:span]
            for h in range(1, heads):
                chosen = jnp.where(lane == h, mixed[h * span : (h + 1) * span], chosen)
            attended[rows, lanes] = chosen.astype(jnp.bfloat16)
    first = flag_ref[0] == 0
    bias = jnp.concatenate(
        [
            jnp.where(first, small_ref[B_OUT, :half], small_sib_ref[B_OUT, :half]),
            jnp.where(first, small_sib_ref[B_OUT, :half], small_ref[B_OUT, :half]),
        ],
        axis=1,
    )
    summed = jnp.dot(attended[:, :half], wo_ref[...], preferred_element_type=jnp.float32)
    summed = summed + jnp.dot(attended[:, half:], wo_sib_ref[...], preferred_element_type=jnp.float32)
    result = values[...] + (summed + bias).reshape(values.shape)
    for source, (dy, dx) in enumerate(targets):
        part = result[:, source].reshape(tokens, width).astype(jnp.bfloat16)
        target = (flag_ref[5] ^ dy) * plan.n_cols + (flag_ref[6] ^ dx)
        for core in range(plan.n_ch):
            out_ref[target, core] = part[:, core * half : (core + 1) * half]


def attend_windows(plan, targets, flags, arrived, weights):
    tokens, width = arrived[0].shape
    sources = len(targets)
    windows = tokens // SUBLANES
    half = width // plan.n_ch
    operands = (*weights, *arrived)
    return pl.pallas_call(
        functools.partial(attend_kernel, plan, targets),
        in_specs=[pl.BlockSpec(memory_space=pltpu.SMEM)] + in_vmem(len(operands)),
        out_specs=pl.BlockSpec(memory_space=pltpu.VMEM),
        out_shape=jax.ShapeDtypeStruct((sources, plan.n_ch, tokens, half), jnp.bfloat16),
        scratch_shapes=[
            pltpu.VMEM((windows, sources, SUBLANES, width), jnp.float32),
            pltpu.VMEM((3, sources * tokens, width), jnp.bfloat16),
            pltpu.VMEM((sources * tokens, width), jnp.bfloat16),
        ],
        compiler_params=pltpu.CompilerParams(vmem_limit_bytes=VMEM_BYTES),
        cost_estimate=pl.CostEstimate(
            flops=8 * sources * tokens * width * width, bytes_accessed=4 * width * width, transcendentals=0
        ),
        name="attend",
    )(flags, *operands)


def edges_kernel(group, column_ref, cells_hbm, taps_hbm, *refs):
    count = (len(refs) - 6) // 2
    vectors_hbm, (top_ref, bottom_ref, side_ref, small_ref, held, taps), (*vectors, sems) = (
        refs[:count], refs[count : count + 6], refs[count + 6 :]
    )
    rows, width = cells_hbm.shape[0], cells_hbm.shape[2]
    column = column_ref[0]
    start = pl.multiple_of(column // group * group, group)
    pairs = [
        (cells_hbm.at[0], top_ref),
        (cells_hbm.at[rows - 1], bottom_ref),
        (cells_hbm.at[:, pl.ds(start, group)], held),
        (taps_hbm, taps),
        *zip(vectors_hbm, vectors),
    ]
    copies = [pltpu.make_async_copy(*pair, sems.at[i]) for i, pair in enumerate(pairs)]
    for copy in copies:
        copy.start()
    shape = (rows, rows * group)
    pick = one_hot(lax.broadcasted_iota(jnp.int32, shape, 0) * group + (column - start))
    small_ref[...] = jnp.zeros_like(small_ref)
    for copy in copies:
        copy.wait()
    side_ref[...] = jnp.dot(
        pick, held[...].reshape(rows * group, width), preferred_element_type=jnp.float32
    ).astype(jnp.bfloat16)
    for i in range(3):
        small_ref[3 * i : 3 * i + 3] = taps[i].astype(jnp.float32)
    for i, vector in enumerate(vectors):
        small_ref[9 + i : 10 + i, : vector.shape[1]] = vector[...]


def edges(cells, column, w_depth, vectors):
    rows, cols, width = cells.shape
    group = 2 * SUBLANES
    operands = (cells, w_depth, *vectors)
    return pl.pallas_call(
        functools.partial(edges_kernel, group),
        in_specs=[pl.BlockSpec(memory_space=pltpu.SMEM)]
        + [pl.BlockSpec(memory_space=pltpu.HBM)] * len(operands),
        out_specs=in_vmem(4),
        out_shape=[jax.ShapeDtypeStruct((count, width), cells.dtype) for count in (cols, cols, rows)]
        + [jax.ShapeDtypeStruct((group, w_depth.shape[2]), jnp.float32)],
        scratch_shapes=[
            pltpu.VMEM((rows, group, width), cells.dtype),
            *(pltpu.VMEM(v.shape, v.dtype) for v in operands[1:]),
            pltpu.SemaphoreType.DMA((len(operands) + 2,)),
        ],
        compiler_params=pltpu.CompilerParams(vmem_limit_bytes=EDGES_VMEM_BYTES),
        name="edges",
    )(column[None], *operands)


def halo_rows(top, bottom):
    count = lax.axis_size("gy")
    forward = [(i, i + 1) for i in range(count - 1)]
    backward = [(target, source) for source, target in forward]
    return lax.ppermute(bottom, "gy", forward), lax.ppermute(top, "gy", backward)


def halo_column(column, rows, index):
    above, below = (lax.dynamic_slice_in_dim(row, index, 1, axis=0) for row in rows)
    return lax.ppermute(jnp.concatenate([above, column, below], axis=0), "gx", [(0, 1), (1, 0)])


def send_to(value, dy, dx):
    n_rows, n_cols = lax.axis_size("gy"), lax.axis_size("gx")
    pairs = [
        (y * n_cols + x, (y ^ dy) * n_cols + (x ^ dx)) for y in range(n_rows) for x in range(n_cols)
    ]
    return lax.ppermute(value, ("gy", "gx"), pairs)


def fast_device(
    plan, cells, w_expand, b_expand, w_depth, b_depth, w_project, b_project, ln_gain, w_qkv, w_out, b_out
):
    n_rows, n_cols, n_ch = plan.n_rows, plan.n_cols, plan.n_ch
    width = plan.width
    own_y, own_x, own_c = (lax.axis_index(axis) for axis in ("gy", "gx", "ch"))
    flags = jnp.stack(
        [own_c, own_y > 0, own_y < n_rows - 1, own_x > 0, own_x < n_cols - 1, own_y, own_x]
    ).astype(jnp.int32)
    index = jnp.where(own_x == 0, cells.shape[1] - 1, 0)
    vectors = tuple(v[None] for v in (b_expand, b_depth, b_out, b_project, ln_gain))
    top, bottom, column, small = edges(cells, index, w_depth, vectors)
    top, w_expand, w_project = lax.optimization_barrier((top, w_expand, w_project))
    rows = halo_rows(top, bottom)

    def both(value):
        return value, lax.ppermute(value, "ch", [(0, 1), (1, 0)])

    w_expand, w_project, small = both(w_expand), both(w_project), both(small)
    flags, w_project_sib = lax.optimization_barrier((flags, w_project[1]))
    e_sib, x, ordered = expand_first(plan, flags, cells, w_expand[1], small[1])
    e_own, *kept = expand_second(
        plan, ordered, w_expand[0], small[0], (w_project[0], w_qkv.transpose(1, 0, 2), w_out)
    )
    *rows, x, e_own = lax.optimization_barrier((*rows, x, e_own))
    e = e_own, e_sib
    cols = halo_column(column, rows, index)
    cols, w_qkv, w_out = lax.optimization_barrier((cols, *kept[2:]))
    w_qkv, w_out = both(w_qkv), both(w_out)
    weights = (kept[0], w_expand[1], *small, kept[1], w_project_sib)
    far = [(dy, dx) for dy in (2, 3) for dx in (0, 1)]
    near = [(1, 0), (1, 1), (0, 1), (0, 0)]
    early = deepen(plan, far, flags, e, x, rows, cols, weights, ())
    *early, w_qkv_sib, w_out_sib = lax.optimization_barrier((*early, w_qkv[1], w_out[1]))
    w_qkv, w_out = (w_qkv[0], w_qkv_sib), (w_out[0], w_out_sib)
    arrived = [send_to(value, *target) for value, target in zip(early, far)]
    late = deepen(plan, near, flags, e, x, rows, cols, weights, early)
    *late, arrived[0] = lax.optimization_barrier((*late, arrived[0]))
    arrived = [send_to(value, *target) for value, target in zip(late[:-1], near)] + [late[-1], *arrived]
    leaving = attend_windows(
        plan, near + far, flags, arrived, (*w_qkv, *w_out, *small)
    )
    leaving = leaving.reshape((n_rows * n_cols * n_ch,) + leaving.shape[2:])
    returned = lax.all_to_all(leaving, ("gy", "gx", "ch"), 0, 0, tiled=True)
    returned = returned.reshape(
        n_rows, n_cols, n_ch, plan.depth_h // n_rows, plan.span_w // n_cols, plan.outer_h, plan.outer_w, -1
    )
    return returned.transpose(5, 0, 3, 6, 2, 1, 4, 7).reshape(cells.shape[0], cells.shape[1], -1)


def per_device(cells, *rest):
    plan = Plan(cells, *(lax.axis_size(axis) for axis in ("gy", "gx", "ch")))
    if plan.fits:
        return fast_device(plan, cells, *rest)
    return general_device(cells, *rest)


def solution(mesh):
    placed = (
        P(("grp", "gy"), "gx", None),
        P(None, "ch"),
        P("ch"),
        P(None, None, "ch"),
        P("ch"),
        P("ch", None),
        P(),
        P(),
        P(None, None, "ch"),
        P("ch", None),
        P("ch"),
    )
    return jax.shard_map(
        per_device,
        mesh=mesh,
        in_specs=placed,
        out_specs=P(("grp", "gy"), "gx", "ch"),
        check_vma=False,
    )
```

```python
import functools

import jax
import jax.numpy as jnp
import numpy as np
from jax import lax
from jax.experimental import pallas as pl
from jax.experimental.pallas import tpu as pltpu
from jax.sharding import PartitionSpec as P

SUBLANES = 8
CHUNK = 512
VMEM_BYTES = 24 * 2**20
EDGES_VMEM_BYTES = 61 * 2**20
B_EXPAND, B_DEPTH, B_OUT, B_PROJECT, GAIN = (slice(row, row + 1) for row in range(9, 14))

HEAD_DIM = 32
GRID = 8


def extended(block, sides, width):
    for axis, dim in sides:
        count = lax.axis_size(axis)
        forward = [(i, i + 1) for i in range(count - 1)]
        backward = [(target, source) for source, target in forward]
        low = lax.ppermute(
            lax.slice_in_dim(block, block.shape[dim] - width, None, axis=dim), axis, forward
        )
        high = lax.ppermute(lax.slice_in_dim(block, 0, width, axis=dim), axis, backward)
        block = jnp.concatenate([low, block, high], axis=dim)
    return block


def gelu_exact(values):
    return jax.nn.gelu(values, approximate=False)


def expand_cells(source, w_expand, b_expand):
    pre = jnp.einsum("hwc,ce->hwe", source, w_expand, preferred_element_type=jnp.float32)
    return gelu_exact(pre + b_expand).astype(jnp.bfloat16)


def depthwise(padded, w_depth, b_depth, tile_h, tile_w):
    summed = jnp.zeros((tile_h, tile_w, padded.shape[2]), jnp.float32)
    for row_off in range(3):
        for col_off in range(3):
            summed = summed + padded[row_off : row_off + tile_h, col_off : col_off + tile_w].astype(
                jnp.float32
            ) * w_depth[row_off, col_off].astype(jnp.float32)
    return gelu_exact(summed + b_depth).astype(jnp.bfloat16)


def split_order(tile, depth_h, depth_w):
    tile_h, tile_w, width = tile.shape
    shaped = tile.reshape(tile_h // depth_h, depth_h, tile_w // depth_w, depth_w, width)
    return shaped.transpose(1, 0, 3, 2, 4)


def join_order(arranged):
    depth_h, outer_h, depth_w, outer_w, width = arranged.shape
    return arranged.transpose(1, 0, 3, 2, 4).reshape(outer_h * depth_h, outer_w * depth_w, width)


def into_windows(arrived, steps_h, steps_w):
    local_h, span_h, local_w, span_w, width = arrived.shape
    grouped = arrived.reshape(local_h, GRID, steps_h, local_w, GRID, steps_w, width)
    grouped = grouped.transpose(2, 0, 5, 3, 1, 4, 6)
    return grouped.reshape(steps_h * local_h * steps_w * local_w, GRID * GRID, width)


def out_of_windows(windows, local_h, steps_h, local_w, steps_w):
    width = windows.shape[2]
    grouped = windows.reshape(steps_h, local_h, steps_w, local_w, GRID, GRID, width)
    grouped = grouped.transpose(1, 4, 0, 3, 5, 2, 6)
    return grouped.reshape(local_h, GRID * steps_h, local_w, GRID * steps_w, width)


def attend(window_full, ln_gain, w_qkv):
    values = window_full.astype(jnp.float32)
    centre = jnp.mean(values, axis=-1, keepdims=True)
    centered = values - centre
    spread = jnp.mean(centered * centered, axis=-1, keepdims=True)
    normed = (centered * lax.rsqrt(spread + 1e-05) * ln_gain).astype(jnp.bfloat16)
    projected = jnp.einsum(
        "wtc,cke->kwte", normed, w_qkv, preferred_element_type=jnp.float32
    ).astype(jnp.bfloat16)
    window_count = projected.shape[1]
    tokens = projected.shape[2]
    own_width = projected.shape[3]
    heads_own = own_width // HEAD_DIM
    shaped = projected.reshape(3, window_count, tokens, heads_own, HEAD_DIM)
    scores = jnp.einsum(
        "wqhd,wkhd->whqk", shaped[0], shaped[1], preferred_element_type=jnp.float32
    ) * HEAD_DIM ** (-0.5)
    weights = jax.nn.softmax(scores, axis=-1).astype(jnp.bfloat16)
    heads_out = jnp.einsum(
        "whqk,wkhd->wqhd", weights, shaped[2], preferred_element_type=jnp.float32
    ).astype(jnp.bfloat16)
    return heads_out.reshape(window_count, tokens, own_width)


def general_device(
    cells, w_expand, b_expand, w_depth, b_depth, w_project, b_project, ln_gain, w_qkv, w_out, b_out
):
    tile_h, tile_w, width = cells.shape
    n_rows = lax.axis_size("gy")
    n_cols = lax.axis_size("gx")
    half = width // lax.axis_size("ch")
    own = lax.axis_index("ch")
    stride_h = tile_h * n_rows // GRID
    stride_w = tile_w * n_cols // GRID
    depth_h = min(tile_h, stride_h)
    depth_w = min(tile_w, stride_w)
    steps_h = stride_h // depth_h
    steps_w = stride_w // depth_w
    local_h = depth_h // n_rows
    local_w = depth_w // n_cols
    expanded = expand_cells(cells, w_expand, b_expand)
    padded = extended(expanded, (("gy", 0), ("gx", 1)), 1)
    depth = depthwise(padded, w_depth, b_depth, tile_h, tile_w)
    partial_value = jnp.einsum("hwe,ec->hwc", depth, w_project, preferred_element_type=jnp.float32)
    share = lax.psum_scatter(
        partial_value.astype(jnp.bfloat16), "ch", scatter_dimension=2, tiled=True
    ).astype(jnp.float32)
    cells_own = lax.dynamic_slice_in_dim(cells, own * half, half, 2)
    bias_own = lax.dynamic_slice_in_dim(b_project, own * half, half, 0)
    mixed_own = (cells_own.astype(jnp.float32) + share + bias_own).astype(jnp.bfloat16)
    arranged = split_order(mixed_own, depth_h, depth_w)
    arrived = lax.all_to_all(
        lax.all_to_all(arranged, "gy", split_axis=0, concat_axis=1, tiled=True),
        "gx",
        split_axis=2,
        concat_axis=3,
        tiled=True,
    )
    window_own = into_windows(arrived, steps_h, steps_w)
    window_full = lax.all_gather(window_own, "ch", axis=2, tiled=True)
    heads_out = attend(window_full, ln_gain, w_qkv)
    attention_terms = jnp.einsum(
        "wte,ec->wtc", heads_out, w_out, preferred_element_type=jnp.float32
    )
    attention_own = lax.psum_scatter(
        attention_terms.astype(jnp.bfloat16), "ch", scatter_dimension=2, tiled=True
    ).astype(jnp.float32)
    outcome = (window_own.astype(jnp.float32) + attention_own + b_out).astype(jnp.bfloat16)
    leaving = out_of_windows(outcome, local_h, steps_h, local_w, steps_w)
    returned = lax.all_to_all(
        lax.all_to_all(leaving, "gy", split_axis=1, concat_axis=0, tiled=True),
        "gx",
        split_axis=3,
        concat_axis=2,
        tiled=True,
    )
    return join_order(returned)


class Plan:
    def __init__(self, cells, n_rows, n_cols, n_ch):
        tile_h, tile_w, self.width = cells.shape
        stride_h, stride_w = tile_h * n_rows // GRID, tile_w * n_cols // GRID
        self.depth_h, self.depth_w = min(tile_h, stride_h), min(tile_w, stride_w)
        self.outer_h, self.outer_w = tile_h // self.depth_h, tile_w // self.depth_w
        self.n_rows, self.n_cols, self.n_ch = n_rows, n_cols, n_ch
        self.span_w = self.depth_w // n_ch
        self.half_h = self.depth_h // 2
        self.fits = (
            (n_rows, n_cols, n_ch) == (4, 2, 2)
            and self.depth_h == stride_h
            and self.depth_w == stride_w
            and self.outer_h * self.outer_w == SUBLANES
            and min(self.outer_h, self.outer_w) >= 2
            and self.depth_h % n_rows == 0
            and self.span_w % (2 * n_cols) == 0
            and self.width % CHUNK == 0
        )

    def columns(self, shape, core):
        token = lax.broadcasted_iota(jnp.int32, shape, 0)
        slot, j = token // SUBLANES, token % self.outer_w
        return token, j * self.depth_w + core * self.span_w + slot - 1

    def order(self, core):
        wide = self.outer_w * self.depth_w
        shape = ((self.span_w + 2) * SUBLANES, self.outer_h * wide)
        token, column = self.columns(shape, core)
        place = token // self.outer_w % self.outer_h * wide + column
        inside = (column >= 0) & (column < wide)
        return one_hot(jnp.where(inside, place, -1))

    def row_order(self, core):
        shape = ((self.span_w + 2) * SUBLANES, self.outer_w * self.depth_w)
        return one_hot(self.columns(shape, core)[1])

    def column_order(self):
        shape = ((self.depth_h + 2) * SUBLANES, self.outer_h * self.depth_h + 2)
        token = lax.broadcasted_iota(jnp.int32, shape, 0)
        return one_hot(token // self.outer_w % self.outer_h * self.depth_h + token // SUBLANES)


def one_hot(place):
    return (lax.broadcasted_iota(jnp.int32, place.shape, 1) == place).astype(jnp.bfloat16)


def gelu_erf(values):
    return (0.5 * values) * (1.0 + lax.erf(values * 0.5**0.5))


def in_vmem(count):
    return [pl.BlockSpec(memory_space=pltpu.VMEM)] * count


def grow(plan, source_ref, weight, small, e_ref):
    slots = plan.span_w + 2
    for low_a in range(0, plan.depth_h, plan.half_h):
        planes = slice(low_a, low_a + plan.half_h)
        source = source_ref[planes].reshape(-1, plan.width)
        for low in range(0, weight.shape[1], CHUNK):
            part = slice(low, low + CHUNK)
            pre = jnp.dot(source, weight[:, part], preferred_element_type=jnp.float32)
            e_ref[planes, :, part] = (
                gelu_erf(pre + small[B_EXPAND, part])
                .astype(jnp.bfloat16)
                .reshape(plan.half_h, slots * SUBLANES, CHUNK)
            )


def expand_first_kernel(plan, flag_ref, cells_ref, w_ref, small_ref, e_ref, x_ref, ordered_ref):
    order = plan.order(flag_ref[0])
    for a in range(plan.depth_h):
        block = cells_ref[:, a].reshape(-1, plan.width)
        picked = jnp.dot(order, block, preferred_element_type=jnp.float32)
        ordered_ref[a] = picked.astype(jnp.bfloat16)
        x_ref[a] = picked[SUBLANES:-SUBLANES].astype(jnp.bfloat16)
    grow(plan, ordered_ref, w_ref, small_ref, e_ref)


def expand_first(plan, flags, cells, weight, small):
    shaped = cells.reshape(plan.outer_h, plan.depth_h, -1, plan.width)
    rows = (plan.span_w + 2) * SUBLANES
    return pl.pallas_call(
        functools.partial(expand_first_kernel, plan),
        in_specs=[pl.BlockSpec(memory_space=pltpu.SMEM)] + in_vmem(3),
        out_specs=in_vmem(3),
        out_shape=[
            jax.ShapeDtypeStruct((plan.depth_h, rows, weight.shape[1]), jnp.bfloat16),
            jax.ShapeDtypeStruct((plan.depth_h, plan.span_w * SUBLANES, plan.width), jnp.bfloat16),
            jax.ShapeDtypeStruct((plan.depth_h, rows, plan.width), jnp.bfloat16),
        ],
        compiler_params=pltpu.CompilerParams(vmem_limit_bytes=VMEM_BYTES),
        cost_estimate=pl.CostEstimate(
            flops=8 * cells.size * weight.shape[1], bytes_accessed=8 * cells.size, transcendentals=0
        ),
        name="expand_first",
    )(flags, shaped, weight, small)


def expand_second_kernel(plan, ordered_ref, w_ref, small_ref, *refs):
    count = (len(refs) - 2) // 2
    others, (e_ref, *kept), sems = refs[:count], refs[count:-1], refs[-1]
    copies = [
        pltpu.make_async_copy(*pair, sems.at[i]) for i, pair in enumerate(zip((w_ref, *others), kept))
    ]
    for copy in copies:
        copy.start()
    grow(plan, ordered_ref, w_ref, small_ref, e_ref)
    for copy in copies:
        copy.wait()


def expand_second(plan, ordered, weight, small, others):
    kept = weight, *others
    return pl.pallas_call(
        functools.partial(expand_second_kernel, plan),
        in_specs=in_vmem(3) + [pl.BlockSpec(memory_space=pl.ANY)] * len(others),
        out_specs=in_vmem(1 + len(kept)),
        out_shape=[
            jax.ShapeDtypeStruct((*ordered.shape[:2], weight.shape[1]), jnp.bfloat16),
            *(jax.ShapeDtypeStruct(v.shape, v.dtype) for v in kept),
        ],
        scratch_shapes=[pltpu.SemaphoreType.DMA((len(kept),))],
        compiler_params=pltpu.CompilerParams(vmem_limit_bytes=VMEM_BYTES),
        cost_estimate=pl.CostEstimate(
            flops=2 * ordered.size * weight.shape[1], bytes_accessed=4 * ordered.size, transcendentals=0
        ),
        name="expand_second",
    )(ordered, weight, small, *others)


def outside_kernel_part(plan, flag_ref, one_ref, other_ref, beside_ref, sides, halo_ref, beside_out_ref):
    core, up, down, left, right = (flag_ref[i] for i in range(5))
    planes, slots, outer_w = plan.depth_h + 2, plan.span_w + 2, plan.outer_w
    order = plan.row_order(core)
    even = flag_ref[5] % 2 == 0
    rows = jnp.where(even, other_ref[...], one_ref[...]), jnp.where(even, one_ref[...], other_ref[...])
    cells = [jnp.dot(order, row, preferred_element_type=jnp.float32) for row in rows]
    cells.append(jnp.dot(plan.column_order(), beside_ref[...], preferred_element_type=jnp.float32))
    cells = jnp.concatenate([value.astype(jnp.bfloat16) for value in cells], axis=0)
    up, down = up.astype(jnp.float32), down.astype(jnp.float32)
    beside = jnp.where(core == 0, left, right).astype(jnp.float32)
    token = lax.broadcasted_iota(jnp.int32, (cells.shape[0], 1), 0) - 2 * slots * SUBLANES
    plane, i = token // SUBLANES, token // outer_w % plan.outer_h
    mask = jnp.where(token < -slots * SUBLANES, up, jnp.where(token < 0, down, beside))
    mask = mask * jnp.where((token >= 0) & (plane == 0) & (i == 0), up, 1.0)
    mask = mask * jnp.where((plane == planes - 1) & (i == plan.outer_h - 1), down, 1.0)
    for side, (weight, small) in enumerate(sides):
        own = weight.shape[1]
        for low in range(0, own, CHUNK):
            lanes = slice(low, low + CHUNK)
            there = slice(side * own + low, side * own + low + CHUNK)
            pre = jnp.dot(cells, weight[:, lanes], preferred_element_type=jnp.float32)
            grown = (gelu_erf(pre + small[B_EXPAND, lanes]) * mask).astype(jnp.bfloat16)
            halo_ref[0, :, there] = grown[: slots * SUBLANES]
            halo_ref[1, :, there] = grown[slots * SUBLANES : 2 * slots * SUBLANES]
            beside_out_ref[:, :, there] = grown[2 * slots * SUBLANES :].reshape(planes, SUBLANES, CHUNK)


def deepen_kernel(plan, targets, first, *refs):
    flag_ref, e_own_ref, e_sib_ref, x_ref, *refs = refs
    small_ref, small_sib_ref, wp_ref, wp_sib_ref, *refs = refs
    *refs, deep, mixed = refs
    if first:
        one_ref, other_ref, beside_ref, we_ref, we_sib_ref, *outs, halo_ref, sides_ref = refs
        weights = (we_ref, small_ref), (we_sib_ref, small_sib_ref)
        outside_kernel_part(plan, flag_ref, one_ref, other_ref, beside_ref, weights, halo_ref, sides_ref)
    else:
        halo_ref, sides_ref, *refs = refs
        outs = refs[-len(targets) :]
    core, own_y, own_x = flag_ref[0], flag_ref[5], flag_ref[6]
    each = plan.depth_h // plan.n_rows
    blocks = len({dy for dy, _ in targets})
    count, slots, outer_w = blocks * each, plan.span_w + 2, plan.outer_w
    base = (own_y ^ targets[0][0]) // blocks * count
    low_rows = jnp.where(base == 0, outer_w, 0)
    high_rows = jnp.where(base + count == plan.depth_h, outer_w, 0)
    row = lax.broadcasted_iota(jnp.int32, (1, SUBLANES, 128), 1)
    from_low, from_high = row < low_rows, row >= SUBLANES - high_rows
    at_left = row % outer_w == jnp.where(core == 0, 0, -1)
    at_right = row % outer_w == jnp.where(core == 0, -1, outer_w - 1)
    before = lax.rem(base + plan.depth_h - 1, plan.depth_h)
    after = lax.rem(base + count, plan.depth_h)

    own = wp_ref.shape[0]
    total = None
    for side, (e_ref, wp, small) in enumerate(
        ((e_own_ref, wp_ref, small_ref), (e_sib_ref, wp_sib_ref, small_sib_ref))
    ):
        for low in range(0, own, 128):
            now, there = slice(low, low + 128), slice(side * own + low, side * own + low + 128)
            taps = [small[tap : tap + 1, now] for tap in range(9)]
            bias = small[B_DEPTH, now]

            def shaped(values):
                return values.astype(jnp.float32).reshape(slots, SUBLANES, 128)

            def plane_of(p):
                values = shaped(e_ref[before if p == 0 else after if p == count + 1 else base + p - 1, :, now])
                if p == 0:
                    rolled = pltpu.roll(values, low_rows, 1)
                    values = jnp.where(from_low, shaped(halo_ref[0, :, there]), rolled)
                if p == count + 1:
                    rolled = pltpu.roll(values, lax.rem(SUBLANES - high_rows, SUBLANES), 1)
                    values = jnp.where(from_high, shaped(halo_ref[1, :, there]), rolled)
                met = sides_ref[base + p, :, there].astype(jnp.float32)[None]
                return jnp.concatenate(
                    [
                        jnp.where(at_left, met, values[:1]),
                        values[1:-1],
                        jnp.where(at_right, met, values[-1:]),
                    ],
                    axis=0,
                )

            window = [plane_of(0), plane_of(1)]
            for a in range(count):
                window.append(plane_of(a + 2))
                summed = jnp.broadcast_to(bias, (plan.span_w, SUBLANES, 128))
                for di in range(3):
                    for dj in range(3):
                        summed = summed + window[a + di][dj : dj + plan.span_w] * taps[3 * di + dj]
                deep[a, :, there] = gelu_erf(summed).astype(jnp.bfloat16).reshape(-1, 128)
            if (low + 128) % CHUNK == 0:
                rows = slice(low + 128 - CHUNK, low + 128)
                source = deep[:, :, side * own + rows.start : side * own + rows.stop]
                term = jnp.dot(
                    source.reshape(-1, CHUNK), wp[rows], preferred_element_type=jnp.float32
                )
                total = term if total is None else total + term
    residual = x_ref[pl.ds(base, count)].astype(jnp.float32) + small_ref[B_PROJECT, : plan.width]
    mixed[...] = (total.reshape(residual.shape) + residual).reshape(mixed.shape)
    rows = plan.span_w // plan.n_cols * SUBLANES
    for out, (dy, dx) in zip(outs, targets):
        block = (own_y ^ dy) % blocks
        column = own_x ^ dx
        for k in range(each):
            out[k * rows : (k + 1) * rows] = mixed[block * each + k, column].astype(jnp.bfloat16)


def deepen(plan, targets, flags, e, x, small, w_project, outside, first, after=()):
    own = w_project[0].shape[0]
    tokens = plan.span_w * SUBLANES
    each = plan.depth_h // plan.n_rows
    count = len({dy for dy, _ in targets}) * each
    message = (each * (tokens // plan.n_cols), plan.width)
    operands = (*e, x, *small, *w_project, *outside)
    out_shape = [jax.ShapeDtypeStruct(message, jnp.bfloat16)] * len(targets)
    if first:
        slots = (plan.span_w + 2) * SUBLANES
        out_shape.append(jax.ShapeDtypeStruct((2, slots, 2 * own), jnp.bfloat16))
        out_shape.append(jax.ShapeDtypeStruct((plan.depth_h + 2, SUBLANES, 2 * own), jnp.bfloat16))
    return pl.pallas_call(
        functools.partial(deepen_kernel, plan, targets, first),
        in_specs=[pl.BlockSpec(memory_space=pltpu.SMEM)]
        + in_vmem(len(operands))
        + [pl.BlockSpec(memory_space=pl.ANY)] * len(after),
        out_specs=in_vmem(len(out_shape)),
        out_shape=out_shape,
        scratch_shapes=[
            pltpu.VMEM((count, tokens, 2 * own), jnp.bfloat16),
            pltpu.VMEM((count, plan.n_cols, tokens // plan.n_cols, plan.width), jnp.float32),
        ],
        compiler_params=pltpu.CompilerParams(vmem_limit_bytes=VMEM_BYTES),
        cost_estimate=pl.CostEstimate(
            flops=count * tokens * 4 * own * plan.width, bytes_accessed=4 * e[0].size, transcendentals=0
        ),
        name="deepen",
    )(flags, *operands, *after)


def attend_kernel(
    plan, targets, flag_ref, wqkv_ref, wqkv_sib_ref, wo_ref, wo_sib_ref, small_ref, small_sib_ref, *rest
):
    sources = len(targets)
    xs, (out_ref, values, qkv, attended) = rest[:sources], rest[sources:]
    tokens, width = xs[0].shape
    windows = tokens // SUBLANES
    span = sources * SUBLANES
    half = wo_ref.shape[0]
    for source in range(sources):
        values[:, source] = xs[source][...].astype(jnp.float32).reshape(windows, SUBLANES, width)
    full = values[...].reshape(windows * span, width)
    centred = full - jnp.mean(full, axis=-1, keepdims=True)
    spread = jnp.mean(centred * centred, axis=-1, keepdims=True)
    normed = (centred * lax.rsqrt(spread + 1e-05) * small_ref[GAIN, :width]).astype(jnp.bfloat16)
    for side, weight in enumerate((wqkv_ref, wqkv_sib_ref)):
        for kind in range(3):
            qkv[kind, :, side * half : (side + 1) * half] = jnp.dot(
                normed, weight[kind], preferred_element_type=jnp.float32
            ).astype(jnp.bfloat16)
    heads = 128 // HEAD_DIM
    lane = lax.broadcasted_iota(jnp.int32, (1, 128), 1) // HEAD_DIM
    scale = HEAD_DIM ** (-0.5) * np.log2(np.e)
    for window in range(windows):
        rows = slice(window * span, (window + 1) * span)
        for low in range(0, width, 128):
            lanes = slice(low, low + 128)
            query, keys, value = (qkv[kind, rows, lanes] for kind in range(3))
            spread_query = jnp.concatenate(
                [jnp.where(lane == h, query, jnp.zeros_like(query)) for h in range(heads)], axis=0
            )
            scores = lax.dot_general(
                keys, spread_query, (((1,), (1,)), ((), ())), preferred_element_type=jnp.float32
            )
            top = jnp.max(scores, axis=0, keepdims=True)
            powers = jnp.exp2((scores - top) * scale)
            weights = powers * (1.0 / jnp.sum(powers, axis=0, keepdims=True))
            mixed = lax.dot_general(
                weights.astype(jnp.bfloat16), value, (((0,), (0,)), ((), ())),
                preferred_element_type=jnp.float32,
            )
            chosen = mixed[:span]
            for h in range(1, heads):
                chosen = jnp.where(lane == h, mixed[h * span : (h + 1) * span], chosen)
            attended[rows, lanes] = chosen.astype(jnp.bfloat16)
    first = flag_ref[0] == 0
    bias = jnp.concatenate(
        [
            jnp.where(first, small_ref[B_OUT, :half], small_sib_ref[B_OUT, :half]),
            jnp.where(first, small_sib_ref[B_OUT, :half], small_ref[B_OUT, :half]),
        ],
        axis=1,
    )
    summed = jnp.dot(attended[:, :half], wo_ref[...], preferred_element_type=jnp.float32)
    summed = summed + jnp.dot(attended[:, half:], wo_sib_ref[...], preferred_element_type=jnp.float32)
    result = values[...] + (summed + bias).reshape(values.shape)
    for source, (dy, dx) in enumerate(targets):
        part = result[:, source].reshape(tokens, width).astype(jnp.bfloat16)
        target = (flag_ref[5] ^ dy) * plan.n_cols + (flag_ref[6] ^ dx)
        for core in range(plan.n_ch):
            out_ref[target, core] = part[:, core * half : (core + 1) * half]


def attend_windows(plan, targets, flags, arrived, weights):
    tokens, width = arrived[0].shape
    sources = len(targets)
    windows = tokens // SUBLANES
    half = width // plan.n_ch
    operands = (*weights, *arrived)
    return pl.pallas_call(
        functools.partial(attend_kernel, plan, targets),
        in_specs=[pl.BlockSpec(memory_space=pltpu.SMEM)] + in_vmem(len(operands)),
        out_specs=pl.BlockSpec(memory_space=pltpu.VMEM),
        out_shape=jax.ShapeDtypeStruct((sources, plan.n_ch, tokens, half), jnp.bfloat16),
        scratch_shapes=[
            pltpu.VMEM((windows, sources, SUBLANES, width), jnp.float32),
            pltpu.VMEM((3, sources * tokens, width), jnp.bfloat16),
            pltpu.VMEM((sources * tokens, width), jnp.bfloat16),
        ],
        compiler_params=pltpu.CompilerParams(vmem_limit_bytes=VMEM_BYTES),
        cost_estimate=pl.CostEstimate(
            flops=8 * sources * tokens * width * width, bytes_accessed=4 * width * width, transcendentals=0
        ),
        name="attend",
    )(flags, *operands)


def edges_kernel(group, column_ref, row_ref, cells_hbm, taps_hbm, *refs):
    count = (len(refs) - 6) // 2
    vectors_hbm, (one_ref, other_ref, side_ref, small_ref, held, taps), (*vectors, sems) = (
        refs[:count], refs[count : count + 6], refs[count + 6 :]
    )
    rows, width = cells_hbm.shape[0], cells_hbm.shape[2]
    column, one = column_ref[0], row_ref[0]
    start = pl.multiple_of(column // group * group, group)
    pairs = [
        (cells_hbm.at[one], one_ref),
        (cells_hbm.at[rows - 1 - one], other_ref),
        (cells_hbm.at[:, pl.ds(start, group)], held),
        (taps_hbm, taps),
        *zip(vectors_hbm, vectors),
    ]
    copies = [pltpu.make_async_copy(*pair, sems.at[i]) for i, pair in enumerate(pairs)]
    for copy in copies:
        copy.start()
    shape = (rows, rows * group)
    pick = one_hot(lax.broadcasted_iota(jnp.int32, shape, 0) * group + (column - start))
    small_ref[...] = jnp.zeros_like(small_ref)
    for copy in copies:
        copy.wait()
    side_ref[...] = jnp.dot(
        pick, held[...].reshape(rows * group, width), preferred_element_type=jnp.float32
    ).astype(jnp.bfloat16)
    for i in range(3):
        small_ref[3 * i : 3 * i + 3] = taps[i].astype(jnp.float32)
    for i, vector in enumerate(vectors):
        small_ref[9 + i : 10 + i, : vector.shape[1]] = vector[...]


def edges(cells, column, row, w_depth, vectors):
    rows, cols, width = cells.shape
    group = 2 * SUBLANES
    operands = (cells, w_depth, *vectors)
    return pl.pallas_call(
        functools.partial(edges_kernel, group),
        in_specs=[pl.BlockSpec(memory_space=pltpu.SMEM)] * 2
        + [pl.BlockSpec(memory_space=pltpu.HBM)] * len(operands),
        out_specs=in_vmem(4),
        out_shape=[jax.ShapeDtypeStruct((count, width), cells.dtype) for count in (cols, cols, rows)]
        + [jax.ShapeDtypeStruct((group, w_depth.shape[2]), jnp.float32)],
        scratch_shapes=[
            pltpu.VMEM((rows, group, width), cells.dtype),
            *(pltpu.VMEM(v.shape, v.dtype) for v in operands[1:]),
            pltpu.SemaphoreType.DMA((len(operands) + 2,)),
        ],
        compiler_params=pltpu.CompilerParams(vmem_limit_bytes=EDGES_VMEM_BYTES),
        name="edges",
    )(column[None], row[None], *operands)


def lay_out_kernel(plan, arrived_ref, out_ref):
    each, run = plan.depth_h // plan.n_rows, plan.span_w // plan.n_cols
    columns, tokens = plan.outer_w * plan.depth_w, run * SUBLANES
    peers = plan.n_ch * plan.n_cols
    row = lax.broadcasted_iota(jnp.int32, (plan.outer_h * columns, peers * tokens), 0)
    i, j, b = row // columns, row % columns // plan.depth_w, row % plan.depth_w
    core, column, slot = b // plan.span_w, b % plan.span_w // run, b % run
    order = one_hot(
        (column * plan.n_ch + core) * tokens + slot * SUBLANES + i * plan.outer_w + j
    )
    for block in range(plan.n_rows):
        for k in range(each):
            source = arrived_ref[block * peers : (block + 1) * peers, k * tokens : (k + 1) * tokens]
            placed = jnp.dot(
                order, source.reshape(peers * tokens, -1), preferred_element_type=jnp.float32
            ).astype(jnp.bfloat16)
            out_ref[:, block * each + k] = placed.reshape(plan.outer_h, columns, -1)


def lay_out(plan, arrived):
    columns = plan.outer_w * plan.depth_w
    return pl.pallas_call(
        functools.partial(lay_out_kernel, plan),
        in_specs=in_vmem(1),
        out_specs=pl.BlockSpec(memory_space=pltpu.VMEM),
        out_shape=jax.ShapeDtypeStruct(
            (plan.outer_h, plan.depth_h, columns, arrived.shape[2]), jnp.bfloat16
        ),
        compiler_params=pltpu.CompilerParams(vmem_limit_bytes=VMEM_BYTES),
        name="lay_out",
    )(arrived)


def swap_rows(one, other):
    count = lax.axis_size("gy")
    sets = [[(i, i + 1) for i in range(low, count - 1, 2)] for low in (0, 1)]
    return [
        lax.ppermute(value, "gy", pairs + [(target, source) for source, target in pairs])
        for value, pairs in zip((one, other), sets)
    ]


def halo_column(column, rows, index, even):
    one, other = (lax.dynamic_slice_in_dim(row, index, 1, axis=0) for row in rows)
    parts = [jnp.where(even, other, one), column, jnp.where(even, one, other)]
    return lax.ppermute(jnp.concatenate(parts, axis=0), "gx", [(0, 1), (1, 0)])


def send_to(value, dy, dx):
    n_rows, n_cols = lax.axis_size("gy"), lax.axis_size("gx")
    pairs = [
        (y * n_cols + x, (y ^ dy) * n_cols + (x ^ dx)) for y in range(n_rows) for x in range(n_cols)
    ]
    return lax.ppermute(value, ("gy", "gx"), pairs)


def fast_device(
    plan, cells, w_expand, b_expand, w_depth, b_depth, w_project, b_project, ln_gain, w_qkv, w_out, b_out
):
    n_rows, n_cols, n_ch = plan.n_rows, plan.n_cols, plan.n_ch
    width = plan.width
    own_y, own_x, own_c = (lax.axis_index(axis) for axis in ("gy", "gx", "ch"))
    flags = jnp.stack(
        [own_c, own_y > 0, own_y < n_rows - 1, own_x > 0, own_x < n_cols - 1, own_y, own_x]
    ).astype(jnp.int32)
    index = jnp.where(own_x == 0, cells.shape[1] - 1, 0)
    vectors = tuple(v[None] for v in (b_expand, b_depth, b_out, b_project, ln_gain))
    even = own_y % 2 == 0
    one, other, column, small = edges(
        cells, index, jnp.where(even, cells.shape[0] - 1, 0), w_depth, vectors
    )
    one, w_expand, w_project = lax.optimization_barrier((one, w_expand, w_project))
    rows = swap_rows(one, other)

    def both(value):
        return value, lax.ppermute(value, "ch", [(0, 1), (1, 0)])

    w_expand, w_project, small = both(w_expand), both(w_project), both(small)
    flags, w_project_sib = lax.optimization_barrier((flags, w_project[1]))
    e_sib, x, ordered = expand_first(plan, flags, cells, w_expand[1], small[1])
    e_own, *kept = expand_second(
        plan, ordered, w_expand[0], small[0], (w_project[0], w_qkv.transpose(1, 0, 2), w_out)
    )
    *rows, x = lax.optimization_barrier((*rows, x))
    e = e_own, e_sib
    cols = halo_column(column, rows, index, even)
    cols, w_qkv, w_out = lax.optimization_barrier((cols, *kept[2:]))
    w_qkv, w_out = both(w_qkv), both(w_out)
    w_project = kept[1], w_project_sib
    far = [(dy, dx) for dy in (2, 3) for dx in (0, 1)]
    near = [(1, 1), (1, 0), (0, 1), (0, 0)]
    outside = (*rows, cols, kept[0], w_expand[1])
    *sent, halo, sides = deepen(plan, far, flags, e, x, small, w_project, outside, True)
    *sent, w_qkv_sib, w_out_sib = lax.optimization_barrier((*sent, w_qkv[1], w_out[1]))
    w_qkv, w_out = (w_qkv[0], w_qkv_sib), (w_out[0], w_out_sib)
    arrived = [send_to(value, *target) for value, target in zip(sent, far)]
    for targets, places in ((near, (0,)),):
        sent = deepen(plan, targets, flags, e, x, small, w_project, (halo, sides), False, sent)
        held = [arrived[place] for place in places]
        sent = lax.optimization_barrier((*sent, *held))
        sent, held = sent[: len(targets)], sent[len(targets) :]
        for place, value in zip(places, held):
            arrived[place] = value
        arrived += [
            value if target == (0, 0) else send_to(value, *target) for value, target in zip(sent, targets)
        ]
    leaving = attend_windows(
        plan, far + near, flags, arrived, (*w_qkv, *w_out, *small)
    )
    leaving = leaving.reshape((n_rows * n_cols * n_ch,) + leaving.shape[2:])
    returned = lax.all_to_all(leaving, ("gy", "gx", "ch"), 0, 0, tiled=True)
    return lay_out(plan, returned).reshape(cells.shape[0], cells.shape[1], -1)


def per_device(cells, *rest):
    plan = Plan(cells, *(lax.axis_size(axis) for axis in ("gy", "gx", "ch")))
    if plan.fits:
        return fast_device(plan, cells, *rest)
    return general_device(cells, *rest)


def solution(mesh):
    placed = (
        P(("grp", "gy"), "gx", None),
        P(None, "ch"),
        P("ch"),
        P(None, None, "ch"),
        P("ch"),
        P("ch", None),
        P(),
        P(),
        P(None, None, "ch"),
        P("ch", None),
        P("ch"),
    )
    return jax.shard_map(
        per_device,
        mesh=mesh,
        in_specs=placed,
        out_specs=P(("grp", "gy"), "gx", "ch"),
        check_vma=False,
    )
```

```python
import functools

import jax
import jax.numpy as jnp
import numpy as np
from jax import lax
from jax.experimental import pallas as pl
from jax.experimental.pallas import tpu as pltpu
from jax.sharding import PartitionSpec as P

SUBLANES = 8
CHUNK = 512
VMEM_BYTES = 24 * 2**20
EDGES_VMEM_BYTES = 61 * 2**20
B_EXPAND, B_DEPTH, B_OUT, B_PROJECT, GAIN = (slice(row, row + 1) for row in range(9, 14))

HEAD_DIM = 32
GRID = 8


def extended(block, sides, width):
    for axis, dim in sides:
        count = lax.axis_size(axis)
        forward = [(i, i + 1) for i in range(count - 1)]
        backward = [(target, source) for source, target in forward]
        low = lax.ppermute(
            lax.slice_in_dim(block, block.shape[dim] - width, None, axis=dim), axis, forward
        )
        high = lax.ppermute(lax.slice_in_dim(block, 0, width, axis=dim), axis, backward)
        block = jnp.concatenate([low, block, high], axis=dim)
    return block


def gelu_exact(values):
    return jax.nn.gelu(values, approximate=False)


def expand_cells(source, w_expand, b_expand):
    pre = jnp.einsum("hwc,ce->hwe", source, w_expand, preferred_element_type=jnp.float32)
    return gelu_exact(pre + b_expand).astype(jnp.bfloat16)


def depthwise(padded, w_depth, b_depth, tile_h, tile_w):
    summed = jnp.zeros((tile_h, tile_w, padded.shape[2]), jnp.float32)
    for row_off in range(3):
        for col_off in range(3):
            summed = summed + padded[row_off : row_off + tile_h, col_off : col_off + tile_w].astype(
                jnp.float32
            ) * w_depth[row_off, col_off].astype(jnp.float32)
    return gelu_exact(summed + b_depth).astype(jnp.bfloat16)


def split_order(tile, depth_h, depth_w):
    tile_h, tile_w, width = tile.shape
    shaped = tile.reshape(tile_h // depth_h, depth_h, tile_w // depth_w, depth_w, width)
    return shaped.transpose(1, 0, 3, 2, 4)


def join_order(arranged):
    depth_h, outer_h, depth_w, outer_w, width = arranged.shape
    return arranged.transpose(1, 0, 3, 2, 4).reshape(outer_h * depth_h, outer_w * depth_w, width)


def into_windows(arrived, steps_h, steps_w):
    local_h, span_h, local_w, span_w, width = arrived.shape
    grouped = arrived.reshape(local_h, GRID, steps_h, local_w, GRID, steps_w, width)
    grouped = grouped.transpose(2, 0, 5, 3, 1, 4, 6)
    return grouped.reshape(steps_h * local_h * steps_w * local_w, GRID * GRID, width)


def out_of_windows(windows, local_h, steps_h, local_w, steps_w):
    width = windows.shape[2]
    grouped = windows.reshape(steps_h, local_h, steps_w, local_w, GRID, GRID, width)
    grouped = grouped.transpose(1, 4, 0, 3, 5, 2, 6)
    return grouped.reshape(local_h, GRID * steps_h, local_w, GRID * steps_w, width)


def attend(window_full, ln_gain, w_qkv):
    values = window_full.astype(jnp.float32)
    centre = jnp.mean(values, axis=-1, keepdims=True)
    centered = values - centre
    spread = jnp.mean(centered * centered, axis=-1, keepdims=True)
    normed = (centered * lax.rsqrt(spread + 1e-05) * ln_gain).astype(jnp.bfloat16)
    projected = jnp.einsum(
        "wtc,cke->kwte", normed, w_qkv, preferred_element_type=jnp.float32
    ).astype(jnp.bfloat16)
    window_count = projected.shape[1]
    tokens = projected.shape[2]
    own_width = projected.shape[3]
    heads_own = own_width // HEAD_DIM
    shaped = projected.reshape(3, window_count, tokens, heads_own, HEAD_DIM)
    scores = jnp.einsum(
        "wqhd,wkhd->whqk", shaped[0], shaped[1], preferred_element_type=jnp.float32
    ) * HEAD_DIM ** (-0.5)
    weights = jax.nn.softmax(scores, axis=-1).astype(jnp.bfloat16)
    heads_out = jnp.einsum(
        "whqk,wkhd->wqhd", weights, shaped[2], preferred_element_type=jnp.float32
    ).astype(jnp.bfloat16)
    return heads_out.reshape(window_count, tokens, own_width)


def general_device(
    cells, w_expand, b_expand, w_depth, b_depth, w_project, b_project, ln_gain, w_qkv, w_out, b_out
):
    tile_h, tile_w, width = cells.shape
    n_rows = lax.axis_size("gy")
    n_cols = lax.axis_size("gx")
    half = width // lax.axis_size("ch")
    own = lax.axis_index("ch")
    stride_h = tile_h * n_rows // GRID
    stride_w = tile_w * n_cols // GRID
    depth_h = min(tile_h, stride_h)
    depth_w = min(tile_w, stride_w)
    steps_h = stride_h // depth_h
    steps_w = stride_w // depth_w
    local_h = depth_h // n_rows
    local_w = depth_w // n_cols
    expanded = expand_cells(cells, w_expand, b_expand)
    padded = extended(expanded, (("gy", 0), ("gx", 1)), 1)
    depth = depthwise(padded, w_depth, b_depth, tile_h, tile_w)
    partial_value = jnp.einsum("hwe,ec->hwc", depth, w_project, preferred_element_type=jnp.float32)
    share = lax.psum_scatter(
        partial_value.astype(jnp.bfloat16), "ch", scatter_dimension=2, tiled=True
    ).astype(jnp.float32)
    cells_own = lax.dynamic_slice_in_dim(cells, own * half, half, 2)
    bias_own = lax.dynamic_slice_in_dim(b_project, own * half, half, 0)
    mixed_own = (cells_own.astype(jnp.float32) + share + bias_own).astype(jnp.bfloat16)
    arranged = split_order(mixed_own, depth_h, depth_w)
    arrived = lax.all_to_all(
        lax.all_to_all(arranged, "gy", split_axis=0, concat_axis=1, tiled=True),
        "gx",
        split_axis=2,
        concat_axis=3,
        tiled=True,
    )
    window_own = into_windows(arrived, steps_h, steps_w)
    window_full = lax.all_gather(window_own, "ch", axis=2, tiled=True)
    heads_out = attend(window_full, ln_gain, w_qkv)
    attention_terms = jnp.einsum(
        "wte,ec->wtc", heads_out, w_out, preferred_element_type=jnp.float32
    )
    attention_own = lax.psum_scatter(
        attention_terms.astype(jnp.bfloat16), "ch", scatter_dimension=2, tiled=True
    ).astype(jnp.float32)
    outcome = (window_own.astype(jnp.float32) + attention_own + b_out).astype(jnp.bfloat16)
    leaving = out_of_windows(outcome, local_h, steps_h, local_w, steps_w)
    returned = lax.all_to_all(
        lax.all_to_all(leaving, "gy", split_axis=1, concat_axis=0, tiled=True),
        "gx",
        split_axis=3,
        concat_axis=2,
        tiled=True,
    )
    return join_order(returned)


class Plan:
    def __init__(self, cells, n_rows, n_cols, n_ch):
        tile_h, tile_w, self.width = cells.shape
        stride_h, stride_w = tile_h * n_rows // GRID, tile_w * n_cols // GRID
        self.depth_h, self.depth_w = min(tile_h, stride_h), min(tile_w, stride_w)
        self.outer_h, self.outer_w = tile_h // self.depth_h, tile_w // self.depth_w
        self.n_rows, self.n_cols, self.n_ch = n_rows, n_cols, n_ch
        self.span_w = self.depth_w // n_ch
        self.half_h = self.depth_h // 2
        self.fits = (
            (n_rows, n_cols, n_ch) == (4, 2, 2)
            and self.depth_h == stride_h
            and self.depth_w == stride_w
            and self.outer_h * self.outer_w == SUBLANES
            and min(self.outer_h, self.outer_w) >= 2
            and self.depth_h % n_rows == 0
            and self.span_w % (2 * n_cols) == 0
            and self.width % CHUNK == 0
        )

    def columns(self, shape, core):
        token = lax.broadcasted_iota(jnp.int32, shape, 0)
        slot, j = token // SUBLANES, token % self.outer_w
        return token, j * self.depth_w + core * self.span_w + slot - 1

    def order(self, core):
        wide = self.outer_w * self.depth_w
        shape = ((self.span_w + 2) * SUBLANES, self.outer_h * wide)
        token, column = self.columns(shape, core)
        place = token // self.outer_w % self.outer_h * wide + column
        inside = (column >= 0) & (column < wide)
        return one_hot(jnp.where(inside, place, -1))

    def row_order(self, core):
        shape = ((self.span_w + 2) * SUBLANES, self.outer_w * self.depth_w)
        return one_hot(self.columns(shape, core)[1])

    def column_order(self):
        shape = ((self.depth_h + 2) * SUBLANES, self.outer_h * self.depth_h + 2)
        token = lax.broadcasted_iota(jnp.int32, shape, 0)
        return one_hot(token // self.outer_w % self.outer_h * self.depth_h + token // SUBLANES)


def one_hot(place):
    return (lax.broadcasted_iota(jnp.int32, place.shape, 1) == place).astype(jnp.bfloat16)


def gelu_erf(values):
    return (0.5 * values) * (1.0 + lax.erf(values * 0.5**0.5))


def in_vmem(count):
    return [pl.BlockSpec(memory_space=pltpu.VMEM)] * count


def grow(plan, source_ref, weight, small, e_ref):
    slots = plan.span_w + 2
    for low_a in range(0, plan.depth_h, plan.half_h):
        planes = slice(low_a, low_a + plan.half_h)
        source = source_ref[planes].reshape(-1, plan.width)
        for low in range(0, weight.shape[1], CHUNK):
            part = slice(low, low + CHUNK)
            pre = jnp.dot(source, weight[:, part], preferred_element_type=jnp.float32)
            e_ref[planes, :, part] = (
                gelu_erf(pre + small[B_EXPAND, part])
                .astype(jnp.bfloat16)
                .reshape(plan.half_h, slots * SUBLANES, CHUNK)
            )


def expand_first_kernel(plan, flag_ref, cells_ref, w_ref, small_ref, e_ref, x_ref, ordered_ref):
    order = plan.order(flag_ref[0])
    for a in range(plan.depth_h):
        block = cells_ref[:, a].reshape(-1, plan.width)
        picked = jnp.dot(order, block, preferred_element_type=jnp.float32)
        ordered_ref[a] = picked.astype(jnp.bfloat16)
        x_ref[a] = picked[SUBLANES:-SUBLANES].astype(jnp.bfloat16)
    grow(plan, ordered_ref, w_ref, small_ref, e_ref)


def expand_first(plan, flags, cells, weight, small):
    shaped = cells.reshape(plan.outer_h, plan.depth_h, -1, plan.width)
    rows = (plan.span_w + 2) * SUBLANES
    return pl.pallas_call(
        functools.partial(expand_first_kernel, plan),
        in_specs=[pl.BlockSpec(memory_space=pltpu.SMEM)] + in_vmem(3),
        out_specs=in_vmem(3),
        out_shape=[
            jax.ShapeDtypeStruct((plan.depth_h, rows, weight.shape[1]), jnp.bfloat16),
            jax.ShapeDtypeStruct((plan.depth_h, plan.span_w * SUBLANES, plan.width), jnp.bfloat16),
            jax.ShapeDtypeStruct((plan.depth_h, rows, plan.width), jnp.bfloat16),
        ],
        compiler_params=pltpu.CompilerParams(vmem_limit_bytes=VMEM_BYTES),
        cost_estimate=pl.CostEstimate(
            flops=8 * cells.size * weight.shape[1], bytes_accessed=8 * cells.size, transcendentals=0
        ),
        name="expand_first",
    )(flags, shaped, weight, small)


def expand_second_kernel(plan, ordered_ref, w_ref, small_ref, *refs):
    count = (len(refs) - 2) // 2
    others, (e_ref, *kept), sems = refs[:count], refs[count:-1], refs[-1]
    copies = [
        pltpu.make_async_copy(*pair, sems.at[i]) for i, pair in enumerate(zip((w_ref, *others), kept))
    ]
    for copy in copies:
        copy.start()
    grow(plan, ordered_ref, w_ref, small_ref, e_ref)
    for copy in copies:
        copy.wait()


def expand_second(plan, ordered, weight, small, others):
    kept = weight, *others
    return pl.pallas_call(
        functools.partial(expand_second_kernel, plan),
        in_specs=in_vmem(3) + [pl.BlockSpec(memory_space=pl.ANY)] * len(others),
        out_specs=in_vmem(1 + len(kept)),
        out_shape=[
            jax.ShapeDtypeStruct((*ordered.shape[:2], weight.shape[1]), jnp.bfloat16),
            *(jax.ShapeDtypeStruct(v.shape, v.dtype) for v in kept),
        ],
        scratch_shapes=[pltpu.SemaphoreType.DMA((len(kept),))],
        compiler_params=pltpu.CompilerParams(vmem_limit_bytes=VMEM_BYTES),
        cost_estimate=pl.CostEstimate(
            flops=2 * ordered.size * weight.shape[1], bytes_accessed=4 * ordered.size, transcendentals=0
        ),
        name="expand_second",
    )(ordered, weight, small, *others)


def outside_kernel_part(plan, flag_ref, one_ref, other_ref, beside_ref, sides, halo_ref, beside_out_ref):
    core, up, down, left, right = (flag_ref[i] for i in range(5))
    planes, slots, outer_w = plan.depth_h + 2, plan.span_w + 2, plan.outer_w
    order = plan.row_order(core)
    even = flag_ref[5] % 2 == 0
    rows = jnp.where(even, other_ref[...], one_ref[...]), jnp.where(even, one_ref[...], other_ref[...])
    cells = [jnp.dot(order, row, preferred_element_type=jnp.float32) for row in rows]
    cells.append(jnp.dot(plan.column_order(), beside_ref[...], preferred_element_type=jnp.float32))
    cells = jnp.concatenate([value.astype(jnp.bfloat16) for value in cells], axis=0)
    up, down = up.astype(jnp.float32), down.astype(jnp.float32)
    beside = jnp.where(core == 0, left, right).astype(jnp.float32)
    token = lax.broadcasted_iota(jnp.int32, (cells.shape[0], 1), 0) - 2 * slots * SUBLANES
    plane, i = token // SUBLANES, token // outer_w % plan.outer_h
    mask = jnp.where(token < -slots * SUBLANES, up, jnp.where(token < 0, down, beside))
    mask = mask * jnp.where((token >= 0) & (plane == 0) & (i == 0), up, 1.0)
    mask = mask * jnp.where((plane == planes - 1) & (i == plan.outer_h - 1), down, 1.0)
    for side, (weight, small) in enumerate(sides):
        own = weight.shape[1]
        for low in range(0, own, CHUNK):
            lanes = slice(low, low + CHUNK)
            there = slice(side * own + low, side * own + low + CHUNK)
            pre = jnp.dot(cells, weight[:, lanes], preferred_element_type=jnp.float32)
            grown = (gelu_erf(pre + small[B_EXPAND, lanes]) * mask).astype(jnp.bfloat16)
            halo_ref[0, :, there] = grown[: slots * SUBLANES]
            halo_ref[1, :, there] = grown[slots * SUBLANES : 2 * slots * SUBLANES]
            beside_out_ref[:, :, there] = grown[2 * slots * SUBLANES :].reshape(planes, SUBLANES, CHUNK)


def deepen_kernel(plan, targets, first, *refs):
    flag_ref, e_own_ref, e_sib_ref, x_ref, *refs = refs
    small_ref, small_sib_ref, wp_ref, wp_sib_ref, *refs = refs
    *refs, deep, mixed = refs
    if first:
        one_ref, other_ref, beside_ref, we_ref, we_sib_ref, *outs, halo_ref, sides_ref = refs
        weights = (we_ref, small_ref), (we_sib_ref, small_sib_ref)
        outside_kernel_part(plan, flag_ref, one_ref, other_ref, beside_ref, weights, halo_ref, sides_ref)
    else:
        halo_ref, sides_ref, *refs = refs
        outs = refs[-len(targets) :]
    core, own_y, own_x = flag_ref[0], flag_ref[5], flag_ref[6]
    each = plan.depth_h // plan.n_rows
    blocks = len({dy for dy, _ in targets})
    count, slots, outer_w = blocks * each, plan.span_w + 2, plan.outer_w
    base = (own_y ^ targets[0][0]) // blocks * count
    low_rows = jnp.where(base == 0, outer_w, 0)
    high_rows = jnp.where(base + count == plan.depth_h, outer_w, 0)
    row = lax.broadcasted_iota(jnp.int32, (1, SUBLANES, 128), 1)
    from_low, from_high = row < low_rows, row >= SUBLANES - high_rows
    at_left = row % outer_w == jnp.where(core == 0, 0, -1)
    at_right = row % outer_w == jnp.where(core == 0, -1, outer_w - 1)
    before = lax.rem(base + plan.depth_h - 1, plan.depth_h)
    after = lax.rem(base + count, plan.depth_h)

    own = wp_ref.shape[0]
    total = None
    for side, (e_ref, wp, small) in enumerate(
        ((e_own_ref, wp_ref, small_ref), (e_sib_ref, wp_sib_ref, small_sib_ref))
    ):
        for low in range(0, own, 128):
            now, there = slice(low, low + 128), slice(side * own + low, side * own + low + 128)
            taps = [small[tap : tap + 1, now] for tap in range(9)]
            bias = small[B_DEPTH, now]

            def shaped(values):
                return values.astype(jnp.float32).reshape(slots, SUBLANES, 128)

            def plane_of(p):
                values = shaped(e_ref[before if p == 0 else after if p == count + 1 else base + p - 1, :, now])
                if p == 0:
                    rolled = pltpu.roll(values, low_rows, 1)
                    values = jnp.where(from_low, shaped(halo_ref[0, :, there]), rolled)
                if p == count + 1:
                    rolled = pltpu.roll(values, lax.rem(SUBLANES - high_rows, SUBLANES), 1)
                    values = jnp.where(from_high, shaped(halo_ref[1, :, there]), rolled)
                met = sides_ref[base + p, :, there].astype(jnp.float32)[None]
                return jnp.concatenate(
                    [
                        jnp.where(at_left, met, values[:1]),
                        values[1:-1],
                        jnp.where(at_right, met, values[-1:]),
                    ],
                    axis=0,
                )

            window = [plane_of(0), plane_of(1)]
            for a in range(count):
                window.append(plane_of(a + 2))
                summed = jnp.broadcast_to(bias, (plan.span_w, SUBLANES, 128))
                for di in range(3):
                    for dj in range(3):
                        summed = summed + window[a + di][dj : dj + plan.span_w] * taps[3 * di + dj]
                deep[a, :, there] = gelu_erf(summed).astype(jnp.bfloat16).reshape(-1, 128)
            if (low + 128) % CHUNK == 0:
                rows = slice(low + 128 - CHUNK, low + 128)
                source = deep[:, :, side * own + rows.start : side * own + rows.stop]
                term = jnp.dot(
                    source.reshape(-1, CHUNK), wp[rows], preferred_element_type=jnp.float32
                )
                total = term if total is None else total + term
    residual = x_ref[pl.ds(base, count)].astype(jnp.float32) + small_ref[B_PROJECT, : plan.width]
    mixed[...] = (total.reshape(residual.shape) + residual).reshape(mixed.shape)
    rows = plan.span_w // plan.n_cols * SUBLANES
    for out, (dy, dx) in zip(outs, targets):
        block = (own_y ^ dy) % blocks
        column = own_x ^ dx
        for k in range(each):
            out[k * rows : (k + 1) * rows] = mixed[block * each + k, column].astype(jnp.bfloat16)


def deepen(plan, targets, flags, e, x, small, w_project, outside, first, after=()):
    own = w_project[0].shape[0]
    tokens = plan.span_w * SUBLANES
    each = plan.depth_h // plan.n_rows
    count = len({dy for dy, _ in targets}) * each
    message = (each * (tokens // plan.n_cols), plan.width)
    operands = (*e, x, *small, *w_project, *outside)
    out_shape = [jax.ShapeDtypeStruct(message, jnp.bfloat16)] * len(targets)
    if first:
        slots = (plan.span_w + 2) * SUBLANES
        out_shape.append(jax.ShapeDtypeStruct((2, slots, 2 * own), jnp.bfloat16))
        out_shape.append(jax.ShapeDtypeStruct((plan.depth_h + 2, SUBLANES, 2 * own), jnp.bfloat16))
    return pl.pallas_call(
        functools.partial(deepen_kernel, plan, targets, first),
        in_specs=[pl.BlockSpec(memory_space=pltpu.SMEM)]
        + in_vmem(len(operands))
        + [pl.BlockSpec(memory_space=pl.ANY)] * len(after),
        out_specs=in_vmem(len(out_shape)),
        out_shape=out_shape,
        scratch_shapes=[
            pltpu.VMEM((count, tokens, 2 * own), jnp.bfloat16),
            pltpu.VMEM((count, plan.n_cols, tokens // plan.n_cols, plan.width), jnp.float32),
        ],
        compiler_params=pltpu.CompilerParams(vmem_limit_bytes=VMEM_BYTES),
        cost_estimate=pl.CostEstimate(
            flops=count * tokens * 4 * own * plan.width, bytes_accessed=4 * e[0].size, transcendentals=0
        ),
        name="deepen",
    )(flags, *operands, *after)


def project_heads(values, small_ref, weights, out_ref):
    windows, tokens, width = values.shape
    full = values.reshape(windows * tokens, width)
    centred = full - jnp.mean(full, axis=-1, keepdims=True)
    spread = jnp.mean(centred * centred, axis=-1, keepdims=True)
    normed = (centred * lax.rsqrt(spread + 1e-05) * small_ref[GAIN, :width]).astype(jnp.bfloat16)
    for side, weight in enumerate(weights):
        half = weight.shape[2]
        for kind in range(3):
            projected = jnp.dot(normed, weight[kind], preferred_element_type=jnp.float32)
            out_ref[kind, :, :, side * half : (side + 1) * half] = projected.astype(
                jnp.bfloat16
            ).reshape(windows, tokens, half)


def gather(xs, values):
    for source, x in enumerate(xs):
        tokens, width = x.shape
        values[:, source] = x[...].astype(jnp.float32).reshape(-1, SUBLANES, width)


def early_kernel(wqkv_ref, wqkv_sib_ref, small_ref, *refs):
    *xs, out_ref, values = refs
    gather(xs, values)
    windows, sources, _, width = values.shape
    grouped = values[...].reshape(windows, sources * SUBLANES, width)
    project_heads(grouped, small_ref, (wqkv_ref, wqkv_sib_ref), out_ref)


def project_early(arrived, weights, small):
    tokens, width = arrived[0].shape
    windows, sources = tokens // SUBLANES, len(arrived)
    operands = (*weights, small, *arrived)
    return pl.pallas_call(
        early_kernel,
        in_specs=in_vmem(len(operands)),
        out_specs=pl.BlockSpec(memory_space=pltpu.VMEM),
        out_shape=jax.ShapeDtypeStruct((3, windows, sources * SUBLANES, width), jnp.bfloat16),
        scratch_shapes=[pltpu.VMEM((windows, sources, SUBLANES, width), jnp.float32)],
        compiler_params=pltpu.CompilerParams(vmem_limit_bytes=VMEM_BYTES),
        cost_estimate=pl.CostEstimate(
            flops=6 * sources * tokens * width * width, bytes_accessed=0, transcendentals=0
        ),
        name="project_early",
    )(*operands)


def attend_kernel(
    plan, targets, flag_ref, early_ref, wqkv_ref, wqkv_sib_ref, wo_ref, wo_sib_ref, small_ref, small_sib_ref,
    *rest,
):
    sources = len(targets)
    xs, (out_ref, values, late, attended) = rest[:sources], rest[sources:]
    tokens, width = xs[0].shape
    windows = tokens // SUBLANES
    span = sources * SUBLANES
    half = wo_ref.shape[0]
    gather(xs, values)
    first_late = early_ref.shape[2] // SUBLANES
    grouped = values[:, first_late:].reshape(windows, span - first_late * SUBLANES, width)
    project_heads(grouped, small_ref, (wqkv_ref, wqkv_sib_ref), late)
    heads = 128 // HEAD_DIM
    lane = lax.broadcasted_iota(jnp.int32, (1, 128), 1) // HEAD_DIM
    scale = HEAD_DIM ** (-0.5) * np.log2(np.e)
    for window in range(windows):
        rows = slice(window * span, (window + 1) * span)
        for low in range(0, width, 128):
            lanes = slice(low, low + 128)
            query, keys, value = (
                jnp.concatenate([part[kind, window, :, lanes] for part in (early_ref, late)], axis=0)
                for kind in range(3)
            )
            spread_query = jnp.concatenate(
                [jnp.where(lane == h, query, jnp.zeros_like(query)) for h in range(heads)], axis=0
            )
            scores = lax.dot_general(
                keys, spread_query, (((1,), (1,)), ((), ())), preferred_element_type=jnp.float32
            )
            top = jnp.max(scores, axis=0, keepdims=True)
            powers = jnp.exp2((scores - top) * scale)
            weights = powers * (1.0 / jnp.sum(powers, axis=0, keepdims=True))
            mixed = lax.dot_general(
                weights.astype(jnp.bfloat16), value, (((0,), (0,)), ((), ())),
                preferred_element_type=jnp.float32,
            )
            chosen = mixed[:span]
            for h in range(1, heads):
                chosen = jnp.where(lane == h, mixed[h * span : (h + 1) * span], chosen)
            attended[rows, lanes] = chosen.astype(jnp.bfloat16)
    first = flag_ref[0] == 0
    bias = jnp.concatenate(
        [
            jnp.where(first, small_ref[B_OUT, :half], small_sib_ref[B_OUT, :half]),
            jnp.where(first, small_sib_ref[B_OUT, :half], small_ref[B_OUT, :half]),
        ],
        axis=1,
    )
    summed = jnp.dot(attended[:, :half], wo_ref[...], preferred_element_type=jnp.float32)
    summed = summed + jnp.dot(attended[:, half:], wo_sib_ref[...], preferred_element_type=jnp.float32)
    result = values[...] + (summed + bias).reshape(values.shape)
    for source, (dy, dx) in enumerate(targets):
        part = result[:, source].reshape(tokens, width).astype(jnp.bfloat16)
        target = (flag_ref[5] ^ dy) * plan.n_cols + (flag_ref[6] ^ dx)
        for core in range(plan.n_ch):
            out_ref[target, core] = part[:, core * half : (core + 1) * half]


def attend_windows(plan, targets, flags, early, arrived, weights):
    tokens, width = arrived[0].shape
    sources = len(targets)
    windows = tokens // SUBLANES
    half = width // plan.n_ch
    operands = (early, *weights, *arrived)
    return pl.pallas_call(
        functools.partial(attend_kernel, plan, targets),
        in_specs=[pl.BlockSpec(memory_space=pltpu.SMEM)] + in_vmem(len(operands)),
        out_specs=pl.BlockSpec(memory_space=pltpu.VMEM),
        out_shape=jax.ShapeDtypeStruct((sources, plan.n_ch, tokens, half), jnp.bfloat16),
        scratch_shapes=[
            pltpu.VMEM((windows, sources, SUBLANES, width), jnp.float32),
            pltpu.VMEM((3, windows, sources * SUBLANES - early.shape[2], width), jnp.bfloat16),
            pltpu.VMEM((sources * tokens, width), jnp.bfloat16),
        ],
        compiler_params=pltpu.CompilerParams(vmem_limit_bytes=VMEM_BYTES),
        cost_estimate=pl.CostEstimate(
            flops=8 * sources * tokens * width * width, bytes_accessed=4 * width * width, transcendentals=0
        ),
        name="attend",
    )(flags, *operands)


def edges_kernel(group, column_ref, row_ref, cells_hbm, taps_hbm, *refs):
    count = (len(refs) - 6) // 2
    vectors_hbm, (one_ref, other_ref, side_ref, small_ref, held, taps), (*vectors, sems) = (
        refs[:count], refs[count : count + 6], refs[count + 6 :]
    )
    rows, width = cells_hbm.shape[0], cells_hbm.shape[2]
    column, one = column_ref[0], row_ref[0]
    start = pl.multiple_of(column // group * group, group)
    pairs = [
        (cells_hbm.at[one], one_ref),
        (cells_hbm.at[rows - 1 - one], other_ref),
        (cells_hbm.at[:, pl.ds(start, group)], held),
        (taps_hbm, taps),
        *zip(vectors_hbm, vectors),
    ]
    copies = [pltpu.make_async_copy(*pair, sems.at[i]) for i, pair in enumerate(pairs)]
    for copy in copies:
        copy.start()
    shape = (rows, rows * group)
    pick = one_hot(lax.broadcasted_iota(jnp.int32, shape, 0) * group + (column - start))
    small_ref[...] = jnp.zeros_like(small_ref)
    for copy in copies:
        copy.wait()
    side_ref[...] = jnp.dot(
        pick, held[...].reshape(rows * group, width), preferred_element_type=jnp.float32
    ).astype(jnp.bfloat16)
    for i in range(3):
        small_ref[3 * i : 3 * i + 3] = taps[i].astype(jnp.float32)
    for i, vector in enumerate(vectors):
        small_ref[9 + i : 10 + i, : vector.shape[1]] = vector[...]


def edges(cells, column, row, w_depth, vectors):
    rows, cols, width = cells.shape
    group = 2 * SUBLANES
    operands = (cells, w_depth, *vectors)
    return pl.pallas_call(
        functools.partial(edges_kernel, group),
        in_specs=[pl.BlockSpec(memory_space=pltpu.SMEM)] * 2
        + [pl.BlockSpec(memory_space=pltpu.HBM)] * len(operands),
        out_specs=in_vmem(4),
        out_shape=[jax.ShapeDtypeStruct((count, width), cells.dtype) for count in (cols, cols, rows)]
        + [jax.ShapeDtypeStruct((group, w_depth.shape[2]), jnp.float32)],
        scratch_shapes=[
            pltpu.VMEM((rows, group, width), cells.dtype),
            *(pltpu.VMEM(v.shape, v.dtype) for v in operands[1:]),
            pltpu.SemaphoreType.DMA((len(operands) + 2,)),
        ],
        compiler_params=pltpu.CompilerParams(vmem_limit_bytes=EDGES_VMEM_BYTES),
        name="edges",
    )(column[None], row[None], *operands)


def lay_out_kernel(plan, arrived_ref, out_ref):
    each, run = plan.depth_h // plan.n_rows, plan.span_w // plan.n_cols
    columns, tokens = plan.outer_w * plan.depth_w, run * SUBLANES
    peers = plan.n_ch * plan.n_cols
    row = lax.broadcasted_iota(jnp.int32, (plan.outer_h * columns, peers * tokens), 0)
    i, j, b = row // columns, row % columns // plan.depth_w, row % plan.depth_w
    core, column, slot = b // plan.span_w, b % plan.span_w // run, b % run
    order = one_hot(
        (column * plan.n_ch + core) * tokens + slot * SUBLANES + i * plan.outer_w + j
    )
    for block in range(plan.n_rows):
        for k in range(each):
            source = arrived_ref[block * peers : (block + 1) * peers, k * tokens : (k + 1) * tokens]
            placed = jnp.dot(
                order, source.reshape(peers * tokens, -1), preferred_element_type=jnp.float32
            ).astype(jnp.bfloat16)
            out_ref[:, block * each + k] = placed.reshape(plan.outer_h, columns, -1)


def lay_out(plan, arrived):
    columns = plan.outer_w * plan.depth_w
    return pl.pallas_call(
        functools.partial(lay_out_kernel, plan),
        in_specs=in_vmem(1),
        out_specs=pl.BlockSpec(memory_space=pltpu.VMEM),
        out_shape=jax.ShapeDtypeStruct(
            (plan.outer_h, plan.depth_h, columns, arrived.shape[2]), jnp.bfloat16
        ),
        compiler_params=pltpu.CompilerParams(vmem_limit_bytes=VMEM_BYTES),
        name="lay_out",
    )(arrived)


def swap_rows(one, other):
    count = lax.axis_size("gy")
    sets = [[(i, i + 1) for i in range(low, count - 1, 2)] for low in (0, 1)]
    return [
        lax.ppermute(value, "gy", pairs + [(target, source) for source, target in pairs])
        for value, pairs in zip((one, other), sets)
    ]


def halo_column(column, rows, index, even):
    one, other = (lax.dynamic_slice_in_dim(row, index, 1, axis=0) for row in rows)
    parts = [jnp.where(even, other, one), column, jnp.where(even, one, other)]
    return lax.ppermute(jnp.concatenate(parts, axis=0), "gx", [(0, 1), (1, 0)])


def send_to(value, dy, dx):
    n_rows, n_cols = lax.axis_size("gy"), lax.axis_size("gx")
    pairs = [
        (y * n_cols + x, (y ^ dy) * n_cols + (x ^ dx)) for y in range(n_rows) for x in range(n_cols)
    ]
    return lax.ppermute(value, ("gy", "gx"), pairs)


def fast_device(
    plan, cells, w_expand, b_expand, w_depth, b_depth, w_project, b_project, ln_gain, w_qkv, w_out, b_out
):
    n_rows, n_cols, n_ch = plan.n_rows, plan.n_cols, plan.n_ch
    width = plan.width
    own_y, own_x, own_c = (lax.axis_index(axis) for axis in ("gy", "gx", "ch"))
    flags = jnp.stack(
        [own_c, own_y > 0, own_y < n_rows - 1, own_x > 0, own_x < n_cols - 1, own_y, own_x]
    ).astype(jnp.int32)
    index = jnp.where(own_x == 0, cells.shape[1] - 1, 0)
    vectors = tuple(v[None] for v in (b_expand, b_depth, b_out, b_project, ln_gain))
    even = own_y % 2 == 0
    one, other, column, small = edges(
        cells, index, jnp.where(even, cells.shape[0] - 1, 0), w_depth, vectors
    )
    one, w_expand, w_project = lax.optimization_barrier((one, w_expand, w_project))
    rows = swap_rows(one, other)

    def both(value):
        return value, lax.ppermute(value, "ch", [(0, 1), (1, 0)])

    w_expand, small = both(w_expand), both(small)
    e_sib, x, ordered = expand_first(plan, flags, both(cells)[1], w_expand[1], small[1])
    e_own, *kept = expand_second(
        plan, ordered, w_expand[0], small[0], (w_project, w_qkv.transpose(1, 0, 2), w_out)
    )
    *rows, x, w_project = lax.optimization_barrier((*rows, x, w_project))
    w_project = both(w_project)
    e = e_own, e_sib
    cols = halo_column(column, rows, index, even)
    cols, w_qkv, w_out = lax.optimization_barrier((cols, *kept[2:]))
    w_qkv, w_out = both(w_qkv), both(w_out)
    w_project = kept[1], w_project[1]
    far = [(dy, dx) for dy in (2, 3) for dx in (0, 1)]
    near = [(1, 1), (1, 0), (0, 1), (0, 0)]
    outside = (*rows, cols, kept[0], w_expand[1])
    *sent, halo, sides = deepen(plan, far, flags, e, x, small, w_project, outside, True)
    *sent, w_qkv_sib, w_out_sib = lax.optimization_barrier((*sent, w_qkv[1], w_out[1]))
    w_qkv, w_out = (w_qkv[0], w_qkv_sib), (w_out[0], w_out_sib)
    arrived = [send_to(value, *target) for value, target in zip(sent, far)]
    for targets, places in ((near, (0,)),):
        sent = deepen(plan, targets, flags, e, x, small, w_project, (halo, sides), False, sent)
        held = [arrived[place] for place in places]
        sent = lax.optimization_barrier((*sent, *held))
        sent, held = sent[: len(targets)], sent[len(targets) :]
        for place, value in zip(places, held):
            arrived[place] = value
        arrived += [
            value if target == (0, 0) else send_to(value, *target) for value, target in zip(sent, targets)
        ]
    early = project_early(arrived[: len(far)], w_qkv, small[0])
    leaving = attend_windows(plan, far + near, flags, early, arrived, (*w_qkv, *w_out, *small))
    leaving = leaving.reshape((n_rows * n_cols * n_ch,) + leaving.shape[2:])
    returned = lax.all_to_all(leaving, ("gy", "gx", "ch"), 0, 0, tiled=True)
    return lay_out(plan, returned).reshape(cells.shape[0], cells.shape[1], -1)


def per_device(cells, *rest):
    plan = Plan(cells, *(lax.axis_size(axis) for axis in ("gy", "gx", "ch")))
    if plan.fits:
        return fast_device(plan, cells, *rest)
    return general_device(cells, *rest)


def solution(mesh):
    placed = (
        P(("grp", "gy"), "gx", None),
        P(None, "ch"),
        P("ch"),
        P(None, None, "ch"),
        P("ch"),
        P("ch", None),
        P(),
        P(),
        P(None, None, "ch"),
        P("ch", None),
        P("ch"),
    )
    return jax.shard_map(
        per_device,
        mesh=mesh,
        in_specs=placed,
        out_specs=P(("grp", "gy"), "gx", "ch"),
        check_vma=False,
    )
```

```python
import functools

import jax
import jax.numpy as jnp
import numpy as np
from jax import lax
from jax.experimental import pallas as pl
from jax.experimental.pallas import tpu as pltpu
from jax.sharding import PartitionSpec as P

SUBLANES = 8
CHUNK = 512
VMEM_BYTES = 24 * 2**20
EDGES_VMEM_BYTES = 61 * 2**20
B_EXPAND, B_DEPTH, B_OUT, B_PROJECT, GAIN = (slice(row, row + 1) for row in range(9, 14))

HEAD_DIM = 32
GRID = 8


def extended(block, sides, width):
    for axis, dim in sides:
        count = lax.axis_size(axis)
        forward = [(i, i + 1) for i in range(count - 1)]
        backward = [(target, source) for source, target in forward]
        low = lax.ppermute(
            lax.slice_in_dim(block, block.shape[dim] - width, None, axis=dim), axis, forward
        )
        high = lax.ppermute(lax.slice_in_dim(block, 0, width, axis=dim), axis, backward)
        block = jnp.concatenate([low, block, high], axis=dim)
    return block


def gelu_exact(values):
    return jax.nn.gelu(values, approximate=False)


def expand_cells(source, w_expand, b_expand):
    pre = jnp.einsum("hwc,ce->hwe", source, w_expand, preferred_element_type=jnp.float32)
    return gelu_exact(pre + b_expand).astype(jnp.bfloat16)


def depthwise(padded, w_depth, b_depth, tile_h, tile_w):
    summed = jnp.zeros((tile_h, tile_w, padded.shape[2]), jnp.float32)
    for row_off in range(3):
        for col_off in range(3):
            summed = summed + padded[row_off : row_off + tile_h, col_off : col_off + tile_w].astype(
                jnp.float32
            ) * w_depth[row_off, col_off].astype(jnp.float32)
    return gelu_exact(summed + b_depth).astype(jnp.bfloat16)


def split_order(tile, depth_h, depth_w):
    tile_h, tile_w, width = tile.shape
    shaped = tile.reshape(tile_h // depth_h, depth_h, tile_w // depth_w, depth_w, width)
    return shaped.transpose(1, 0, 3, 2, 4)


def join_order(arranged):
    depth_h, outer_h, depth_w, outer_w, width = arranged.shape
    return arranged.transpose(1, 0, 3, 2, 4).reshape(outer_h * depth_h, outer_w * depth_w, width)


def into_windows(arrived, steps_h, steps_w):
    local_h, span_h, local_w, span_w, width = arrived.shape
    grouped = arrived.reshape(local_h, GRID, steps_h, local_w, GRID, steps_w, width)
    grouped = grouped.transpose(2, 0, 5, 3, 1, 4, 6)
    return grouped.reshape(steps_h * local_h * steps_w * local_w, GRID * GRID, width)


def out_of_windows(windows, local_h, steps_h, local_w, steps_w):
    width = windows.shape[2]
    grouped = windows.reshape(steps_h, local_h, steps_w, local_w, GRID, GRID, width)
    grouped = grouped.transpose(1, 4, 0, 3, 5, 2, 6)
    return grouped.reshape(local_h, GRID * steps_h, local_w, GRID * steps_w, width)


def attend(window_full, ln_gain, w_qkv):
    values = window_full.astype(jnp.float32)
    centre = jnp.mean(values, axis=-1, keepdims=True)
    centered = values - centre
    spread = jnp.mean(centered * centered, axis=-1, keepdims=True)
    normed = (centered * lax.rsqrt(spread + 1e-05) * ln_gain).astype(jnp.bfloat16)
    projected = jnp.einsum(
        "wtc,cke->kwte", normed, w_qkv, preferred_element_type=jnp.float32
    ).astype(jnp.bfloat16)
    window_count = projected.shape[1]
    tokens = projected.shape[2]
    own_width = projected.shape[3]
    heads_own = own_width // HEAD_DIM
    shaped = projected.reshape(3, window_count, tokens, heads_own, HEAD_DIM)
    scores = jnp.einsum(
        "wqhd,wkhd->whqk", shaped[0], shaped[1], preferred_element_type=jnp.float32
    ) * HEAD_DIM ** (-0.5)
    weights = jax.nn.softmax(scores, axis=-1).astype(jnp.bfloat16)
    heads_out = jnp.einsum(
        "whqk,wkhd->wqhd", weights, shaped[2], preferred_element_type=jnp.float32
    ).astype(jnp.bfloat16)
    return heads_out.reshape(window_count, tokens, own_width)


def general_device(
    cells, w_expand, b_expand, w_depth, b_depth, w_project, b_project, ln_gain, w_qkv, w_out, b_out
):
    tile_h, tile_w, width = cells.shape
    n_rows = lax.axis_size("gy")
    n_cols = lax.axis_size("gx")
    half = width // lax.axis_size("ch")
    own = lax.axis_index("ch")
    stride_h = tile_h * n_rows // GRID
    stride_w = tile_w * n_cols // GRID
    depth_h = min(tile_h, stride_h)
    depth_w = min(tile_w, stride_w)
    steps_h = stride_h // depth_h
    steps_w = stride_w // depth_w
    local_h = depth_h // n_rows
    local_w = depth_w // n_cols
    expanded = expand_cells(cells, w_expand, b_expand)
    padded = extended(expanded, (("gy", 0), ("gx", 1)), 1)
    depth = depthwise(padded, w_depth, b_depth, tile_h, tile_w)
    partial_value = jnp.einsum("hwe,ec->hwc", depth, w_project, preferred_element_type=jnp.float32)
    share = lax.psum_scatter(
        partial_value.astype(jnp.bfloat16), "ch", scatter_dimension=2, tiled=True
    ).astype(jnp.float32)
    cells_own = lax.dynamic_slice_in_dim(cells, own * half, half, 2)
    bias_own = lax.dynamic_slice_in_dim(b_project, own * half, half, 0)
    mixed_own = (cells_own.astype(jnp.float32) + share + bias_own).astype(jnp.bfloat16)
    arranged = split_order(mixed_own, depth_h, depth_w)
    arrived = lax.all_to_all(
        lax.all_to_all(arranged, "gy", split_axis=0, concat_axis=1, tiled=True),
        "gx",
        split_axis=2,
        concat_axis=3,
        tiled=True,
    )
    window_own = into_windows(arrived, steps_h, steps_w)
    window_full = lax.all_gather(window_own, "ch", axis=2, tiled=True)
    heads_out = attend(window_full, ln_gain, w_qkv)
    attention_terms = jnp.einsum(
        "wte,ec->wtc", heads_out, w_out, preferred_element_type=jnp.float32
    )
    attention_own = lax.psum_scatter(
        attention_terms.astype(jnp.bfloat16), "ch", scatter_dimension=2, tiled=True
    ).astype(jnp.float32)
    outcome = (window_own.astype(jnp.float32) + attention_own + b_out).astype(jnp.bfloat16)
    leaving = out_of_windows(outcome, local_h, steps_h, local_w, steps_w)
    returned = lax.all_to_all(
        lax.all_to_all(leaving, "gy", split_axis=1, concat_axis=0, tiled=True),
        "gx",
        split_axis=3,
        concat_axis=2,
        tiled=True,
    )
    return join_order(returned)


class Plan:
    def __init__(self, cells, n_rows, n_cols, n_ch):
        tile_h, tile_w, self.width = cells.shape
        stride_h, stride_w = tile_h * n_rows // GRID, tile_w * n_cols // GRID
        self.depth_h, self.depth_w = min(tile_h, stride_h), min(tile_w, stride_w)
        self.outer_h, self.outer_w = tile_h // self.depth_h, tile_w // self.depth_w
        self.n_rows, self.n_cols, self.n_ch = n_rows, n_cols, n_ch
        self.span_w = self.depth_w // n_ch
        self.half_h = self.depth_h // 2
        self.fits = (
            (n_rows, n_cols, n_ch) == (4, 2, 2)
            and self.depth_h == stride_h
            and self.depth_w == stride_w
            and self.outer_h * self.outer_w == SUBLANES
            and min(self.outer_h, self.outer_w) >= 2
            and self.depth_h % n_rows == 0
            and self.span_w % (2 * n_cols) == 0
            and self.width % CHUNK == 0
        )

    def columns(self, shape, core):
        token = lax.broadcasted_iota(jnp.int32, shape, 0)
        slot, j = token // SUBLANES, token % self.outer_w
        return token, j * self.depth_w + core * self.span_w + slot - 1

    def order(self, core):
        wide = self.outer_w * self.depth_w
        shape = ((self.span_w + 2) * SUBLANES, self.outer_h * wide)
        token, column = self.columns(shape, core)
        place = token // self.outer_w % self.outer_h * wide + column
        inside = (column >= 0) & (column < wide)
        return one_hot(jnp.where(inside, place, -1))

    def row_order(self, core):
        shape = ((self.span_w + 2) * SUBLANES, self.outer_w * self.depth_w)
        return one_hot(self.columns(shape, core)[1])

    def column_order(self):
        shape = ((self.depth_h + 2) * SUBLANES, self.outer_h * self.depth_h + 2)
        token = lax.broadcasted_iota(jnp.int32, shape, 0)
        return one_hot(token // self.outer_w % self.outer_h * self.depth_h + token // SUBLANES)


def one_hot(place):
    return (lax.broadcasted_iota(jnp.int32, place.shape, 1) == place).astype(jnp.bfloat16)


def gelu_erf(values):
    return (0.5 * values) * (1.0 + lax.erf(values * 0.5**0.5))


def in_vmem(count):
    return [pl.BlockSpec(memory_space=pltpu.VMEM)] * count


def grow(plan, source_ref, weight, small, e_ref):
    slots = plan.span_w + 2
    for low_a in range(0, plan.depth_h, plan.half_h):
        planes = slice(low_a, low_a + plan.half_h)
        source = source_ref[planes].reshape(-1, plan.width)
        for low in range(0, weight.shape[1], CHUNK):
            part = slice(low, low + CHUNK)
            pre = jnp.dot(source, weight[:, part], preferred_element_type=jnp.float32)
            e_ref[planes, :, part] = (
                gelu_erf(pre + small[B_EXPAND, part])
                .astype(jnp.bfloat16)
                .reshape(plan.half_h, slots * SUBLANES, CHUNK)
            )


def expand_first_kernel(plan, flag_ref, cells_ref, w_ref, small_ref, e_ref, x_ref, ordered_ref, column_ref):
    column, group, rows = flag_ref[7], 2 * SUBLANES, column_ref.shape[0]
    start = pl.multiple_of(column // group * group, group)
    shape = (rows, rows * group)
    pick = one_hot(lax.broadcasted_iota(jnp.int32, shape, 0) * group + (column - start))
    near = cells_ref[:, :, pl.ds(start, group)].reshape(rows * group, plan.width)
    column_ref[...] = jnp.dot(pick, near, preferred_element_type=jnp.float32).astype(jnp.bfloat16)
    order = plan.order(flag_ref[0])
    for a in range(plan.depth_h):
        block = cells_ref[:, a].reshape(-1, plan.width)
        picked = jnp.dot(order, block, preferred_element_type=jnp.float32)
        ordered_ref[a] = picked.astype(jnp.bfloat16)
        x_ref[a] = picked[SUBLANES:-SUBLANES].astype(jnp.bfloat16)
    grow(plan, ordered_ref, w_ref, small_ref, e_ref)


def expand_first(plan, flags, cells, weight, small):
    shaped = cells.reshape(plan.outer_h, plan.depth_h, -1, plan.width)
    rows = (plan.span_w + 2) * SUBLANES
    return pl.pallas_call(
        functools.partial(expand_first_kernel, plan),
        in_specs=[pl.BlockSpec(memory_space=pltpu.SMEM)] + in_vmem(3),
        out_specs=in_vmem(4),
        out_shape=[
            jax.ShapeDtypeStruct((plan.depth_h, rows, weight.shape[1]), jnp.bfloat16),
            jax.ShapeDtypeStruct((plan.depth_h, plan.span_w * SUBLANES, plan.width), jnp.bfloat16),
            jax.ShapeDtypeStruct((plan.depth_h, rows, plan.width), jnp.bfloat16),
            jax.ShapeDtypeStruct((cells.shape[0], plan.width), jnp.bfloat16),
        ],
        compiler_params=pltpu.CompilerParams(vmem_limit_bytes=VMEM_BYTES),
        cost_estimate=pl.CostEstimate(
            flops=8 * cells.size * weight.shape[1], bytes_accessed=8 * cells.size, transcendentals=0
        ),
        name="expand_first",
    )(flags, shaped, weight, small)


def expand_second_kernel(plan, ordered_ref, w_ref, small_ref, *refs):
    count = (len(refs) - 2) // 2
    others, (e_ref, *kept), sems = refs[:count], refs[count:-1], refs[-1]
    copies = [
        pltpu.make_async_copy(*pair, sems.at[i]) for i, pair in enumerate(zip((w_ref, *others), kept))
    ]
    for copy in copies:
        copy.start()
    grow(plan, ordered_ref, w_ref, small_ref, e_ref)
    for copy in copies:
        copy.wait()


def expand_second(plan, ordered, weight, small, others):
    kept = weight, *others
    return pl.pallas_call(
        functools.partial(expand_second_kernel, plan),
        in_specs=in_vmem(3) + [pl.BlockSpec(memory_space=pl.ANY)] * len(others),
        out_specs=in_vmem(1 + len(kept)),
        out_shape=[
            jax.ShapeDtypeStruct((*ordered.shape[:2], weight.shape[1]), jnp.bfloat16),
            *(jax.ShapeDtypeStruct(v.shape, v.dtype) for v in kept),
        ],
        scratch_shapes=[pltpu.SemaphoreType.DMA((len(kept),))],
        compiler_params=pltpu.CompilerParams(vmem_limit_bytes=VMEM_BYTES),
        cost_estimate=pl.CostEstimate(
            flops=2 * ordered.size * weight.shape[1], bytes_accessed=4 * ordered.size, transcendentals=0
        ),
        name="expand_second",
    )(ordered, weight, small, *others)


def outside_kernel_part(plan, flag_ref, one_ref, other_ref, beside_ref, sides, halo_ref, beside_out_ref):
    core, up, down, left, right = (flag_ref[i] for i in range(5))
    planes, slots, outer_w = plan.depth_h + 2, plan.span_w + 2, plan.outer_w
    order = plan.row_order(core)
    even = flag_ref[5] % 2 == 0
    rows = jnp.where(even, other_ref[...], one_ref[...]), jnp.where(even, one_ref[...], other_ref[...])
    cells = [jnp.dot(order, row, preferred_element_type=jnp.float32) for row in rows]
    cells.append(jnp.dot(plan.column_order(), beside_ref[...], preferred_element_type=jnp.float32))
    cells = jnp.concatenate([value.astype(jnp.bfloat16) for value in cells], axis=0)
    up, down = up.astype(jnp.float32), down.astype(jnp.float32)
    beside = jnp.where(core == 0, left, right).astype(jnp.float32)
    token = lax.broadcasted_iota(jnp.int32, (cells.shape[0], 1), 0) - 2 * slots * SUBLANES
    plane, i = token // SUBLANES, token // outer_w % plan.outer_h
    mask = jnp.where(token < -slots * SUBLANES, up, jnp.where(token < 0, down, beside))
    mask = mask * jnp.where((token >= 0) & (plane == 0) & (i == 0), up, 1.0)
    mask = mask * jnp.where((plane == planes - 1) & (i == plan.outer_h - 1), down, 1.0)
    for side, (weight, small) in enumerate(sides):
        own = weight.shape[1]
        for low in range(0, own, CHUNK):
            lanes = slice(low, low + CHUNK)
            there = slice(side * own + low, side * own + low + CHUNK)
            pre = jnp.dot(cells, weight[:, lanes], preferred_element_type=jnp.float32)
            grown = (gelu_erf(pre + small[B_EXPAND, lanes]) * mask).astype(jnp.bfloat16)
            halo_ref[0, :, there] = grown[: slots * SUBLANES]
            halo_ref[1, :, there] = grown[slots * SUBLANES : 2 * slots * SUBLANES]
            beside_out_ref[:, :, there] = grown[2 * slots * SUBLANES :].reshape(planes, SUBLANES, CHUNK)


def deepen_kernel(plan, targets, first, *refs):
    flag_ref, e_own_ref, e_sib_ref, x_ref, *refs = refs
    small_ref, small_sib_ref, wp_ref, wp_sib_ref, *refs = refs
    *refs, deep, mixed = refs
    if first:
        one_ref, other_ref, beside_ref, we_ref, we_sib_ref, *outs, halo_ref, sides_ref = refs
        weights = (we_ref, small_ref), (we_sib_ref, small_sib_ref)
        outside_kernel_part(plan, flag_ref, one_ref, other_ref, beside_ref, weights, halo_ref, sides_ref)
    else:
        halo_ref, sides_ref, *refs = refs
        outs = refs[-len(targets) :]
    core, own_y, own_x = flag_ref[0], flag_ref[5], flag_ref[6]
    each = plan.depth_h // plan.n_rows
    blocks = len({dy for dy, _ in targets})
    count, slots, outer_w = blocks * each, plan.span_w + 2, plan.outer_w
    base = (own_y ^ targets[0][0]) // blocks * count
    low_rows = jnp.where(base == 0, outer_w, 0)
    high_rows = jnp.where(base + count == plan.depth_h, outer_w, 0)
    row = lax.broadcasted_iota(jnp.int32, (1, SUBLANES, 128), 1)
    from_low, from_high = row < low_rows, row >= SUBLANES - high_rows
    at_left = row % outer_w == jnp.where(core == 0, 0, -1)
    at_right = row % outer_w == jnp.where(core == 0, -1, outer_w - 1)
    before = lax.rem(base + plan.depth_h - 1, plan.depth_h)
    after = lax.rem(base + count, plan.depth_h)

    own = wp_ref.shape[0]
    total = None
    for side, (e_ref, wp, small) in enumerate(
        ((e_own_ref, wp_ref, small_ref), (e_sib_ref, wp_sib_ref, small_sib_ref))
    ):
        for low in range(0, own, 128):
            now, there = slice(low, low + 128), slice(side * own + low, side * own + low + 128)
            taps = [small[tap : tap + 1, now] for tap in range(9)]
            bias = small[B_DEPTH, now]

            def shaped(values):
                return values.astype(jnp.float32).reshape(slots, SUBLANES, 128)

            def plane_of(p):
                values = shaped(e_ref[before if p == 0 else after if p == count + 1 else base + p - 1, :, now])
                if p == 0:
                    rolled = pltpu.roll(values, low_rows, 1)
                    values = jnp.where(from_low, shaped(halo_ref[0, :, there]), rolled)
                if p == count + 1:
                    rolled = pltpu.roll(values, lax.rem(SUBLANES - high_rows, SUBLANES), 1)
                    values = jnp.where(from_high, shaped(halo_ref[1, :, there]), rolled)
                met = sides_ref[base + p, :, there].astype(jnp.float32)[None]
                return jnp.concatenate(
                    [
                        jnp.where(at_left, met, values[:1]),
                        values[1:-1],
                        jnp.where(at_right, met, values[-1:]),
                    ],
                    axis=0,
                )

            window = [plane_of(0), plane_of(1)]
            for a in range(count):
                window.append(plane_of(a + 2))
                summed = jnp.broadcast_to(bias, (plan.span_w, SUBLANES, 128))
                for di in range(3):
                    for dj in range(3):
                        summed = summed + window[a + di][dj : dj + plan.span_w] * taps[3 * di + dj]
                deep[a, :, there] = gelu_erf(summed).astype(jnp.bfloat16).reshape(-1, 128)
            if (low + 128) % CHUNK == 0:
                rows = slice(low + 128 - CHUNK, low + 128)
                source = deep[:, :, side * own + rows.start : side * own + rows.stop]
                term = jnp.dot(
                    source.reshape(-1, CHUNK), wp[rows], preferred_element_type=jnp.float32
                )
                total = term if total is None else total + term
    residual = x_ref[pl.ds(base, count)].astype(jnp.float32) + small_ref[B_PROJECT, : plan.width]
    mixed[...] = (total.reshape(residual.shape) + residual).reshape(mixed.shape)
    rows = plan.span_w // plan.n_cols * SUBLANES
    for out, (dy, dx) in zip(outs, targets):
        block = (own_y ^ dy) % blocks
        column = own_x ^ dx
        for k in range(each):
            out[k * rows : (k + 1) * rows] = mixed[block * each + k, column].astype(jnp.bfloat16)


def deepen(plan, targets, flags, e, x, small, w_project, outside, first, after=()):
    own = w_project[0].shape[0]
    tokens = plan.span_w * SUBLANES
    each = plan.depth_h // plan.n_rows
    count = len({dy for dy, _ in targets}) * each
    message = (each * (tokens // plan.n_cols), plan.width)
    operands = (*e, x, *small, *w_project, *outside)
    out_shape = [jax.ShapeDtypeStruct(message, jnp.bfloat16)] * len(targets)
    if first:
        slots = (plan.span_w + 2) * SUBLANES
        out_shape.append(jax.ShapeDtypeStruct((2, slots, 2 * own), jnp.bfloat16))
        out_shape.append(jax.ShapeDtypeStruct((plan.depth_h + 2, SUBLANES, 2 * own), jnp.bfloat16))
    return pl.pallas_call(
        functools.partial(deepen_kernel, plan, targets, first),
        in_specs=[pl.BlockSpec(memory_space=pltpu.SMEM)]
        + in_vmem(len(operands))
        + [pl.BlockSpec(memory_space=pl.ANY)] * len(after),
        out_specs=in_vmem(len(out_shape)),
        out_shape=out_shape,
        scratch_shapes=[
            pltpu.VMEM((count, tokens, 2 * own), jnp.bfloat16),
            pltpu.VMEM((count, plan.n_cols, tokens // plan.n_cols, plan.width), jnp.float32),
        ],
        compiler_params=pltpu.CompilerParams(vmem_limit_bytes=VMEM_BYTES),
        cost_estimate=pl.CostEstimate(
            flops=count * tokens * 4 * own * plan.width, bytes_accessed=4 * e[0].size, transcendentals=0
        ),
        name="deepen",
    )(flags, *operands, *after)


def project_heads(values, small_ref, weights, out_ref):
    windows, tokens, width = values.shape
    full = values.reshape(windows * tokens, width)
    centred = full - jnp.mean(full, axis=-1, keepdims=True)
    spread = jnp.mean(centred * centred, axis=-1, keepdims=True)
    normed = (centred * lax.rsqrt(spread + 1e-05) * small_ref[GAIN, :width]).astype(jnp.bfloat16)
    for side, weight in enumerate(weights):
        half = weight.shape[2]
        for kind in range(3):
            projected = jnp.dot(normed, weight[kind], preferred_element_type=jnp.float32)
            out_ref[kind, :, :, side * half : (side + 1) * half] = projected.astype(
                jnp.bfloat16
            ).reshape(windows, tokens, half)


def gather(xs, values):
    for source, x in enumerate(xs):
        tokens, width = x.shape
        values[:, source] = x[...].astype(jnp.float32).reshape(-1, SUBLANES, width)


def early_kernel(wqkv_ref, wqkv_sib_ref, small_ref, *refs):
    *xs, out_ref, values = refs
    gather(xs, values)
    windows, sources, _, width = values.shape
    grouped = values[...].reshape(windows, sources * SUBLANES, width)
    project_heads(grouped, small_ref, (wqkv_ref, wqkv_sib_ref), out_ref)


def project_early(arrived, weights, small):
    tokens, width = arrived[0].shape
    windows, sources = tokens // SUBLANES, len(arrived)
    operands = (*weights, small, *arrived)
    return pl.pallas_call(
        early_kernel,
        in_specs=in_vmem(len(operands)),
        out_specs=pl.BlockSpec(memory_space=pltpu.VMEM),
        out_shape=jax.ShapeDtypeStruct((3, windows, sources * SUBLANES, width), jnp.bfloat16),
        scratch_shapes=[pltpu.VMEM((windows, sources, SUBLANES, width), jnp.float32)],
        compiler_params=pltpu.CompilerParams(vmem_limit_bytes=VMEM_BYTES),
        cost_estimate=pl.CostEstimate(
            flops=6 * sources * tokens * width * width, bytes_accessed=0, transcendentals=0
        ),
        name="project_early",
    )(*operands)


def attend_kernel(
    plan, targets, flag_ref, early_ref, wqkv_ref, wqkv_sib_ref, wo_ref, wo_sib_ref, small_ref, small_sib_ref,
    *rest,
):
    sources = len(targets)
    xs, (out_ref, values, late, attended) = rest[:sources], rest[sources:]
    tokens, width = xs[0].shape
    windows = tokens // SUBLANES
    span = sources * SUBLANES
    half = wo_ref.shape[0]
    gather(xs, values)
    first_late = early_ref.shape[2] // SUBLANES
    grouped = values[:, first_late:].reshape(windows, span - first_late * SUBLANES, width)
    project_heads(grouped, small_ref, (wqkv_ref, wqkv_sib_ref), late)
    heads = 128 // HEAD_DIM
    lane = lax.broadcasted_iota(jnp.int32, (1, 128), 1) // HEAD_DIM
    scale = HEAD_DIM ** (-0.5) * np.log2(np.e)
    for window in range(windows):
        rows = slice(window * span, (window + 1) * span)
        for low in range(0, width, 128):
            lanes = slice(low, low + 128)
            query, keys, value = (
                jnp.concatenate([part[kind, window, :, lanes] for part in (early_ref, late)], axis=0)
                for kind in range(3)
            )
            spread_query = jnp.concatenate(
                [jnp.where(lane == h, query, jnp.zeros_like(query)) for h in range(heads)], axis=0
            )
            scores = lax.dot_general(
                keys, spread_query, (((1,), (1,)), ((), ())), preferred_element_type=jnp.float32
            )
            top = jnp.max(scores, axis=0, keepdims=True)
            powers = jnp.exp2((scores - top) * scale)
            weights = powers * (1.0 / jnp.sum(powers, axis=0, keepdims=True))
            mixed = lax.dot_general(
                weights.astype(jnp.bfloat16), value, (((0,), (0,)), ((), ())),
                preferred_element_type=jnp.float32,
            )
            chosen = mixed[:span]
            for h in range(1, heads):
                chosen = jnp.where(lane == h, mixed[h * span : (h + 1) * span], chosen)
            attended[rows, lanes] = chosen.astype(jnp.bfloat16)
    first = flag_ref[0] == 0
    bias = jnp.concatenate(
        [
            jnp.where(first, small_ref[B_OUT, :half], small_sib_ref[B_OUT, :half]),
            jnp.where(first, small_sib_ref[B_OUT, :half], small_ref[B_OUT, :half]),
        ],
        axis=1,
    )
    summed = jnp.dot(attended[:, :half], wo_ref[...], preferred_element_type=jnp.float32)
    summed = summed + jnp.dot(attended[:, half:], wo_sib_ref[...], preferred_element_type=jnp.float32)
    result = values[...] + (summed + bias).reshape(values.shape)
    for source, (dy, dx) in enumerate(targets):
        part = result[:, source].reshape(tokens, width).astype(jnp.bfloat16)
        target = (flag_ref[6] ^ dx) * plan.n_rows + (flag_ref[5] ^ dy)
        for core in range(plan.n_ch):
            out_ref[target, core] = part[:, core * half : (core + 1) * half]


def attend_windows(plan, targets, flags, early, arrived, weights):
    tokens, width = arrived[0].shape
    sources = len(targets)
    windows = tokens // SUBLANES
    half = width // plan.n_ch
    operands = (early, *weights, *arrived)
    return pl.pallas_call(
        functools.partial(attend_kernel, plan, targets),
        in_specs=[pl.BlockSpec(memory_space=pltpu.SMEM)] + in_vmem(len(operands)),
        out_specs=pl.BlockSpec(memory_space=pltpu.VMEM),
        out_shape=jax.ShapeDtypeStruct((sources, plan.n_ch, tokens, half), jnp.bfloat16),
        scratch_shapes=[
            pltpu.VMEM((windows, sources, SUBLANES, width), jnp.float32),
            pltpu.VMEM((3, windows, sources * SUBLANES - early.shape[2], width), jnp.bfloat16),
            pltpu.VMEM((sources * tokens, width), jnp.bfloat16),
        ],
        compiler_params=pltpu.CompilerParams(vmem_limit_bytes=VMEM_BYTES),
        cost_estimate=pl.CostEstimate(
            flops=8 * sources * tokens * width * width, bytes_accessed=4 * width * width, transcendentals=0
        ),
        name="attend",
    )(flags, *operands)


def edges_kernel(row_ref, cells_hbm, taps_hbm, *refs):
    count = (len(refs) - 4) // 2
    vectors_hbm, (one_ref, other_ref, small_ref, taps), (*vectors, sems) = (
        refs[:count], refs[count : count + 4], refs[count + 4 :]
    )
    rows, one = cells_hbm.shape[0], row_ref[0]
    pairs = [
        (cells_hbm.at[one], one_ref),
        (cells_hbm.at[rows - 1 - one], other_ref),
        (taps_hbm, taps),
        *zip(vectors_hbm, vectors),
    ]
    copies = [pltpu.make_async_copy(*pair, sems.at[i]) for i, pair in enumerate(pairs)]
    for copy in copies:
        copy.start()
    small_ref[...] = jnp.zeros_like(small_ref)
    for copy in copies:
        copy.wait()
    for i in range(3):
        small_ref[3 * i : 3 * i + 3] = taps[i].astype(jnp.float32)
    for i, vector in enumerate(vectors):
        small_ref[9 + i : 10 + i, : vector.shape[1]] = vector[...]


def edges(cells, row, w_depth, vectors):
    cols, width = cells.shape[1:]
    operands = (cells, w_depth, *vectors)
    return pl.pallas_call(
        edges_kernel,
        in_specs=[pl.BlockSpec(memory_space=pltpu.SMEM)]
        + [pl.BlockSpec(memory_space=pltpu.HBM)] * len(operands),
        out_specs=in_vmem(3),
        out_shape=[jax.ShapeDtypeStruct((cols, width), cells.dtype)] * 2
        + [jax.ShapeDtypeStruct((2 * SUBLANES, w_depth.shape[2]), jnp.float32)],
        scratch_shapes=[
            *(pltpu.VMEM(v.shape, v.dtype) for v in operands[1:]),
            pltpu.SemaphoreType.DMA((len(operands) + 1,)),
        ],
        compiler_params=pltpu.CompilerParams(vmem_limit_bytes=EDGES_VMEM_BYTES),
        name="edges",
    )(row[None], *operands)


def lay_out_kernel(plan, arrived_ref, out_ref):
    each, run = plan.depth_h // plan.n_rows, plan.span_w // plan.n_cols
    columns, tokens = plan.outer_w * plan.depth_w, run * SUBLANES
    peers = plan.n_ch * plan.n_cols
    row = lax.broadcasted_iota(jnp.int32, (plan.outer_h * columns, peers * tokens), 0)
    i, j, b = row // columns, row % columns // plan.depth_w, row % plan.depth_w
    core, column, slot = b // plan.span_w, b % plan.span_w // run, b % run
    order = one_hot(
        (column * plan.n_ch + core) * tokens + slot * SUBLANES + i * plan.outer_w + j
    )
    for block in range(plan.n_rows):
        for k in range(each):
            source = jnp.concatenate(
                [
                    arrived_ref[low : low + plan.n_ch, k * tokens : (k + 1) * tokens]
                    for low in range(block * plan.n_ch, arrived_ref.shape[0], plan.n_rows * plan.n_ch)
                ],
                axis=0,
            )
            placed = jnp.dot(
                order, source.reshape(peers * tokens, -1), preferred_element_type=jnp.float32
            ).astype(jnp.bfloat16)
            out_ref[:, block * each + k] = placed.reshape(plan.outer_h, columns, -1)


def lay_out(plan, arrived):
    columns = plan.outer_w * plan.depth_w
    return pl.pallas_call(
        functools.partial(lay_out_kernel, plan),
        in_specs=in_vmem(1),
        out_specs=pl.BlockSpec(memory_space=pltpu.VMEM),
        out_shape=jax.ShapeDtypeStruct(
            (plan.outer_h, plan.depth_h, columns, arrived.shape[2]), jnp.bfloat16
        ),
        compiler_params=pltpu.CompilerParams(vmem_limit_bytes=VMEM_BYTES),
        name="lay_out",
    )(arrived)


def swap_rows(one, other):
    count = lax.axis_size("gy")
    sets = [[(i, i + 1) for i in range(low, count - 1, 2)] for low in (0, 1)]
    return [
        lax.ppermute(value, "gy", pairs + [(target, source) for source, target in pairs])
        for value, pairs in zip((one, other), sets)
    ]


def halo_column(column, rows, index, even):
    one, other = (lax.dynamic_slice_in_dim(row, index, 1, axis=0) for row in rows)
    parts = [jnp.where(even, other, one), column, jnp.where(even, one, other)]
    return lax.ppermute(jnp.concatenate(parts, axis=0), "gx", [(0, 1), (1, 0)])


def send_to(value, dy, dx):
    n_rows, n_cols = lax.axis_size("gy"), lax.axis_size("gx")
    pairs = [
        (y * n_cols + x, (y ^ dy) * n_cols + (x ^ dx)) for y in range(n_rows) for x in range(n_cols)
    ]
    return lax.ppermute(value, ("gy", "gx"), pairs)


def fast_device(
    plan, cells, w_expand, b_expand, w_depth, b_depth, w_project, b_project, ln_gain, w_qkv, w_out, b_out
):
    n_rows, n_cols, n_ch = plan.n_rows, plan.n_cols, plan.n_ch
    width = plan.width
    own_y, own_x, own_c = (lax.axis_index(axis) for axis in ("gy", "gx", "ch"))
    index = jnp.where(own_x == 0, cells.shape[1] - 1, 0)
    flags = jnp.stack(
        [own_c, own_y > 0, own_y < n_rows - 1, own_x > 0, own_x < n_cols - 1, own_y, own_x, index]
    ).astype(jnp.int32)
    vectors = tuple(v[None] for v in (b_expand, b_depth, b_out, b_project, ln_gain))
    even = own_y % 2 == 0
    one, other, small = edges(cells, jnp.where(even, cells.shape[0] - 1, 0), w_depth, vectors)
    one, w_expand, w_project = lax.optimization_barrier((one, w_expand, w_project))
    rows = swap_rows(one, other)

    def both(value):
        return value, lax.ppermute(value, "ch", [(0, 1), (1, 0)])

    w_expand, small = both(w_expand), both(small)
    e_sib, x, ordered, column = expand_first(plan, flags, both(cells)[1], w_expand[1], small[1])
    e_own, *kept = expand_second(
        plan, ordered, w_expand[0], small[0], (w_project, w_qkv.transpose(1, 0, 2), w_out)
    )
    *rows, x, w_project, column = lax.optimization_barrier((*rows, x, w_project, column))
    w_project = both(w_project)
    e = e_own, e_sib
    cols = halo_column(column, rows, index, even)
    cols, w_qkv, w_out = lax.optimization_barrier((cols, *kept[2:]))
    w_qkv, w_out = both(w_qkv), both(w_out)
    w_project = kept[1], w_project[1]
    far = [(dy, dx) for dy in (2, 3) for dx in (0, 1)]
    near = [(1, 1), (1, 0), (0, 1), (0, 0)]
    outside = (*rows, cols, kept[0], w_expand[1])
    *sent, halo, sides = deepen(plan, far, flags, e, x, small, w_project, outside, True)
    *sent, w_qkv_sib, w_out_sib = lax.optimization_barrier((*sent, w_qkv[1], w_out[1]))
    w_qkv, w_out = (w_qkv[0], w_qkv_sib), (w_out[0], w_out_sib)
    arrived = [send_to(value, *target) for value, target in zip(sent, far)]
    for targets, places in ((near, (0,)),):
        sent = deepen(plan, targets, flags, e, x, small, w_project, (halo, sides), False, sent)
        held = [arrived[place] for place in places]
        sent = lax.optimization_barrier((*sent, *held))
        sent, held = sent[: len(targets)], sent[len(targets) :]
        for place, value in zip(places, held):
            arrived[place] = value
        arrived += [
            value if target == (0, 0) else send_to(value, *target) for value, target in zip(sent, targets)
        ]
    early = project_early(arrived[: len(far)], w_qkv, small[0])
    leaving = attend_windows(plan, far + near, flags, early, arrived, (*w_qkv, *w_out, *small))
    leaving = leaving.reshape((n_rows * n_cols * n_ch,) + leaving.shape[2:])
    returned = lax.all_to_all(leaving, ("gx", "gy", "ch"), 0, 0, tiled=True)
    return lay_out(plan, returned).reshape(cells.shape[0], cells.shape[1], -1)


def per_device(cells, *rest):
    plan = Plan(cells, *(lax.axis_size(axis) for axis in ("gy", "gx", "ch")))
    if plan.fits:
        return fast_device(plan, cells, *rest)
    return general_device(cells, *rest)


def solution(mesh):
    placed = (
        P(("grp", "gy"), "gx", None),
        P(None, "ch"),
        P("ch"),
        P(None, None, "ch"),
        P("ch"),
        P("ch", None),
        P(),
        P(),
        P(None, None, "ch"),
        P("ch", None),
        P("ch"),
    )
    return jax.shard_map(
        per_device,
        mesh=mesh,
        in_specs=placed,
        out_specs=P(("grp", "gy"), "gx", "ch"),
        check_vma=False,
    )
```

```python
import functools

import jax
import jax.numpy as jnp
import numpy as np
from jax import lax
from jax.experimental import pallas as pl
from jax.experimental.pallas import tpu as pltpu
from jax.sharding import PartitionSpec as P

SUBLANES = 8
CHUNK = 512
VMEM_BYTES = 24 * 2**20
EDGES_VMEM_BYTES = 61 * 2**20
B_EXPAND, B_DEPTH, B_OUT, B_PROJECT, GAIN = (slice(row, row + 1) for row in range(9, 14))

HEAD_DIM = 32
GRID = 8


def extended(block, sides, width):
    for axis, dim in sides:
        count = lax.axis_size(axis)
        forward = [(i, i + 1) for i in range(count - 1)]
        backward = [(target, source) for source, target in forward]
        low = lax.ppermute(
            lax.slice_in_dim(block, block.shape[dim] - width, None, axis=dim), axis, forward
        )
        high = lax.ppermute(lax.slice_in_dim(block, 0, width, axis=dim), axis, backward)
        block = jnp.concatenate([low, block, high], axis=dim)
    return block


def gelu_exact(values):
    return jax.nn.gelu(values, approximate=False)


def expand_cells(source, w_expand, b_expand):
    pre = jnp.einsum("hwc,ce->hwe", source, w_expand, preferred_element_type=jnp.float32)
    return gelu_exact(pre + b_expand).astype(jnp.bfloat16)


def depthwise(padded, w_depth, b_depth, tile_h, tile_w):
    summed = jnp.zeros((tile_h, tile_w, padded.shape[2]), jnp.float32)
    for row_off in range(3):
        for col_off in range(3):
            summed = summed + padded[row_off : row_off + tile_h, col_off : col_off + tile_w].astype(
                jnp.float32
            ) * w_depth[row_off, col_off].astype(jnp.float32)
    return gelu_exact(summed + b_depth).astype(jnp.bfloat16)


def split_order(tile, depth_h, depth_w):
    tile_h, tile_w, width = tile.shape
    shaped = tile.reshape(tile_h // depth_h, depth_h, tile_w // depth_w, depth_w, width)
    return shaped.transpose(1, 0, 3, 2, 4)


def join_order(arranged):
    depth_h, outer_h, depth_w, outer_w, width = arranged.shape
    return arranged.transpose(1, 0, 3, 2, 4).reshape(outer_h * depth_h, outer_w * depth_w, width)


def into_windows(arrived, steps_h, steps_w):
    local_h, span_h, local_w, span_w, width = arrived.shape
    grouped = arrived.reshape(local_h, GRID, steps_h, local_w, GRID, steps_w, width)
    grouped = grouped.transpose(2, 0, 5, 3, 1, 4, 6)
    return grouped.reshape(steps_h * local_h * steps_w * local_w, GRID * GRID, width)


def out_of_windows(windows, local_h, steps_h, local_w, steps_w):
    width = windows.shape[2]
    grouped = windows.reshape(steps_h, local_h, steps_w, local_w, GRID, GRID, width)
    grouped = grouped.transpose(1, 4, 0, 3, 5, 2, 6)
    return grouped.reshape(local_h, GRID * steps_h, local_w, GRID * steps_w, width)


def attend(window_full, ln_gain, w_qkv):
    values = window_full.astype(jnp.float32)
    centre = jnp.mean(values, axis=-1, keepdims=True)
    centered = values - centre
    spread = jnp.mean(centered * centered, axis=-1, keepdims=True)
    normed = (centered * lax.rsqrt(spread + 1e-05) * ln_gain).astype(jnp.bfloat16)
    projected = jnp.einsum(
        "wtc,cke->kwte", normed, w_qkv, preferred_element_type=jnp.float32
    ).astype(jnp.bfloat16)
    window_count = projected.shape[1]
    tokens = projected.shape[2]
    own_width = projected.shape[3]
    heads_own = own_width // HEAD_DIM
    shaped = projected.reshape(3, window_count, tokens, heads_own, HEAD_DIM)
    scores = jnp.einsum(
        "wqhd,wkhd->whqk", shaped[0], shaped[1], preferred_element_type=jnp.float32
    ) * HEAD_DIM ** (-0.5)
    weights = jax.nn.softmax(scores, axis=-1).astype(jnp.bfloat16)
    heads_out = jnp.einsum(
        "whqk,wkhd->wqhd", weights, shaped[2], preferred_element_type=jnp.float32
    ).astype(jnp.bfloat16)
    return heads_out.reshape(window_count, tokens, own_width)


def general_device(
    cells, w_expand, b_expand, w_depth, b_depth, w_project, b_project, ln_gain, w_qkv, w_out, b_out
):
    tile_h, tile_w, width = cells.shape
    n_rows = lax.axis_size("gy")
    n_cols = lax.axis_size("gx")
    half = width // lax.axis_size("ch")
    own = lax.axis_index("ch")
    stride_h = tile_h * n_rows // GRID
    stride_w = tile_w * n_cols // GRID
    depth_h = min(tile_h, stride_h)
    depth_w = min(tile_w, stride_w)
    steps_h = stride_h // depth_h
    steps_w = stride_w // depth_w
    local_h = depth_h // n_rows
    local_w = depth_w // n_cols
    expanded = expand_cells(cells, w_expand, b_expand)
    padded = extended(expanded, (("gy", 0), ("gx", 1)), 1)
    depth = depthwise(padded, w_depth, b_depth, tile_h, tile_w)
    partial_value = jnp.einsum("hwe,ec->hwc", depth, w_project, preferred_element_type=jnp.float32)
    share = lax.psum_scatter(
        partial_value.astype(jnp.bfloat16), "ch", scatter_dimension=2, tiled=True
    ).astype(jnp.float32)
    cells_own = lax.dynamic_slice_in_dim(cells, own * half, half, 2)
    bias_own = lax.dynamic_slice_in_dim(b_project, own * half, half, 0)
    mixed_own = (cells_own.astype(jnp.float32) + share + bias_own).astype(jnp.bfloat16)
    arranged = split_order(mixed_own, depth_h, depth_w)
    arrived = lax.all_to_all(
        lax.all_to_all(arranged, "gy", split_axis=0, concat_axis=1, tiled=True),
        "gx",
        split_axis=2,
        concat_axis=3,
        tiled=True,
    )
    window_own = into_windows(arrived, steps_h, steps_w)
    window_full = lax.all_gather(window_own, "ch", axis=2, tiled=True)
    heads_out = attend(window_full, ln_gain, w_qkv)
    attention_terms = jnp.einsum(
        "wte,ec->wtc", heads_out, w_out, preferred_element_type=jnp.float32
    )
    attention_own = lax.psum_scatter(
        attention_terms.astype(jnp.bfloat16), "ch", scatter_dimension=2, tiled=True
    ).astype(jnp.float32)
    outcome = (window_own.astype(jnp.float32) + attention_own + b_out).astype(jnp.bfloat16)
    leaving = out_of_windows(outcome, local_h, steps_h, local_w, steps_w)
    returned = lax.all_to_all(
        lax.all_to_all(leaving, "gy", split_axis=1, concat_axis=0, tiled=True),
        "gx",
        split_axis=3,
        concat_axis=2,
        tiled=True,
    )
    return join_order(returned)


class Plan:
    def __init__(self, cells, n_rows, n_cols, n_ch):
        tile_h, tile_w, self.width = cells.shape
        stride_h, stride_w = tile_h * n_rows // GRID, tile_w * n_cols // GRID
        self.depth_h, self.depth_w = min(tile_h, stride_h), min(tile_w, stride_w)
        self.outer_h, self.outer_w = tile_h // self.depth_h, tile_w // self.depth_w
        self.n_rows, self.n_cols, self.n_ch = n_rows, n_cols, n_ch
        self.span_w = self.depth_w // n_ch
        self.half_h = self.depth_h // 2
        self.fits = (
            (n_rows, n_cols, n_ch) == (4, 2, 2)
            and self.depth_h == stride_h
            and self.depth_w == stride_w
            and self.outer_h * self.outer_w == SUBLANES
            and min(self.outer_h, self.outer_w) >= 2
            and self.depth_h % n_rows == 0
            and self.span_w % (2 * n_cols) == 0
            and self.width % CHUNK == 0
        )

    def columns(self, shape, core):
        token = lax.broadcasted_iota(jnp.int32, shape, 0)
        slot, j = token // SUBLANES, token % self.outer_w
        return token, j * self.depth_w + core * self.span_w + slot - 1

    def order(self, core):
        wide = self.outer_w * self.depth_w
        shape = ((self.span_w + 2) * SUBLANES, self.outer_h * wide)
        token, column = self.columns(shape, core)
        place = token // self.outer_w % self.outer_h * wide + column
        inside = (column >= 0) & (column < wide)
        return one_hot(jnp.where(inside, place, -1))

    def row_order(self, core):
        shape = ((self.span_w + 2) * SUBLANES, self.outer_w * self.depth_w)
        return one_hot(self.columns(shape, core)[1])

    def column_order(self):
        shape = ((self.depth_h + 2) * SUBLANES, self.outer_h * self.depth_h + 2)
        token = lax.broadcasted_iota(jnp.int32, shape, 0)
        return one_hot(token // self.outer_w % self.outer_h * self.depth_h + token // SUBLANES)


def one_hot(place):
    return (lax.broadcasted_iota(jnp.int32, place.shape, 1) == place).astype(jnp.bfloat16)


def gelu_erf(values):
    return (0.5 * values) * (1.0 + lax.erf(values * 0.5**0.5))


def in_vmem(count):
    return [pl.BlockSpec(memory_space=pltpu.VMEM)] * count


def grow(plan, source_ref, weight, small, e_ref):
    slots = plan.span_w + 2
    for low_a in range(0, plan.depth_h, plan.half_h):
        planes = slice(low_a, low_a + plan.half_h)
        source = source_ref[planes].reshape(-1, plan.width)
        for low in range(0, weight.shape[1], CHUNK):
            part = slice(low, low + CHUNK)
            pre = jnp.dot(source, weight[:, part], preferred_element_type=jnp.float32)
            e_ref[planes, :, part] = (
                gelu_erf(pre + small[B_EXPAND, part])
                .astype(jnp.bfloat16)
                .reshape(plan.half_h, slots * SUBLANES, CHUNK)
            )


def expand_first_kernel(plan, flag_ref, cells_ref, w_ref, small_ref, e_ref, x_ref, ordered_ref, column_ref):
    column, group, rows = flag_ref[7], 2 * SUBLANES, column_ref.shape[0]
    start = pl.multiple_of(column // group * group, group)
    shape = (rows, rows * group)
    pick = one_hot(lax.broadcasted_iota(jnp.int32, shape, 0) * group + (column - start))
    near = cells_ref[:, :, pl.ds(start, group)].reshape(rows * group, plan.width)
    column_ref[...] = jnp.dot(pick, near, preferred_element_type=jnp.float32).astype(jnp.bfloat16)
    order = plan.order(flag_ref[0])
    for a in range(plan.depth_h):
        block = cells_ref[:, a].reshape(-1, plan.width)
        picked = jnp.dot(order, block, preferred_element_type=jnp.float32)
        ordered_ref[a] = picked.astype(jnp.bfloat16)
        x_ref[a] = picked[SUBLANES:-SUBLANES].astype(jnp.bfloat16)
    grow(plan, ordered_ref, w_ref, small_ref, e_ref)


def expand_first(plan, flags, cells, weight, small):
    shaped = cells.reshape(plan.outer_h, plan.depth_h, -1, plan.width)
    rows = (plan.span_w + 2) * SUBLANES
    return pl.pallas_call(
        functools.partial(expand_first_kernel, plan),
        in_specs=[pl.BlockSpec(memory_space=pltpu.SMEM)] + in_vmem(3),
        out_specs=in_vmem(4),
        out_shape=[
            jax.ShapeDtypeStruct((plan.depth_h, rows, weight.shape[1]), jnp.bfloat16),
            jax.ShapeDtypeStruct((plan.depth_h, plan.span_w * SUBLANES, plan.width), jnp.bfloat16),
            jax.ShapeDtypeStruct((plan.depth_h, rows, plan.width), jnp.bfloat16),
            jax.ShapeDtypeStruct((cells.shape[0], plan.width), jnp.bfloat16),
        ],
        compiler_params=pltpu.CompilerParams(vmem_limit_bytes=VMEM_BYTES),
        cost_estimate=pl.CostEstimate(
            flops=8 * cells.size * weight.shape[1], bytes_accessed=8 * cells.size, transcendentals=0
        ),
        name="expand_first",
    )(flags, shaped, weight, small)


def expand_second_kernel(plan, ordered_ref, w_ref, small_ref, *refs):
    count = (len(refs) - 2) // 2
    others, (e_ref, *kept), sems = refs[:count], refs[count:-1], refs[-1]
    copies = [
        pltpu.make_async_copy(*pair, sems.at[i]) for i, pair in enumerate(zip((w_ref, *others), kept))
    ]
    for copy in copies:
        copy.start()
    grow(plan, ordered_ref, w_ref, small_ref, e_ref)
    for copy in copies:
        copy.wait()


def expand_second(plan, ordered, weight, small, others):
    kept = weight, *others
    return pl.pallas_call(
        functools.partial(expand_second_kernel, plan),
        in_specs=in_vmem(3) + [pl.BlockSpec(memory_space=pl.ANY)] * len(others),
        out_specs=in_vmem(1 + len(kept)),
        out_shape=[
            jax.ShapeDtypeStruct((*ordered.shape[:2], weight.shape[1]), jnp.bfloat16),
            *(jax.ShapeDtypeStruct(v.shape, v.dtype) for v in kept),
        ],
        scratch_shapes=[pltpu.SemaphoreType.DMA((len(kept),))],
        compiler_params=pltpu.CompilerParams(vmem_limit_bytes=VMEM_BYTES),
        cost_estimate=pl.CostEstimate(
            flops=2 * ordered.size * weight.shape[1], bytes_accessed=4 * ordered.size, transcendentals=0
        ),
        name="expand_second",
    )(ordered, weight, small, *others)


def outside_kernel_part(plan, flag_ref, one_ref, other_ref, beside_ref, sides, halo_ref, beside_out_ref):
    core, up, down, left, right = (flag_ref[i] for i in range(5))
    planes, slots, outer_w = plan.depth_h + 2, plan.span_w + 2, plan.outer_w
    order = plan.row_order(core)
    even = flag_ref[5] % 2 == 0
    rows = jnp.where(even, other_ref[...], one_ref[...]), jnp.where(even, one_ref[...], other_ref[...])
    cells = [jnp.dot(order, row, preferred_element_type=jnp.float32) for row in rows]
    cells.append(jnp.dot(plan.column_order(), beside_ref[...], preferred_element_type=jnp.float32))
    cells = jnp.concatenate([value.astype(jnp.bfloat16) for value in cells], axis=0)
    up, down = up.astype(jnp.float32), down.astype(jnp.float32)
    beside = jnp.where(core == 0, left, right).astype(jnp.float32)
    token = lax.broadcasted_iota(jnp.int32, (cells.shape[0], 1), 0) - 2 * slots * SUBLANES
    plane, i = token // SUBLANES, token // outer_w % plan.outer_h
    mask = jnp.where(token < -slots * SUBLANES, up, jnp.where(token < 0, down, beside))
    mask = mask * jnp.where((token >= 0) & (plane == 0) & (i == 0), up, 1.0)
    mask = mask * jnp.where((plane == planes - 1) & (i == plan.outer_h - 1), down, 1.0)
    for side, (weight, small) in enumerate(sides):
        own = weight.shape[1]
        for low in range(0, own, CHUNK):
            lanes = slice(low, low + CHUNK)
            there = slice(side * own + low, side * own + low + CHUNK)
            pre = jnp.dot(cells, weight[:, lanes], preferred_element_type=jnp.float32)
            grown = (gelu_erf(pre + small[B_EXPAND, lanes]) * mask).astype(jnp.bfloat16)
            halo_ref[0, :, there] = grown[: slots * SUBLANES]
            halo_ref[1, :, there] = grown[slots * SUBLANES : 2 * slots * SUBLANES]
            beside_out_ref[:, :, there] = grown[2 * slots * SUBLANES :].reshape(planes, SUBLANES, CHUNK)


def deepen_kernel(plan, targets, first, *refs):
    flag_ref, e_own_ref, e_sib_ref, x_ref, *refs = refs
    small_ref, small_sib_ref, wp_ref, wp_sib_ref, *refs = refs
    *refs, deep, mixed = refs
    if first:
        one_ref, other_ref, beside_ref, we_ref, we_sib_ref, *outs, halo_ref, sides_ref = refs
        weights = (we_ref, small_ref), (we_sib_ref, small_sib_ref)
        outside_kernel_part(plan, flag_ref, one_ref, other_ref, beside_ref, weights, halo_ref, sides_ref)
    else:
        halo_ref, sides_ref, *refs = refs
        outs = refs[-len(targets) :]
    core, own_y, own_x = flag_ref[0], flag_ref[5], flag_ref[6]
    each = plan.depth_h // plan.n_rows
    blocks = len({dy for dy, _ in targets})
    count, slots, outer_w = blocks * each, plan.span_w + 2, plan.outer_w
    base = (own_y ^ targets[0][0]) // blocks * count
    low_rows = jnp.where(base == 0, outer_w, 0)
    high_rows = jnp.where(base + count == plan.depth_h, outer_w, 0)
    row = lax.broadcasted_iota(jnp.int32, (1, SUBLANES, 128), 1)
    from_low, from_high = row < low_rows, row >= SUBLANES - high_rows
    at_left = row % outer_w == jnp.where(core == 0, 0, -1)
    at_right = row % outer_w == jnp.where(core == 0, -1, outer_w - 1)
    before = lax.rem(base + plan.depth_h - 1, plan.depth_h)
    after = lax.rem(base + count, plan.depth_h)

    own = wp_ref.shape[0]
    total = None
    for side, (e_ref, wp, small) in enumerate(
        ((e_own_ref, wp_ref, small_ref), (e_sib_ref, wp_sib_ref, small_sib_ref))
    ):
        for low in range(0, own, 128):
            now, there = slice(low, low + 128), slice(side * own + low, side * own + low + 128)
            taps = [small[tap : tap + 1, now] for tap in range(9)]
            bias = small[B_DEPTH, now]

            def shaped(values):
                return values.astype(jnp.float32).reshape(slots, SUBLANES, 128)

            def plane_of(p):
                values = shaped(e_ref[before if p == 0 else after if p == count + 1 else base + p - 1, :, now])
                if p == 0:
                    rolled = pltpu.roll(values, low_rows, 1)
                    values = jnp.where(from_low, shaped(halo_ref[0, :, there]), rolled)
                if p == count + 1:
                    rolled = pltpu.roll(values, lax.rem(SUBLANES - high_rows, SUBLANES), 1)
                    values = jnp.where(from_high, shaped(halo_ref[1, :, there]), rolled)
                met = sides_ref[base + p, :, there].astype(jnp.float32)[None]
                return jnp.concatenate(
                    [
                        jnp.where(at_left, met, values[:1]),
                        values[1:-1],
                        jnp.where(at_right, met, values[-1:]),
                    ],
                    axis=0,
                )

            window = [plane_of(0), plane_of(1)]
            for a in range(count):
                window.append(plane_of(a + 2))
                summed = jnp.broadcast_to(bias, (plan.span_w, SUBLANES, 128))
                for di in range(3):
                    for dj in range(3):
                        summed = summed + window[a + di][dj : dj + plan.span_w] * taps[3 * di + dj]
                deep[a, :, there] = gelu_erf(summed).astype(jnp.bfloat16).reshape(-1, 128)
            if (low + 128) % CHUNK == 0:
                rows = slice(low + 128 - CHUNK, low + 128)
                source = deep[:, :, side * own + rows.start : side * own + rows.stop]
                term = jnp.dot(
                    source.reshape(-1, CHUNK), wp[rows], preferred_element_type=jnp.float32
                )
                total = term if total is None else total + term
    residual = x_ref[pl.ds(base, count)].astype(jnp.float32) + small_ref[B_PROJECT, : plan.width]
    mixed[...] = (total.reshape(residual.shape) + residual).reshape(mixed.shape)
    rows = plan.span_w // plan.n_cols * SUBLANES
    for out, (dy, dx) in zip(outs, targets):
        block = (own_y ^ dy) % blocks
        column = own_x ^ dx
        for k in range(each):
            out[k * rows : (k + 1) * rows] = mixed[block * each + k, column].astype(jnp.bfloat16)


def deepen(plan, targets, flags, e, x, small, w_project, outside, first, after=()):
    own = w_project[0].shape[0]
    tokens = plan.span_w * SUBLANES
    each = plan.depth_h // plan.n_rows
    count = len({dy for dy, _ in targets}) * each
    message = (each * (tokens // plan.n_cols), plan.width)
    operands = (*e, x, *small, *w_project, *outside)
    out_shape = [jax.ShapeDtypeStruct(message, jnp.bfloat16)] * len(targets)
    if first:
        slots = (plan.span_w + 2) * SUBLANES
        out_shape.append(jax.ShapeDtypeStruct((2, slots, 2 * own), jnp.bfloat16))
        out_shape.append(jax.ShapeDtypeStruct((plan.depth_h + 2, SUBLANES, 2 * own), jnp.bfloat16))
    return pl.pallas_call(
        functools.partial(deepen_kernel, plan, targets, first),
        in_specs=[pl.BlockSpec(memory_space=pltpu.SMEM)]
        + in_vmem(len(operands))
        + [pl.BlockSpec(memory_space=pl.ANY)] * len(after),
        out_specs=in_vmem(len(out_shape)),
        out_shape=out_shape,
        scratch_shapes=[
            pltpu.VMEM((count, tokens, 2 * own), jnp.bfloat16),
            pltpu.VMEM((count, plan.n_cols, tokens // plan.n_cols, plan.width), jnp.float32),
        ],
        compiler_params=pltpu.CompilerParams(vmem_limit_bytes=VMEM_BYTES),
        cost_estimate=pl.CostEstimate(
            flops=count * tokens * 4 * own * plan.width, bytes_accessed=4 * e[0].size, transcendentals=0
        ),
        name="deepen",
    )(flags, *operands, *after)


def project_heads(values, small_ref, weights, out_ref):
    windows, tokens, width = values.shape
    full = values.reshape(windows * tokens, width)
    centred = full - jnp.mean(full, axis=-1, keepdims=True)
    spread = jnp.mean(centred * centred, axis=-1, keepdims=True)
    normed = (centred * lax.rsqrt(spread + 1e-05) * small_ref[GAIN, :width]).astype(jnp.bfloat16)
    for side, weight in enumerate(weights):
        half = weight.shape[2]
        for kind in range(3):
            projected = jnp.dot(normed, weight[kind], preferred_element_type=jnp.float32)
            out_ref[kind, :, :, side * half : (side + 1) * half] = projected.astype(
                jnp.bfloat16
            ).reshape(windows, tokens, half)


def gather(xs, values):
    for source, x in enumerate(xs):
        tokens, width = x.shape
        values[:, source] = x[...].astype(jnp.float32).reshape(-1, SUBLANES, width)


def early_kernel(wqkv_ref, wqkv_sib_ref, small_ref, *refs):
    *xs, out_ref, values = refs
    gather(xs, values)
    windows, sources, _, width = values.shape
    grouped = values[...].reshape(windows, sources * SUBLANES, width)
    project_heads(grouped, small_ref, (wqkv_ref, wqkv_sib_ref), out_ref)


def project_early(arrived, weights, small):
    tokens, width = arrived[0].shape
    windows, sources = tokens // SUBLANES, len(arrived)
    operands = (*weights, small, *arrived)
    return pl.pallas_call(
        early_kernel,
        in_specs=in_vmem(len(operands)),
        out_specs=pl.BlockSpec(memory_space=pltpu.VMEM),
        out_shape=jax.ShapeDtypeStruct((3, windows, sources * SUBLANES, width), jnp.bfloat16),
        scratch_shapes=[pltpu.VMEM((windows, sources, SUBLANES, width), jnp.float32)],
        compiler_params=pltpu.CompilerParams(vmem_limit_bytes=VMEM_BYTES),
        cost_estimate=pl.CostEstimate(
            flops=6 * sources * tokens * width * width, bytes_accessed=0, transcendentals=0
        ),
        name="project_early",
    )(*operands)


def attend_kernel(
    plan, targets, flag_ref, early_ref, wqkv_ref, wqkv_sib_ref, wo_ref, wo_sib_ref, small_ref, small_sib_ref,
    *rest,
):
    sources = len(targets)
    xs, (out_ref, values, late, attended) = rest[:sources], rest[sources:]
    tokens, width = xs[0].shape
    windows = tokens // SUBLANES
    span = sources * SUBLANES
    half = wo_ref.shape[0]
    gather(xs, values)
    first_late = early_ref.shape[2] // SUBLANES
    grouped = values[:, first_late:].reshape(windows, span - first_late * SUBLANES, width)
    project_heads(grouped, small_ref, (wqkv_ref, wqkv_sib_ref), late)
    heads = 128 // HEAD_DIM
    lane = lax.broadcasted_iota(jnp.int32, (1, 128), 1) // HEAD_DIM
    scale = HEAD_DIM ** (-0.5) * np.log2(np.e)
    for window in range(windows):
        rows = slice(window * span, (window + 1) * span)
        for low in range(0, width, 128):
            lanes = slice(low, low + 128)
            query, keys, value = (
                jnp.concatenate([part[kind, window, :, lanes] for part in (early_ref, late)], axis=0)
                for kind in range(3)
            )
            spread_query = jnp.concatenate(
                [jnp.where(lane == h, query, jnp.zeros_like(query)) for h in range(heads)], axis=0
            )
            scores = lax.dot_general(
                keys, spread_query, (((1,), (1,)), ((), ())), preferred_element_type=jnp.float32
            )
            top = jnp.max(scores, axis=0, keepdims=True)
            powers = jnp.exp2((scores - top) * scale)
            weights = powers * (1.0 / jnp.sum(powers, axis=0, keepdims=True))
            mixed = lax.dot_general(
                weights.astype(jnp.bfloat16), value, (((0,), (0,)), ((), ())),
                preferred_element_type=jnp.float32,
            )
            chosen = mixed[:span]
            for h in range(1, heads):
                chosen = jnp.where(lane == h, mixed[h * span : (h + 1) * span], chosen)
            attended[rows, lanes] = chosen.astype(jnp.bfloat16)
    first = flag_ref[0] == 0
    bias = jnp.concatenate(
        [
            jnp.where(first, small_ref[B_OUT, :half], small_sib_ref[B_OUT, :half]),
            jnp.where(first, small_sib_ref[B_OUT, :half], small_ref[B_OUT, :half]),
        ],
        axis=1,
    )
    summed = jnp.dot(attended[:, :half], wo_ref[...], preferred_element_type=jnp.float32)
    summed = summed + jnp.dot(attended[:, half:], wo_sib_ref[...], preferred_element_type=jnp.float32)
    result = values[...] + (summed + bias).reshape(values.shape)
    for source, (dy, dx) in enumerate(targets):
        part = result[:, source].reshape(tokens, width).astype(jnp.bfloat16)
        target = (flag_ref[6] ^ dx) * plan.n_rows + (flag_ref[5] ^ dy)
        for core in range(plan.n_ch):
            out_ref[target, core] = part[:, core * half : (core + 1) * half]


def attend_windows(plan, targets, flags, early, arrived, weights):
    tokens, width = arrived[0].shape
    sources = len(targets)
    windows = tokens // SUBLANES
    half = width // plan.n_ch
    operands = (early, *weights, *arrived)
    return pl.pallas_call(
        functools.partial(attend_kernel, plan, targets),
        in_specs=[pl.BlockSpec(memory_space=pltpu.SMEM)] + in_vmem(len(operands)),
        out_specs=pl.BlockSpec(memory_space=pltpu.VMEM),
        out_shape=jax.ShapeDtypeStruct((sources, plan.n_ch, tokens, half), jnp.bfloat16),
        scratch_shapes=[
            pltpu.VMEM((windows, sources, SUBLANES, width), jnp.float32),
            pltpu.VMEM((3, windows, sources * SUBLANES - early.shape[2], width), jnp.bfloat16),
            pltpu.VMEM((sources * tokens, width), jnp.bfloat16),
        ],
        compiler_params=pltpu.CompilerParams(vmem_limit_bytes=VMEM_BYTES),
        cost_estimate=pl.CostEstimate(
            flops=8 * sources * tokens * width * width, bytes_accessed=4 * width * width, transcendentals=0
        ),
        name="attend",
    )(flags, *operands)


def edges_kernel(row_ref, cells_hbm, taps_hbm, *refs):
    count = (len(refs) - 4) // 2
    vectors_hbm, (one_ref, other_ref, small_ref, taps), (*vectors, sems) = (
        refs[:count], refs[count : count + 4], refs[count + 4 :]
    )
    rows, one = cells_hbm.shape[0], row_ref[0]
    pairs = [
        (cells_hbm.at[one], one_ref),
        (cells_hbm.at[rows - 1 - one], other_ref),
        (taps_hbm, taps),
        *zip(vectors_hbm, vectors),
    ]
    copies = [pltpu.make_async_copy(*pair, sems.at[i]) for i, pair in enumerate(pairs)]
    for copy in copies:
        copy.start()
    small_ref[...] = jnp.zeros_like(small_ref)
    for copy in copies:
        copy.wait()
    for i in range(3):
        small_ref[3 * i : 3 * i + 3] = taps[i].astype(jnp.float32)
    for i, vector in enumerate(vectors):
        small_ref[9 + i : 10 + i, : vector.shape[1]] = vector[...]


def edges(cells, row, w_depth, vectors):
    cols, width = cells.shape[1:]
    operands = (cells, w_depth, *vectors)
    return pl.pallas_call(
        edges_kernel,
        in_specs=[pl.BlockSpec(memory_space=pltpu.SMEM)]
        + [pl.BlockSpec(memory_space=pltpu.HBM)] * len(operands),
        out_specs=in_vmem(3),
        out_shape=[jax.ShapeDtypeStruct((cols, width), cells.dtype)] * 2
        + [jax.ShapeDtypeStruct((2 * SUBLANES, w_depth.shape[2]), jnp.float32)],
        scratch_shapes=[
            *(pltpu.VMEM(v.shape, v.dtype) for v in operands[1:]),
            pltpu.SemaphoreType.DMA((len(operands) + 1,)),
        ],
        compiler_params=pltpu.CompilerParams(vmem_limit_bytes=EDGES_VMEM_BYTES),
        name="edges",
    )(row[None], *operands)


def lay_out_kernel(plan, arrived_ref, out_ref):
    each, run = plan.depth_h // plan.n_rows, plan.span_w // plan.n_cols
    columns, tokens = plan.outer_w * plan.depth_w, run * SUBLANES
    peers = plan.n_ch * plan.n_cols
    row = lax.broadcasted_iota(jnp.int32, (plan.outer_h * columns, peers * tokens), 0)
    i, j, b = row // columns, row % columns // plan.depth_w, row % plan.depth_w
    core, column, slot = b // plan.span_w, b % plan.span_w // run, b % run
    order = one_hot(
        (column * plan.n_ch + core) * tokens + slot * SUBLANES + i * plan.outer_w + j
    )
    for block in range(plan.n_rows):
        for k in range(each):
            source = jnp.concatenate(
                [
                    arrived_ref[low : low + plan.n_ch, k * tokens : (k + 1) * tokens]
                    for low in range(block * plan.n_ch, arrived_ref.shape[0], plan.n_rows * plan.n_ch)
                ],
                axis=0,
            )
            placed = jnp.dot(
                order, source.reshape(peers * tokens, -1), preferred_element_type=jnp.float32
            ).astype(jnp.bfloat16)
            out_ref[:, block * each + k] = placed.reshape(plan.outer_h, columns, -1)


def lay_out(plan, arrived):
    columns = plan.outer_w * plan.depth_w
    return pl.pallas_call(
        functools.partial(lay_out_kernel, plan),
        in_specs=in_vmem(1),
        out_specs=pl.BlockSpec(memory_space=pltpu.VMEM),
        out_shape=jax.ShapeDtypeStruct(
            (plan.outer_h, plan.depth_h, columns, arrived.shape[2]), jnp.bfloat16
        ),
        compiler_params=pltpu.CompilerParams(vmem_limit_bytes=VMEM_BYTES),
        name="lay_out",
    )(arrived)


def swap_rows(one, other):
    count = lax.axis_size("gy")
    sets = [[(i, i + 1) for i in range(low, count - 1, 2)] for low in (0, 1)]
    return [
        lax.ppermute(value, "gy", pairs + [(target, source) for source, target in pairs])
        for value, pairs in zip((one, other), sets)
    ]


def halo_column(column, rows, index, even):
    one, other = (lax.dynamic_slice_in_dim(row, index, 1, axis=0) for row in rows)
    parts = [jnp.where(even, other, one), column, jnp.where(even, one, other)]
    return lax.ppermute(jnp.concatenate(parts, axis=0), "gx", [(0, 1), (1, 0)])


def send_to(value, dy, dx):
    n_rows, n_cols = lax.axis_size("gy"), lax.axis_size("gx")
    pairs = [
        (y * n_cols + x, (y ^ dy) * n_cols + (x ^ dx)) for y in range(n_rows) for x in range(n_cols)
    ]
    return lax.ppermute(value, ("gy", "gx"), pairs)


def fast_device(
    plan, cells, w_expand, b_expand, w_depth, b_depth, w_project, b_project, ln_gain, w_qkv, w_out, b_out
):
    n_rows, n_cols, n_ch = plan.n_rows, plan.n_cols, plan.n_ch
    width = plan.width
    own_y, own_x, own_c = (lax.axis_index(axis) for axis in ("gy", "gx", "ch"))
    index = jnp.where(own_x == 0, cells.shape[1] - 1, 0)
    flags = jnp.stack(
        [own_c, own_y > 0, own_y < n_rows - 1, own_x > 0, own_x < n_cols - 1, own_y, own_x, index]
    ).astype(jnp.int32)
    vectors = tuple(v[None] for v in (b_expand, b_depth, b_out, b_project, ln_gain))
    even = own_y % 2 == 0
    one, other, small = edges(cells, jnp.where(even, cells.shape[0] - 1, 0), w_depth, vectors)
    one, w_expand, w_project = lax.optimization_barrier((one, w_expand, w_project))
    rows = swap_rows(one, other)

    def both(value):
        return value, lax.ppermute(value, "ch", [(0, 1), (1, 0)])

    w_expand, small = both(w_expand), both(small)
    w_project = both(w_project)
    e_sib, x, ordered, column = expand_first(plan, flags, both(cells)[1], w_expand[1], small[1])
    e_own, *kept = expand_second(
        plan, ordered, w_expand[0], small[0], (w_project[0], w_qkv.transpose(1, 0, 2), w_out)
    )
    *rows, x, column = lax.optimization_barrier((*rows, x, column))
    e = e_own, e_sib
    cols = halo_column(column, rows, index, even)
    cols, w_qkv, w_out = lax.optimization_barrier((cols, *kept[2:]))
    w_qkv, w_out = both(w_qkv), both(w_out)
    w_project = kept[1], w_project[1]
    far = [(dy, dx) for dy in (2, 3) for dx in (0, 1)]
    near = [(1, 1), (1, 0), (0, 1), (0, 0)]
    outside = (*rows, cols, kept[0], w_expand[1])
    *sent, halo, sides = deepen(plan, far, flags, e, x, small, w_project, outside, True)
    *sent, w_qkv_sib, w_out_sib = lax.optimization_barrier((*sent, w_qkv[1], w_out[1]))
    w_qkv, w_out = (w_qkv[0], w_qkv_sib), (w_out[0], w_out_sib)
    arrived = [send_to(value, *target) for value, target in zip(sent, far)]
    for targets, places in ((near, (0,)),):
        sent = deepen(plan, targets, flags, e, x, small, w_project, (halo, sides), False, sent)
        held = [arrived[place] for place in places]
        sent = lax.optimization_barrier((*sent, *held))
        sent, held = sent[: len(targets)], sent[len(targets) :]
        for place, value in zip(places, held):
            arrived[place] = value
        arrived += [
            value if target == (0, 0) else send_to(value, *target) for value, target in zip(sent, targets)
        ]
    early = project_early(arrived[: len(far)], w_qkv, small[0])
    leaving = attend_windows(plan, far + near, flags, early, arrived, (*w_qkv, *w_out, *small))
    leaving = leaving.reshape((n_rows * n_cols * n_ch,) + leaving.shape[2:])
    returned = lax.all_to_all(leaving, ("gx", "gy", "ch"), 0, 0, tiled=True)
    return lay_out(plan, returned).reshape(cells.shape[0], cells.shape[1], -1)


def per_device(cells, *rest):
    plan = Plan(cells, *(lax.axis_size(axis) for axis in ("gy", "gx", "ch")))
    if plan.fits:
        return fast_device(plan, cells, *rest)
    return general_device(cells, *rest)


def solution(mesh):
    placed = (
        P(("grp", "gy"), "gx", None),
        P(None, "ch"),
        P("ch"),
        P(None, None, "ch"),
        P("ch"),
        P("ch", None),
        P(),
        P(),
        P(None, None, "ch"),
        P("ch", None),
        P("ch"),
    )
    return jax.shard_map(
        per_device,
        mesh=mesh,
        in_specs=placed,
        out_specs=P(("grp", "gy"), "gx", "ch"),
        check_vma=False,
    )
```

```python
import functools

import jax
import jax.numpy as jnp
import numpy as np
from jax import lax
from jax.experimental import pallas as pl
from jax.experimental.pallas import tpu as pltpu
from jax.sharding import PartitionSpec as P

SUBLANES = 8
CHUNK = 512
VMEM_BYTES = 24 * 2**20
EDGES_VMEM_BYTES = 61 * 2**20
B_EXPAND, B_DEPTH, B_OUT, B_PROJECT, GAIN = (slice(row, row + 1) for row in range(9, 14))

HEAD_DIM = 32
GRID = 8


def extended(block, sides, width):
    for axis, dim in sides:
        count = lax.axis_size(axis)
        forward = [(i, i + 1) for i in range(count - 1)]
        backward = [(target, source) for source, target in forward]
        low = lax.ppermute(
            lax.slice_in_dim(block, block.shape[dim] - width, None, axis=dim), axis, forward
        )
        high = lax.ppermute(lax.slice_in_dim(block, 0, width, axis=dim), axis, backward)
        block = jnp.concatenate([low, block, high], axis=dim)
    return block


def gelu_exact(values):
    return jax.nn.gelu(values, approximate=False)


def expand_cells(source, w_expand, b_expand):
    pre = jnp.einsum("hwc,ce->hwe", source, w_expand, preferred_element_type=jnp.float32)
    return gelu_exact(pre + b_expand).astype(jnp.bfloat16)


def depthwise(padded, w_depth, b_depth, tile_h, tile_w):
    summed = jnp.zeros((tile_h, tile_w, padded.shape[2]), jnp.float32)
    for row_off in range(3):
        for col_off in range(3):
            summed = summed + padded[row_off : row_off + tile_h, col_off : col_off + tile_w].astype(
                jnp.float32
            ) * w_depth[row_off, col_off].astype(jnp.float32)
    return gelu_exact(summed + b_depth).astype(jnp.bfloat16)


def split_order(tile, depth_h, depth_w):
    tile_h, tile_w, width = tile.shape
    shaped = tile.reshape(tile_h // depth_h, depth_h, tile_w // depth_w, depth_w, width)
    return shaped.transpose(1, 0, 3, 2, 4)


def join_order(arranged):
    depth_h, outer_h, depth_w, outer_w, width = arranged.shape
    return arranged.transpose(1, 0, 3, 2, 4).reshape(outer_h * depth_h, outer_w * depth_w, width)


def into_windows(arrived, steps_h, steps_w):
    local_h, span_h, local_w, span_w, width = arrived.shape
    grouped = arrived.reshape(local_h, GRID, steps_h, local_w, GRID, steps_w, width)
    grouped = grouped.transpose(2, 0, 5, 3, 1, 4, 6)
    return grouped.reshape(steps_h * local_h * steps_w * local_w, GRID * GRID, width)


def out_of_windows(windows, local_h, steps_h, local_w, steps_w):
    width = windows.shape[2]
    grouped = windows.reshape(steps_h, local_h, steps_w, local_w, GRID, GRID, width)
    grouped = grouped.transpose(1, 4, 0, 3, 5, 2, 6)
    return grouped.reshape(local_h, GRID * steps_h, local_w, GRID * steps_w, width)


def attend(window_full, ln_gain, w_qkv):
    values = window_full.astype(jnp.float32)
    centre = jnp.mean(values, axis=-1, keepdims=True)
    centered = values - centre
    spread = jnp.mean(centered * centered, axis=-1, keepdims=True)
    normed = (centered * lax.rsqrt(spread + 1e-05) * ln_gain).astype(jnp.bfloat16)
    projected = jnp.einsum(
        "wtc,cke->kwte", normed, w_qkv, preferred_element_type=jnp.float32
    ).astype(jnp.bfloat16)
    window_count = projected.shape[1]
    tokens = projected.shape[2]
    own_width = projected.shape[3]
    heads_own = own_width // HEAD_DIM
    shaped = projected.reshape(3, window_count, tokens, heads_own, HEAD_DIM)
    scores = jnp.einsum(
        "wqhd,wkhd->whqk", shaped[0], shaped[1], preferred_element_type=jnp.float32
    ) * HEAD_DIM ** (-0.5)
    weights = jax.nn.softmax(scores, axis=-1).astype(jnp.bfloat16)
    heads_out = jnp.einsum(
        "whqk,wkhd->wqhd", weights, shaped[2], preferred_element_type=jnp.float32
    ).astype(jnp.bfloat16)
    return heads_out.reshape(window_count, tokens, own_width)


def general_device(
    cells, w_expand, b_expand, w_depth, b_depth, w_project, b_project, ln_gain, w_qkv, w_out, b_out
):
    tile_h, tile_w, width = cells.shape
    n_rows = lax.axis_size("gy")
    n_cols = lax.axis_size("gx")
    half = width // lax.axis_size("ch")
    own = lax.axis_index("ch")
    stride_h = tile_h * n_rows // GRID
    stride_w = tile_w * n_cols // GRID
    depth_h = min(tile_h, stride_h)
    depth_w = min(tile_w, stride_w)
    steps_h = stride_h // depth_h
    steps_w = stride_w // depth_w
    local_h = depth_h // n_rows
    local_w = depth_w // n_cols
    expanded = expand_cells(cells, w_expand, b_expand)
    padded = extended(expanded, (("gy", 0), ("gx", 1)), 1)
    depth = depthwise(padded, w_depth, b_depth, tile_h, tile_w)
    partial_value = jnp.einsum("hwe,ec->hwc", depth, w_project, preferred_element_type=jnp.float32)
    share = lax.psum_scatter(
        partial_value.astype(jnp.bfloat16), "ch", scatter_dimension=2, tiled=True
    ).astype(jnp.float32)
    cells_own = lax.dynamic_slice_in_dim(cells, own * half, half, 2)
    bias_own = lax.dynamic_slice_in_dim(b_project, own * half, half, 0)
    mixed_own = (cells_own.astype(jnp.float32) + share + bias_own).astype(jnp.bfloat16)
    arranged = split_order(mixed_own, depth_h, depth_w)
    arrived = lax.all_to_all(
        lax.all_to_all(arranged, "gy", split_axis=0, concat_axis=1, tiled=True),
        "gx",
        split_axis=2,
        concat_axis=3,
        tiled=True,
    )
    window_own = into_windows(arrived, steps_h, steps_w)
    window_full = lax.all_gather(window_own, "ch", axis=2, tiled=True)
    heads_out = attend(window_full, ln_gain, w_qkv)
    attention_terms = jnp.einsum(
        "wte,ec->wtc", heads_out, w_out, preferred_element_type=jnp.float32
    )
    attention_own = lax.psum_scatter(
        attention_terms.astype(jnp.bfloat16), "ch", scatter_dimension=2, tiled=True
    ).astype(jnp.float32)
    outcome = (window_own.astype(jnp.float32) + attention_own + b_out).astype(jnp.bfloat16)
    leaving = out_of_windows(outcome, local_h, steps_h, local_w, steps_w)
    returned = lax.all_to_all(
        lax.all_to_all(leaving, "gy", split_axis=1, concat_axis=0, tiled=True),
        "gx",
        split_axis=3,
        concat_axis=2,
        tiled=True,
    )
    return join_order(returned)


class Plan:
    def __init__(self, cells, n_rows, n_cols, n_ch):
        tile_h, tile_w, self.width = cells.shape
        stride_h, stride_w = tile_h * n_rows // GRID, tile_w * n_cols // GRID
        self.depth_h, self.depth_w = min(tile_h, stride_h), min(tile_w, stride_w)
        self.outer_h, self.outer_w = tile_h // self.depth_h, tile_w // self.depth_w
        self.n_rows, self.n_cols, self.n_ch = n_rows, n_cols, n_ch
        self.span_w = self.depth_w // n_ch
        self.half_h = self.depth_h // 2
        self.fits = (
            (n_rows, n_cols, n_ch) == (4, 2, 2)
            and self.depth_h == stride_h
            and self.depth_w == stride_w
            and self.outer_h * self.outer_w == SUBLANES
            and min(self.outer_h, self.outer_w) >= 2
            and self.depth_h % n_rows == 0
            and self.span_w % (2 * n_cols) == 0
            and self.width % CHUNK == 0
        )

    def columns(self, shape, core):
        token = lax.broadcasted_iota(jnp.int32, shape, 0)
        slot, j = token // SUBLANES, token % self.outer_w
        return token, j * self.depth_w + core * self.span_w + slot - 1

    def order(self, core):
        wide = self.outer_w * self.depth_w
        shape = ((self.span_w + 2) * SUBLANES, self.outer_h * wide)
        token, column = self.columns(shape, core)
        place = token // self.outer_w % self.outer_h * wide + column
        inside = (column >= 0) & (column < wide)
        return one_hot(jnp.where(inside, place, -1))

    def row_order(self, core):
        shape = ((self.span_w + 2) * SUBLANES, self.outer_w * self.depth_w)
        return one_hot(self.columns(shape, core)[1])

    def column_order(self):
        shape = ((self.depth_h + 2) * SUBLANES, self.outer_h * self.depth_h + 2)
        token = lax.broadcasted_iota(jnp.int32, shape, 0)
        return one_hot(token // self.outer_w % self.outer_h * self.depth_h + token // SUBLANES)


def one_hot(place):
    return (lax.broadcasted_iota(jnp.int32, place.shape, 1) == place).astype(jnp.bfloat16)


def gelu_erf(values):
    return (0.5 * values) * (1.0 + lax.erf(values * 0.5**0.5))


def in_vmem(count):
    return [pl.BlockSpec(memory_space=pltpu.VMEM)] * count


def grow(plan, source_ref, weight, small, e_ref):
    slots = plan.span_w + 2
    for low_a in range(0, plan.depth_h, plan.half_h):
        planes = slice(low_a, low_a + plan.half_h)
        source = source_ref[planes].reshape(-1, plan.width)
        for low in range(0, weight.shape[1], CHUNK):
            part = slice(low, low + CHUNK)
            pre = jnp.dot(source, weight[:, part], preferred_element_type=jnp.float32)
            e_ref[planes, :, part] = (
                gelu_erf(pre + small[B_EXPAND, part])
                .astype(jnp.bfloat16)
                .reshape(plan.half_h, slots * SUBLANES, CHUNK)
            )


def expand_first_kernel(plan, flag_ref, cells_ref, w_ref, small_ref, e_ref, x_ref, ordered_ref, column_ref):
    column, group, rows = flag_ref[7], 2 * SUBLANES, column_ref.shape[0]
    start = pl.multiple_of(column // group * group, group)
    shape = (rows, rows * group)
    pick = one_hot(lax.broadcasted_iota(jnp.int32, shape, 0) * group + (column - start))
    near = cells_ref[:, :, pl.ds(start, group)].reshape(rows * group, plan.width)
    column_ref[...] = jnp.dot(pick, near, preferred_element_type=jnp.float32).astype(jnp.bfloat16)
    order = plan.order(flag_ref[0])
    for a in range(plan.depth_h):
        block = cells_ref[:, a].reshape(-1, plan.width)
        picked = jnp.dot(order, block, preferred_element_type=jnp.float32)
        ordered_ref[a] = picked.astype(jnp.bfloat16)
        x_ref[a] = picked[SUBLANES:-SUBLANES].astype(jnp.bfloat16)
    grow(plan, ordered_ref, w_ref, small_ref, e_ref)


def expand_first(plan, flags, cells, weight, small):
    shaped = cells.reshape(plan.outer_h, plan.depth_h, -1, plan.width)
    rows = (plan.span_w + 2) * SUBLANES
    return pl.pallas_call(
        functools.partial(expand_first_kernel, plan),
        in_specs=[pl.BlockSpec(memory_space=pltpu.SMEM)] + in_vmem(3),
        out_specs=in_vmem(4),
        out_shape=[
            jax.ShapeDtypeStruct((plan.depth_h, rows, weight.shape[1]), jnp.bfloat16),
            jax.ShapeDtypeStruct((plan.depth_h, plan.span_w * SUBLANES, plan.width), jnp.bfloat16),
            jax.ShapeDtypeStruct((plan.depth_h, rows, plan.width), jnp.bfloat16),
            jax.ShapeDtypeStruct((cells.shape[0], plan.width), jnp.bfloat16),
        ],
        compiler_params=pltpu.CompilerParams(vmem_limit_bytes=VMEM_BYTES),
        cost_estimate=pl.CostEstimate(
            flops=8 * cells.size * weight.shape[1], bytes_accessed=8 * cells.size, transcendentals=0
        ),
        name="expand_first",
    )(flags, shaped, weight, small)


def expand_second_kernel(plan, ordered_ref, w_ref, small_ref, *refs):
    count = (len(refs) - 2) // 2
    others, (e_ref, *kept), sems = refs[:count], refs[count:-1], refs[-1]
    copies = [
        pltpu.make_async_copy(*pair, sems.at[i]) for i, pair in enumerate(zip((w_ref, *others), kept))
    ]
    for copy in copies:
        copy.start()
    grow(plan, ordered_ref, w_ref, small_ref, e_ref)
    for copy in copies:
        copy.wait()


def expand_second(plan, ordered, weight, small, others):
    kept = weight, *others
    return pl.pallas_call(
        functools.partial(expand_second_kernel, plan),
        in_specs=in_vmem(3) + [pl.BlockSpec(memory_space=pl.ANY)] * len(others),
        out_specs=in_vmem(1 + len(kept)),
        out_shape=[
            jax.ShapeDtypeStruct((*ordered.shape[:2], weight.shape[1]), jnp.bfloat16),
            *(jax.ShapeDtypeStruct(v.shape, v.dtype) for v in kept),
        ],
        scratch_shapes=[pltpu.SemaphoreType.DMA((len(kept),))],
        compiler_params=pltpu.CompilerParams(vmem_limit_bytes=VMEM_BYTES),
        cost_estimate=pl.CostEstimate(
            flops=2 * ordered.size * weight.shape[1], bytes_accessed=4 * ordered.size, transcendentals=0
        ),
        name="expand_second",
    )(ordered, weight, small, *others)


def outside_kernel_part(plan, flag_ref, one_ref, other_ref, beside_ref, sides, halo_ref, beside_out_ref):
    core, up, down, left, right = (flag_ref[i] for i in range(5))
    planes, slots, outer_w = plan.depth_h + 2, plan.span_w + 2, plan.outer_w
    order = plan.row_order(core)
    even = flag_ref[5] % 2 == 0
    rows = jnp.where(even, other_ref[...], one_ref[...]), jnp.where(even, one_ref[...], other_ref[...])
    cells = [jnp.dot(order, row, preferred_element_type=jnp.float32) for row in rows]
    cells.append(jnp.dot(plan.column_order(), beside_ref[...], preferred_element_type=jnp.float32))
    cells = jnp.concatenate([value.astype(jnp.bfloat16) for value in cells], axis=0)
    up, down = up.astype(jnp.float32), down.astype(jnp.float32)
    beside = jnp.where(core == 0, left, right).astype(jnp.float32)
    token = lax.broadcasted_iota(jnp.int32, (cells.shape[0], 1), 0) - 2 * slots * SUBLANES
    plane, i = token // SUBLANES, token // outer_w % plan.outer_h
    mask = jnp.where(token < -slots * SUBLANES, up, jnp.where(token < 0, down, beside))
    mask = mask * jnp.where((token >= 0) & (plane == 0) & (i == 0), up, 1.0)
    mask = mask * jnp.where((plane == planes - 1) & (i == plan.outer_h - 1), down, 1.0)
    for side, (weight, small) in enumerate(sides):
        own = weight.shape[1]
        for low in range(0, own, CHUNK):
            lanes = slice(low, low + CHUNK)
            there = slice(side * own + low, side * own + low + CHUNK)
            pre = jnp.dot(cells, weight[:, lanes], preferred_element_type=jnp.float32)
            grown = (gelu_erf(pre + small[B_EXPAND, lanes]) * mask).astype(jnp.bfloat16)
            halo_ref[0, :, there] = grown[: slots * SUBLANES]
            halo_ref[1, :, there] = grown[slots * SUBLANES : 2 * slots * SUBLANES]
            beside_out_ref[:, :, there] = grown[2 * slots * SUBLANES :].reshape(planes, SUBLANES, CHUNK)


def deepen_kernel(plan, targets, first, *refs):
    flag_ref, e_own_ref, e_sib_ref, x_ref, *refs = refs
    small_ref, small_sib_ref, wp_ref, wp_sib_ref, *refs = refs
    *refs, deep, mixed = refs
    if first:
        one_ref, other_ref, beside_ref, we_ref, we_sib_ref, *outs, halo_ref, sides_ref = refs
        weights = (we_ref, small_ref), (we_sib_ref, small_sib_ref)
        outside_kernel_part(plan, flag_ref, one_ref, other_ref, beside_ref, weights, halo_ref, sides_ref)
    else:
        halo_ref, sides_ref, *refs = refs
        outs = refs[-len(targets) :]
    core, own_y, own_x = flag_ref[0], flag_ref[5], flag_ref[6]
    each = plan.depth_h // plan.n_rows
    blocks = len({dy for dy, _ in targets})
    count, slots, outer_w = blocks * each, plan.span_w + 2, plan.outer_w
    base = (own_y ^ targets[0][0]) // blocks * count
    low_rows = jnp.where(base == 0, outer_w, 0)
    high_rows = jnp.where(base + count == plan.depth_h, outer_w, 0)
    row = lax.broadcasted_iota(jnp.int32, (1, SUBLANES, 128), 1)
    from_low, from_high = row < low_rows, row >= SUBLANES - high_rows
    at_left = row % outer_w == jnp.where(core == 0, 0, -1)
    at_right = row % outer_w == jnp.where(core == 0, -1, outer_w - 1)
    before = lax.rem(base + plan.depth_h - 1, plan.depth_h)
    after = lax.rem(base + count, plan.depth_h)

    own = wp_ref.shape[0]
    total = None
    for side, (e_ref, wp, small) in enumerate(
        ((e_own_ref, wp_ref, small_ref), (e_sib_ref, wp_sib_ref, small_sib_ref))
    ):
        for low in range(0, own, 128):
            now, there = slice(low, low + 128), slice(side * own + low, side * own + low + 128)
            taps = [small[tap : tap + 1, now] for tap in range(9)]
            bias = small[B_DEPTH, now]

            def shaped(values):
                return values.astype(jnp.float32).reshape(slots, SUBLANES, 128)

            def plane_of(p):
                values = shaped(e_ref[before if p == 0 else after if p == count + 1 else base + p - 1, :, now])
                if p == 0:
                    rolled = pltpu.roll(values, low_rows, 1)
                    values = jnp.where(from_low, shaped(halo_ref[0, :, there]), rolled)
                if p == count + 1:
                    rolled = pltpu.roll(values, lax.rem(SUBLANES - high_rows, SUBLANES), 1)
                    values = jnp.where(from_high, shaped(halo_ref[1, :, there]), rolled)
                met = sides_ref[base + p, :, there].astype(jnp.float32)[None]
                return jnp.concatenate(
                    [
                        jnp.where(at_left, met, values[:1]),
                        values[1:-1],
                        jnp.where(at_right, met, values[-1:]),
                    ],
                    axis=0,
                )

            window = [plane_of(0), plane_of(1)]
            for a in range(count):
                window.append(plane_of(a + 2))
                summed = jnp.broadcast_to(bias, (plan.span_w, SUBLANES, 128))
                for di in range(3):
                    for dj in range(3):
                        summed = summed + window[a + di][dj : dj + plan.span_w] * taps[3 * di + dj]
                deep[a, :, there] = gelu_erf(summed).astype(jnp.bfloat16).reshape(-1, 128)
            if (low + 128) % CHUNK == 0:
                rows = slice(low + 128 - CHUNK, low + 128)
                source = deep[:, :, side * own + rows.start : side * own + rows.stop]
                term = jnp.dot(
                    source.reshape(-1, CHUNK), wp[rows], preferred_element_type=jnp.float32
                )
                total = term if total is None else total + term
    residual = x_ref[pl.ds(base, count)].astype(jnp.float32) + small_ref[B_PROJECT, : plan.width]
    mixed[...] = (total.reshape(residual.shape) + residual).reshape(mixed.shape)
    rows = plan.span_w // plan.n_cols * SUBLANES
    for out, (dy, dx) in zip(outs, targets):
        block = (own_y ^ dy) % blocks
        column = own_x ^ dx
        for k in range(each):
            out[k * rows : (k + 1) * rows] = mixed[block * each + k, column].astype(jnp.bfloat16)


def deepen(plan, targets, flags, e, x, small, w_project, outside, first, after=()):
    own = w_project[0].shape[0]
    tokens = plan.span_w * SUBLANES
    each = plan.depth_h // plan.n_rows
    count = len({dy for dy, _ in targets}) * each
    message = (each * (tokens // plan.n_cols), plan.width)
    operands = (*e, x, *small, *w_project, *outside)
    out_shape = [jax.ShapeDtypeStruct(message, jnp.bfloat16)] * len(targets)
    if first:
        slots = (plan.span_w + 2) * SUBLANES
        out_shape.append(jax.ShapeDtypeStruct((2, slots, 2 * own), jnp.bfloat16))
        out_shape.append(jax.ShapeDtypeStruct((plan.depth_h + 2, SUBLANES, 2 * own), jnp.bfloat16))
    return pl.pallas_call(
        functools.partial(deepen_kernel, plan, targets, first),
        in_specs=[pl.BlockSpec(memory_space=pltpu.SMEM)]
        + in_vmem(len(operands))
        + [pl.BlockSpec(memory_space=pl.ANY)] * len(after),
        out_specs=in_vmem(len(out_shape)),
        out_shape=out_shape,
        scratch_shapes=[
            pltpu.VMEM((count, tokens, 2 * own), jnp.bfloat16),
            pltpu.VMEM((count, plan.n_cols, tokens // plan.n_cols, plan.width), jnp.float32),
        ],
        compiler_params=pltpu.CompilerParams(vmem_limit_bytes=VMEM_BYTES),
        cost_estimate=pl.CostEstimate(
            flops=count * tokens * 4 * own * plan.width, bytes_accessed=4 * e[0].size, transcendentals=0
        ),
        name="deepen",
    )(flags, *operands, *after)


def project_heads(values, small_ref, weights, out_ref):
    windows, tokens, width = values.shape
    full = values.reshape(windows * tokens, width)
    centred = full - jnp.mean(full, axis=-1, keepdims=True)
    spread = jnp.mean(centred * centred, axis=-1, keepdims=True)
    normed = (centred * lax.rsqrt(spread + 1e-05) * small_ref[GAIN, :width]).astype(jnp.bfloat16)
    for side, weight in enumerate(weights):
        half = weight.shape[2]
        for kind in range(3):
            projected = jnp.dot(normed, weight[kind], preferred_element_type=jnp.float32)
            out_ref[kind, :, :, side * half : (side + 1) * half] = projected.astype(
                jnp.bfloat16
            ).reshape(windows, tokens, half)


def gather(xs, values):
    for source, x in enumerate(xs):
        tokens, width = x.shape
        values[:, source] = x[...].astype(jnp.float32).reshape(-1, SUBLANES, width)


def early_kernel(wqkv_ref, wqkv_sib_ref, small_ref, *refs):
    *xs, out_ref, values = refs
    gather(xs, values)
    windows, sources, _, width = values.shape
    grouped = values[...].reshape(windows, sources * SUBLANES, width)
    project_heads(grouped, small_ref, (wqkv_ref, wqkv_sib_ref), out_ref)


def project_early(arrived, weights, small):
    tokens, width = arrived[0].shape
    windows, sources = tokens // SUBLANES, len(arrived)
    operands = (*weights, small, *arrived)
    return pl.pallas_call(
        early_kernel,
        in_specs=in_vmem(len(operands)),
        out_specs=pl.BlockSpec(memory_space=pltpu.VMEM),
        out_shape=jax.ShapeDtypeStruct((3, windows, sources * SUBLANES, width), jnp.bfloat16),
        scratch_shapes=[pltpu.VMEM((windows, sources, SUBLANES, width), jnp.float32)],
        compiler_params=pltpu.CompilerParams(vmem_limit_bytes=VMEM_BYTES),
        cost_estimate=pl.CostEstimate(
            flops=6 * sources * tokens * width * width, bytes_accessed=0, transcendentals=0
        ),
        name="project_early",
    )(*operands)


def attend_kernel(
    plan, targets, flag_ref, early_ref, wqkv_ref, wqkv_sib_ref, wo_ref, wo_sib_ref, small_ref, small_sib_ref,
    *rest,
):
    sources = len(targets)
    xs, (out_ref, values, late, attended) = rest[:sources], rest[sources:]
    tokens, width = xs[0].shape
    windows = tokens // SUBLANES
    span = sources * SUBLANES
    half = wo_ref.shape[0]
    gather(xs, values)
    first_late = early_ref.shape[2] // SUBLANES
    grouped = values[:, first_late:].reshape(windows, span - first_late * SUBLANES, width)
    project_heads(grouped, small_ref, (wqkv_ref, wqkv_sib_ref), late)
    heads = 128 // HEAD_DIM
    lane = lax.broadcasted_iota(jnp.int32, (1, 128), 1) // HEAD_DIM
    scale = HEAD_DIM ** (-0.5) * np.log2(np.e)
    for window in range(windows):
        rows = slice(window * span, (window + 1) * span)
        for low in range(0, width, 128):
            lanes = slice(low, low + 128)
            query, keys, value = (
                jnp.concatenate([part[kind, window, :, lanes] for part in (early_ref, late)], axis=0)
                for kind in range(3)
            )
            spread_query = jnp.concatenate(
                [jnp.where(lane == h, query, jnp.zeros_like(query)) for h in range(heads)], axis=0
            )
            scores = lax.dot_general(
                keys, spread_query, (((1,), (1,)), ((), ())), preferred_element_type=jnp.float32
            )
            top = jnp.max(scores, axis=0, keepdims=True)
            powers = jnp.exp2((scores - top) * scale)
            weights = powers * (1.0 / jnp.sum(powers, axis=0, keepdims=True))
            mixed = lax.dot_general(
                weights.astype(jnp.bfloat16), value, (((0,), (0,)), ((), ())),
                preferred_element_type=jnp.float32,
            )
            chosen = mixed[:span]
            for h in range(1, heads):
                chosen = jnp.where(lane == h, mixed[h * span : (h + 1) * span], chosen)
            attended[rows, lanes] = chosen.astype(jnp.bfloat16)
    first = flag_ref[0] == 0
    bias = jnp.concatenate(
        [
            jnp.where(first, small_ref[B_OUT, :half], small_sib_ref[B_OUT, :half]),
            jnp.where(first, small_sib_ref[B_OUT, :half], small_ref[B_OUT, :half]),
        ],
        axis=1,
    )
    summed = jnp.dot(attended[:, :half], wo_ref[...], preferred_element_type=jnp.float32)
    summed = summed + jnp.dot(attended[:, half:], wo_sib_ref[...], preferred_element_type=jnp.float32)
    result = values[...] + (summed + bias).reshape(values.shape)
    for source, (dy, dx) in enumerate(targets):
        part = result[:, source].reshape(tokens, width).astype(jnp.bfloat16)
        target = (flag_ref[6] ^ dx) * plan.n_rows + (flag_ref[5] ^ dy)
        for core in range(plan.n_ch):
            out_ref[target, core] = part[:, core * half : (core + 1) * half]


def attend_windows(plan, targets, flags, early, arrived, weights):
    tokens, width = arrived[0].shape
    sources = len(targets)
    windows = tokens // SUBLANES
    half = width // plan.n_ch
    operands = (early, *weights, *arrived)
    return pl.pallas_call(
        functools.partial(attend_kernel, plan, targets),
        in_specs=[pl.BlockSpec(memory_space=pltpu.SMEM)] + in_vmem(len(operands)),
        out_specs=pl.BlockSpec(memory_space=pltpu.VMEM),
        out_shape=jax.ShapeDtypeStruct((sources, plan.n_ch, tokens, half), jnp.bfloat16),
        scratch_shapes=[
            pltpu.VMEM((windows, sources, SUBLANES, width), jnp.float32),
            pltpu.VMEM((3, windows, sources * SUBLANES - early.shape[2], width), jnp.bfloat16),
            pltpu.VMEM((sources * tokens, width), jnp.bfloat16),
        ],
        compiler_params=pltpu.CompilerParams(vmem_limit_bytes=VMEM_BYTES),
        cost_estimate=pl.CostEstimate(
            flops=8 * sources * tokens * width * width, bytes_accessed=4 * width * width, transcendentals=0
        ),
        name="attend",
    )(flags, *operands)


def edges_kernel(row_ref, cells_hbm, taps_hbm, *refs):
    count = (len(refs) - 4) // 2
    vectors_hbm, (one_ref, other_ref, small_ref, taps), (*vectors, sems) = (
        refs[:count], refs[count : count + 4], refs[count + 4 :]
    )
    rows, one = cells_hbm.shape[0], row_ref[0]
    pairs = [
        (cells_hbm.at[one], one_ref),
        (cells_hbm.at[rows - 1 - one], other_ref),
        (taps_hbm, taps),
        *zip(vectors_hbm, vectors),
    ]
    copies = [pltpu.make_async_copy(*pair, sems.at[i]) for i, pair in enumerate(pairs)]
    for copy in copies:
        copy.start()
    small_ref[...] = jnp.zeros_like(small_ref)
    for copy in copies:
        copy.wait()
    for i in range(3):
        small_ref[3 * i : 3 * i + 3] = taps[i].astype(jnp.float32)
    for i, vector in enumerate(vectors):
        small_ref[9 + i : 10 + i, : vector.shape[1]] = vector[...]


def edges(cells, row, w_depth, vectors):
    cols, width = cells.shape[1:]
    operands = (cells, w_depth, *vectors)
    return pl.pallas_call(
        edges_kernel,
        in_specs=[pl.BlockSpec(memory_space=pltpu.SMEM)]
        + [pl.BlockSpec(memory_space=pltpu.HBM)] * len(operands),
        out_specs=in_vmem(3),
        out_shape=[jax.ShapeDtypeStruct((cols, width), cells.dtype)] * 2
        + [jax.ShapeDtypeStruct((2 * SUBLANES, w_depth.shape[2]), jnp.float32)],
        scratch_shapes=[
            *(pltpu.VMEM(v.shape, v.dtype) for v in operands[1:]),
            pltpu.SemaphoreType.DMA((len(operands) + 1,)),
        ],
        compiler_params=pltpu.CompilerParams(vmem_limit_bytes=EDGES_VMEM_BYTES),
        name="edges",
    )(row[None], *operands)


def lay_out_kernel(plan, arrived_ref, out_ref):
    each, run = plan.depth_h // plan.n_rows, plan.span_w // plan.n_cols
    columns, tokens = plan.outer_w * plan.depth_w, run * SUBLANES
    peers = plan.n_ch * plan.n_cols
    row = lax.broadcasted_iota(jnp.int32, (plan.outer_h * columns, peers * tokens), 0)
    i, j, b = row // columns, row % columns // plan.depth_w, row % plan.depth_w
    core, column, slot = b // plan.span_w, b % plan.span_w // run, b % run
    order = one_hot(
        (column * plan.n_ch + core) * tokens + slot * SUBLANES + i * plan.outer_w + j
    )
    for block in range(plan.n_rows):
        for k in range(each):
            source = jnp.concatenate(
                [
                    arrived_ref[low : low + plan.n_ch, k * tokens : (k + 1) * tokens]
                    for low in range(block * plan.n_ch, arrived_ref.shape[0], plan.n_rows * plan.n_ch)
                ],
                axis=0,
            )
            placed = jnp.dot(
                order, source.reshape(peers * tokens, -1), preferred_element_type=jnp.float32
            ).astype(jnp.bfloat16)
            out_ref[:, block * each + k] = placed.reshape(plan.outer_h, columns, -1)


def lay_out(plan, arrived):
    columns = plan.outer_w * plan.depth_w
    return pl.pallas_call(
        functools.partial(lay_out_kernel, plan),
        in_specs=in_vmem(1),
        out_specs=pl.BlockSpec(memory_space=pltpu.VMEM),
        out_shape=jax.ShapeDtypeStruct(
            (plan.outer_h, plan.depth_h, columns, arrived.shape[2]), jnp.bfloat16
        ),
        compiler_params=pltpu.CompilerParams(vmem_limit_bytes=VMEM_BYTES),
        name="lay_out",
    )(arrived)


def swap_rows(one, other):
    count = lax.axis_size("gy")
    sets = [[(i, i + 1) for i in range(low, count - 1, 2)] for low in (0, 1)]
    return [
        lax.ppermute(value, "gy", pairs + [(target, source) for source, target in pairs])
        for value, pairs in zip((one, other), sets)
    ]


def halo_column(column, rows, index, even):
    one, other = (lax.dynamic_slice_in_dim(row, index, 1, axis=0) for row in rows)
    parts = [jnp.where(even, other, one), column, jnp.where(even, one, other)]
    return lax.ppermute(jnp.concatenate(parts, axis=0), "gx", [(0, 1), (1, 0)])


def send_to(value, dy, dx):
    n_rows, n_cols = lax.axis_size("gy"), lax.axis_size("gx")
    pairs = [
        (y * n_cols + x, (y ^ dy) * n_cols + (x ^ dx)) for y in range(n_rows) for x in range(n_cols)
    ]
    return lax.ppermute(value, ("gy", "gx"), pairs)


def fast_device(
    plan, cells, w_expand, b_expand, w_depth, b_depth, w_project, b_project, ln_gain, w_qkv, w_out, b_out
):
    n_rows, n_cols, n_ch = plan.n_rows, plan.n_cols, plan.n_ch
    width = plan.width
    own_y, own_x, own_c = (lax.axis_index(axis) for axis in ("gy", "gx", "ch"))
    index = jnp.where(own_x == 0, cells.shape[1] - 1, 0)
    flags = jnp.stack(
        [own_c, own_y > 0, own_y < n_rows - 1, own_x > 0, own_x < n_cols - 1, own_y, own_x, index]
    ).astype(jnp.int32)
    vectors = tuple(v[None] for v in (b_expand, b_depth, b_out, b_project, ln_gain))
    even = own_y % 2 == 0
    one, other, small = edges(cells, jnp.where(even, cells.shape[0] - 1, 0), w_depth, vectors)
    one, w_expand, w_project = lax.optimization_barrier((one, w_expand, w_project))
    rows = swap_rows(one, other)

    def both(value):
        return value, lax.ppermute(value, "ch", [(0, 1), (1, 0)])

    w_expand, small = both(w_expand), both(small)
    w_project = both(w_project)
    e_sib, x, ordered, column = expand_first(plan, flags, both(cells)[1], w_expand[1], small[1])
    e_own, *kept = expand_second(
        plan, ordered, w_expand[0], small[0], (w_project[0], w_qkv.transpose(1, 0, 2), w_out)
    )
    *rows, x, column = lax.optimization_barrier((*rows, x, column))
    e = e_own, e_sib
    cols = halo_column(column, rows, index, even)
    cols, w_qkv, w_out = lax.optimization_barrier((cols, *kept[2:]))
    w_qkv, w_out = both(w_qkv), both(w_out)
    w_project = kept[1], w_project[1]
    far = [(dy, dx) for dy in (2, 3) for dx in (0, 1)]
    near = [(1, 0), (1, 1), (0, 1), (0, 0)]
    outside = (*rows, cols, kept[0], w_expand[1])
    *sent, halo, sides = deepen(plan, far, flags, e, x, small, w_project, outside, True)
    *sent, w_qkv_sib, w_out_sib = lax.optimization_barrier((*sent, w_qkv[1], w_out[1]))
    w_qkv, w_out = (w_qkv[0], w_qkv_sib), (w_out[0], w_out_sib)
    arrived = [send_to(value, *target) for value, target in zip(sent, far)]
    for targets, places in ((near, (0,)),):
        sent = deepen(plan, targets, flags, e, x, small, w_project, (halo, sides), False, sent)
        held = [arrived[place] for place in places]
        sent = lax.optimization_barrier((*sent, *held))
        sent, held = sent[: len(targets)], sent[len(targets) :]
        for place, value in zip(places, held):
            arrived[place] = value
        arrived += [
            value if target == (0, 0) else send_to(value, *target) for value, target in zip(sent, targets)
        ]
    early = project_early(arrived[: len(far)], w_qkv, small[0])
    leaving = attend_windows(plan, far + near, flags, early, arrived, (*w_qkv, *w_out, *small))
    leaving = leaving.reshape((n_rows * n_cols * n_ch,) + leaving.shape[2:])
    returned = lax.all_to_all(leaving, ("gx", "gy", "ch"), 0, 0, tiled=True)
    return lay_out(plan, returned).reshape(cells.shape[0], cells.shape[1], -1)


def per_device(cells, *rest):
    plan = Plan(cells, *(lax.axis_size(axis) for axis in ("gy", "gx", "ch")))
    if plan.fits:
        return fast_device(plan, cells, *rest)
    return general_device(cells, *rest)


def solution(mesh):
    placed = (
        P(("grp", "gy"), "gx", None),
        P(None, "ch"),
        P("ch"),
        P(None, None, "ch"),
        P("ch"),
        P("ch", None),
        P(),
        P(),
        P(None, None, "ch"),
        P("ch", None),
        P("ch"),
    )
    return jax.shard_map(
        per_device,
        mesh=mesh,
        in_specs=placed,
        out_specs=P(("grp", "gy"), "gx", "ch"),
        check_vma=False,
    )
```
